256 devices in a mesh: clip: 2 (over z_hi), tm: 16 (over y, z_lo), space: 8 (over x, core).
Axes of the slice: x: 4, y: 4, z: 8 (z_hi: 2, z_lo: 4; z = z_hi * 4 + z_lo), core: 2. Of those that a mesh axis runs over, the one named last changes fastest.
Arguments:
- frames_in: bfloat16 [2, 32, 64, 128, 256], P('clip', 'tm', 'space'), may hold values from -6 to 6
- cotangent: bfloat16 [2, 32, 64, 128, 256], P('clip', 'tm', 'space'), may hold values from -6 to 6
- spatial_weight: bfloat16 [3, 3, 256, 256], replicated, may hold values from -0.125 to 0.125
- temporal_weight: bfloat16 [3, 256, 256], replicated, may hold values from -0.21875 to 0.21875
Outputs:
- block_out: bfloat16 [2, 32, 64, 128, 256], P('clip', 'tm', 'space')
- input_grad: bfloat16 [2, 32, 64, 128, 256], P('clip', 'tm', 'space')
- spatial_grad: float32 [3, 3, 256, 256], replicated
- temporal_grad: float32 [3, 256, 256], replicated
The draws below stay inside these ranges and needn't reach their ends.
All inputs are finite; a program needn't handle non-finite values.
Results may differ from the reference program's by a relative error of at most 0.0054.
Values may be sent and summed in bfloat16 or wider, within the bound.
No kernel may reach another device: no remote copies, remote signals or barrier semaphores. Data moves between devices by JAX's collectives and lax.ppermute only.
A program may use at most 64 MiB of HBM per device.

```python
import jax
import jax.numpy as jnp

C = 256
COLS = 128
CLIPS = 2
FRAMES = 32
ROWS = 64
PIXELS = 524288


def level_of(stream_key, extent, shards, low, largest):
    gain = 1.0
    for position, shards_of in shards:
        steps = jax.random.uniform(jax.random.fold_in(jax.random.fold_in(stream_key, 6), position), (shards_of,), jnp.float32, low / len(shards), largest / len(shards))
        gain = gain * jnp.repeat(jnp.exp(steps), extent[position] // shards_of).reshape((-1,) + (1,) * (len(extent) - 1 - position))
    return gain


def centred(own_key, extent, deviation, most, cuts=(), kind=jnp.bfloat16):
    entries = deviation * jax.random.normal(own_key, extent, jnp.float32)
    if cuts:
        entries = entries * level_of(own_key, extent, cuts, -0.22, 0.18)
    return jnp.clip(entries, -most, most).astype(kind)


def setup_inputs(seed: int = 0) -> dict:
    arg_keys = jax.random.split(jax.random.key(seed), 5)
    return {
        "frames_in": centred(arg_keys[0], (CLIPS, FRAMES, ROWS, COLS, C), 1.0, 6.0, ((0, 2), (1, 16), (2, 8))),
        "cotangent": centred(arg_keys[1], (CLIPS, FRAMES, ROWS, COLS, C), 1.0, 6.0, ((0, 2), (1, 16), (2, 8))),
        "spatial_weight": centred(arg_keys[2], (3, 3, C, C), (9 * C) ** -0.5, 0.125),
        "temporal_weight": centred(arg_keys[3], (3, C, C), (3 * C) ** -0.5, 0.21875),
    }


def spatial_conv(padded, kernel, height, width):
    chans = padded.shape[-1]
    total = jnp.zeros((padded.shape[0] * height * width, kernel.shape[-1]), jnp.float32)
    for i in range(3):
        for j in range(3):
            window = padded[:, i:i + height, j:j + width, :].reshape(-1, chans)
            total = total + jnp.dot(window, kernel[i, j], preferred_element_type=jnp.float32)
    return total.reshape(padded.shape[0], height, width, kernel.shape[-1])

def reference(frames_in, cotangent, spatial_weight, temporal_weight):
    outs, grads = ([], [])
    wgrad_s = jnp.zeros((3, 3, C, C), jnp.float32)
    wgrad_t = jnp.zeros((3, C, C), jnp.float32)
    flipped = jnp.transpose(spatial_weight, (0, 1, 3, 2))[::-1, ::-1]
    for clip_idx in range(CLIPS):
        xin = frames_in[clip_idx]
        dyv = cotangent[clip_idx]
        nfr, height, width = (xin.shape[0], xin.shape[1], xin.shape[2])
        xpad = jnp.pad(xin, ((0, 0), (1, 1), (1, 1), (0, 0)))
        pre = spatial_conv(xpad, spatial_weight, height, width)
        act = jax.nn.silu(pre).astype(jnp.bfloat16)
        actpad = jnp.pad(act, ((2, 0), (0, 0), (0, 0), (0, 0)))
        dypad = jnp.pad(dyv, ((0, 2), (0, 0), (0, 0), (0, 0)))
        mixed = jnp.zeros((nfr * height * width, C), jnp.float32)
        agrad = jnp.zeros((nfr * height * width, C), jnp.float32)
        dyflat = dyv.reshape(-1, C)
        for k in range(3):
            past = actpad[2 - k:2 - k + nfr].reshape(-1, C)
            mixed = mixed + jnp.dot(past, temporal_weight[k], preferred_element_type=jnp.float32)
            ahead = dypad[k:k + nfr].reshape(-1, C)
            agrad = agrad + jnp.dot(ahead, temporal_weight[k].T, preferred_element_type=jnp.float32)
            wgrad_t = wgrad_t.at[k].add(jnp.dot(past.T, dyflat, preferred_element_type=jnp.float32))
        mixed = mixed.astype(jnp.bfloat16).reshape(xin.shape)
        outs.append((xin.astype(jnp.float32) + mixed.astype(jnp.float32)).astype(jnp.bfloat16))
        agrad = agrad.astype(jnp.bfloat16).reshape(xin.shape)
        sig = jax.nn.sigmoid(pre)
        pgrad = (agrad.astype(jnp.float32) * sig * (1.0 + pre * (1.0 - sig))).astype(jnp.bfloat16)
        pflat = pgrad.reshape(-1, C)
        for i in range(3):
            for j in range(3):
                window = xpad[:, i:i + height, j:j + width, :].reshape(-1, C)
                wgrad_s = wgrad_s.at[i, j].add(jnp.dot(window.T, pflat, preferred_element_type=jnp.float32))
        ppad = jnp.pad(pgrad, ((0, 0), (1, 1), (1, 1), (0, 0)))
        back = spatial_conv(ppad, flipped, height, width)
        grads.append((dyv.astype(jnp.float32) + back).astype(jnp.bfloat16))
    scale = 1.0 / jnp.sqrt(jnp.float32(PIXELS))
    return (jnp.stack(outs), jnp.stack(grads), wgrad_s * scale, wgrad_t * scale)
```

```python
import functools

import jax
import jax.numpy as jnp
from jax import lax
from jax.experimental import pallas as pl
from jax.experimental.pallas import tpu as pltpu
from jax.sharding import Mesh, PartitionSpec as P

BF = jnp.bfloat16
F32 = jnp.float32
TM = ("y", "zl")
SPACE = ("x", "core")
PLANE = ("y", "x")
COLUMN = ("clip", "zl")
COLS = 128
NT = (((1,), (1,)), ((), ()))


def call(kernel, outs, ins, scratch=(), flops=0, moved=0, limit=32, smem=()):
    vmem = pl.BlockSpec(memory_space=pltpu.VMEM)
    specs = [pl.BlockSpec(memory_space=pltpu.SMEM) if i in smem else vmem for i in range(len(ins))]
    return pl.pallas_call(
        kernel,
        out_shape=outs,
        in_specs=specs,
        out_specs=jax.tree.map(lambda _: vmem, outs),
        scratch_shapes=list(scratch),
        cost_estimate=pl.CostEstimate(flops=flops, bytes_accessed=moved, transcendentals=0),
        compiler_params=pltpu.CompilerParams(vmem_limit_bytes=limit << 20),
    )(*ins)


def shape(dims, kind=BF):
    return jax.ShapeDtypeStruct(dims, kind)


def shifted(value, column, step):
    edge = 0 if step == 1 else COLS - 1
    rolled = pltpu.roll(value, step % value.shape[0], 0)
    return jnp.where(column == edge, 0.0, rolled)


def columns_of(rows, width):
    return lax.broadcasted_iota(jnp.int32, (rows, width), 0) % COLS


def window(ref, frame, start, rows, offsets):
    parts = [ref[frame, pl.ds(start + off * COLS, rows), :] for off in offsets]
    return jnp.concatenate(parts, axis=1)


CHUNK = 512


def fill(padded, block, top, bottom, frame):
    size = block.shape[1]
    padded[frame, 0:COLS, :] = top[frame]
    padded[frame, COLS : COLS + size, :] = block[frame]
    padded[frame, COLS + size :, :] = bottom[frame]


def forward_kernel(x, top, bottom, weight, act, slope, x_t, act_t, padded):
    frames, size, chans = x.shape
    for f in range(frames):
        fill(padded, x, top, bottom, f)

    @pl.loop(0, frames * (size // CHUNK))
    def _(step):
        f = step // (size // CHUNK)
        start = pl.multiple_of((step % (size // CHUNK)) * CHUNK, CHUNK)
        rows = window(padded, f, start, CHUNK, (0, 1, 2))
        column = columns_of(CHUNK, chans)
        z = [
            jnp.dot(rows, weight[:, j].reshape(3 * chans, chans), preferred_element_type=F32)
            for j in range(3)
        ]
        pre = shifted(z[0], column, 1) + z[1] + shifted(z[2], column, -1)
        sigma = 1.0 / (1.0 + jnp.exp(-pre))
        active = (pre * sigma).astype(BF)
        act[f, pl.ds(start, CHUNK), :] = active
        slope[f, pl.ds(start, CHUNK), :] = sigma * (1.0 + pre * (1.0 - sigma))
        act_t[f, :, pl.ds(start, CHUNK)] = active.T

    for f in range(frames):
        x_t[f] = padded[f].T


def gradient_kernel(core, dy, ahead, weight, slope, x_t, act_t, pgrad, keep, send, dyx, wide, terms):
    frames, size, chans = dy.shape
    for f in range(frames):
        dyx[f * size : (f + 1) * size, :] = dy[f]
        dyx[(frames + f) * size : (frames + f + 1) * size, :] = ahead[f]

    @pl.loop(0, frames * (size // CHUNK))
    def _(step):
        start = pl.multiple_of(step * CHUNK, CHUNK)
        rows = jnp.concatenate([dyx[pl.ds(start + k * size, CHUNK), :] for k in range(3)], axis=1)
        taps = jnp.concatenate([weight[k] for k in range(3)], axis=1)
        agrad = lax.dot_general(rows, taps, NT, preferred_element_type=F32).astype(BF)
        grad = (agrad.astype(F32) * slope[pl.ds(start, CHUNK), :]).astype(BF)
        pgrad[pl.ds(start, CHUNK), :] = grad
        full = grad.astype(F32)
        column = columns_of(CHUNK, chans)
        wide[0, pl.ds(start, CHUNK), :] = shifted(full, column, -1).astype(BF)
        wide[1, pl.ds(start, CHUNK), :] = grad
        wide[2, pl.ds(start, CHUNK), :] = shifted(full, column, 1).astype(BF)

    left = jnp.concatenate(
        [
            jnp.concatenate([x_t[f, :, i * COLS : i * COLS + size] for f in range(frames)], axis=1)
            for i in range(3)
        ],
        axis=0,
    )
    for j in range(3):
        out = jnp.dot(left, wide[j], preferred_element_type=F32).astype(BF)
        for i in range(3):
            for h in range(2):
                at = ((3 * i + j) * 2 + h) * chans
                terms[at : at + chans, :] = out[i * chans : (i + 1) * chans, h * 128 : (h + 1) * 128]
    left_t = jnp.concatenate([act_t[f] for f in range(frames)], axis=1)
    for k in range(3):
        right = dyx[k * size : (k + frames) * size, :]
        out = jnp.dot(left_t, right, preferred_element_type=F32).astype(BF)
        for h in range(2):
            at = ((9 + k) * 2 + h) * chans
            terms[at : at + chans, :] = out[:, h * 128 : (h + 1) * 128]
    half = terms.shape[0] // 2
    for c in range(2):

        @pl.when(core[0] == c)
        def _():
            keep[...] = terms[c * half : (c + 1) * half, :]
            send[...] = terms[(1 - c) * half : (2 - c) * half, :]


def add_kernel(a, b, out):
    out[...] = (a[...].astype(F32) + b[...].astype(F32)).astype(BF)


def sum_kernel(scale, parts, out):
    total = parts[0].astype(F32)
    for i in range(1, parts.shape[0]):
        total = total + parts[i].astype(F32)
    out[...] = (total * scale).astype(out.dtype)


def spread_kernel(value, out):
    for i in range(out.shape[0]):
        out[i] = value[...].astype(out.dtype)


def final_kernel(core, own, other, spatial, temporal):
    half = own.shape[0] // 2
    for c in range(2):

        @pl.when(core[0] == c)
        def _():
            for t in range(12):
                source = own if t // 6 == c else other
                at = (t % 6) * 512
                for h in range(2):
                    part = source[at + h * 256 : at + (h + 1) * 256, :].astype(F32)
                    if t < 9:
                        spatial[t, :, h * 128 : (h + 1) * 128] = part
                    else:
                        temporal[t - 9, :, h * 128 : (h + 1) * 128] = part


def back_kernel(grad, top, bottom, weight, dy, out, padded):
    frames, size, chans = dy.shape
    for f in range(frames):
        fill(padded, grad, top, bottom, f)

    @pl.loop(0, frames * (size // CHUNK))
    def _(step):
        f = step // (size // CHUNK)
        start = pl.multiple_of((step % (size // CHUNK)) * CHUNK, CHUNK)
        rows = window(padded, f, start, CHUNK, (2, 1, 0))
        column = columns_of(CHUNK, chans)
        z = [
            lax.dot_general(
                rows,
                jnp.concatenate([weight[i, j] for i in range(3)], axis=1),
                NT,
                preferred_element_type=F32,
            )
            for j in range(3)
        ]
        back = shifted(z[0], column, -1) + z[1] + shifted(z[2], column, 1)
        out[f, pl.ds(start, CHUNK), :] = (dy[f, pl.ds(start, CHUNK), :].astype(F32) + back).astype(BF)


def mix_kernel(act, behind, weight, x, out, ext):
    frames, size, chans = act.shape
    for f in range(frames):
        ext[f * size : (f + 1) * size, :] = behind[f]
        ext[(frames + f) * size : (frames + f + 1) * size, :] = act[f]

    @pl.loop(0, frames * (size // CHUNK))
    def _(step):
        start = pl.multiple_of(step * CHUNK, CHUNK)
        rows = jnp.concatenate(
            [ext[pl.ds(start + (2 - k) * size, CHUNK), :] for k in range(3)], axis=1
        )
        mixed = jnp.dot(rows, weight[...].reshape(3 * chans, chans), preferred_element_type=F32)
        own = x[pl.ds(start, CHUNK), :].astype(F32)
        out[pl.ds(start, CHUNK), :] = (own + mixed.astype(BF).astype(F32)).astype(BF)


def steps(axes, by):
    count = lax.axis_size(axes)
    return [(i, i + by) for i in range(count) if 0 <= i + by < count]


def exchange(value, axes):
    return lax.all_to_all(value, axes, split_axis=0, concat_axis=0, tiled=True)


def rims(block):
    size = block.shape[1]
    top = lax.ppermute(block[:, size - COLS :, :], SPACE, steps(SPACE, 1))
    bottom = lax.ppermute(block[:, :COLS, :], SPACE, steps(SPACE, -1))
    return top, bottom


def local(scale, frames_in, cotangent, spatial_weight, temporal_weight):
    dims = frames_in.shape
    frames, chans = dims[1], dims[4]
    size = dims[2] * dims[3]
    x = frames_in.reshape(frames, size, chans)
    dy = cotangent.reshape(frames, size, chans)
    work = 2 * frames * size * chans * chans
    core = lax.axis_index("core").astype(jnp.int32).reshape(1)
    top, bottom = rims(x)
    ahead = lax.ppermute(dy, TM, steps(TM, -1))
    act, slope, x_t, act_t = call(
        forward_kernel,
        [
            shape((frames, size, chans)),
            shape((frames, size, chans), F32),
            shape((frames, chans, size + 2 * COLS)),
            shape((frames, chans, size)),
        ],
        (x, top, bottom, spatial_weight),
        [pltpu.VMEM((frames, size + 2 * COLS, chans), BF)],
        flops=9 * work,
        moved=9 << 20,
    )
    act_later, ahead = lax.optimization_barrier((act, ahead))
    behind = lax.ppermute(act_later, TM, steps(TM, 1))
    flat = frames * size
    rows = 12 * chans
    pgrad, keep, send = call(
        gradient_kernel,
        [shape((flat, chans)), shape((rows, 128)), shape((rows, 128))],
        (core, dy, ahead, temporal_weight, slope.reshape(flat, chans), x_t, act_t),
        [
            pltpu.VMEM((2 * flat, chans), BF),
            pltpu.VMEM((3, flat, chans), BF),
            pltpu.VMEM((2 * rows, 128), BF),
        ],
        flops=15 * work,
        moved=11 << 20,
        smem=(0,),
    )
    got = lax.ppermute(send, "core", [(0, 1), (1, 0)])
    pgrad = pgrad.reshape(frames, size, chans)
    half = call(add_kernel, shape((rows, 128)), (keep, got), moved=3 << 20)
    plane, column = lax.axis_size(PLANE), lax.axis_size(COLUMN)
    share = rows // plane
    piece = share // column
    first = exchange(half.reshape(plane, share, 128), PLANE)
    grad_top, grad_bottom = rims(pgrad)
    part = call(functools.partial(sum_kernel, 1.0), shape((share, 128), F32), (first,), moved=1 << 20)
    second = exchange(part.reshape(column, piece, 128), COLUMN)
    total = call(functools.partial(sum_kernel, scale), shape((piece, 128), F32), (second,), moved=1 << 17)
    spread = call(spread_kernel, shape((column, piece, 128), F32), (total,), moved=1 << 17)
    third = exchange(spread, COLUMN).reshape(share, 128)
    wider = call(spread_kernel, shape((plane, share, 128)), (third,), moved=1 << 20)
    own = exchange(wider, PLANE).reshape(rows, 128)
    other = lax.ppermute(own, "core", [(0, 1), (1, 0)])
    spatial, temporal = call(
        final_kernel,
        [shape((9, chans, chans), F32), shape((3, chans, chans), F32)],
        (core, own, other),
        moved=5 << 20,
        smem=(0,),
    )
    input_grad = call(
        back_kernel,
        shape((frames, size, chans)),
        (pgrad, grad_top, grad_bottom, spatial_weight, dy),
        [pltpu.VMEM((frames, size + 2 * COLS, chans), BF)],
        flops=9 * work,
        moved=5 << 20,
    )
    block_out = call(
        mix_kernel,
        shape((flat, chans)),
        (act, behind, temporal_weight, x.reshape(flat, chans)),
        [pltpu.VMEM((2 * flat, chans), BF)],
        flops=3 * work,
        moved=4 << 20,
    )
    return (
        block_out.reshape(dims),
        input_grad.reshape(dims),
        spatial.reshape(3, 3, chans, chans),
        temporal,
    )


def solution(mesh):
    fine = Mesh(mesh.devices.reshape(2, 4, 4, 4, 2), ("clip", "y", "zl", "x", "core"))
    blocks = P("clip", TM, SPACE, None, None)

    def run(frames_in, cotangent, spatial_weight, temporal_weight):
        clips, frames, height, width, _ = frames_in.shape
        scale = (clips * frames * height * width) ** -0.5
        return jax.shard_map(
            functools.partial(local, scale),
            mesh=fine,
            in_specs=(blocks, blocks, P(), P()),
            out_specs=(blocks, blocks, P(), P()),
            check_vma=False,
        )(frames_in, cotangent, spatial_weight, temporal_weight)

    return run
```

```python
import functools

import jax
import jax.numpy as jnp
from jax import lax
from jax.experimental import pallas as pl
from jax.experimental.pallas import tpu as pltpu
from jax.sharding import Mesh, PartitionSpec as P

BF = jnp.bfloat16
F32 = jnp.float32
TM = ("y", "zl")
SPACE = ("x", "core")
PLANE = ("x", "y")
COLS = 128
NT = (((1,), (1,)), ((), ()))


def call(kernel, outs, ins, scratch=(), flops=0, moved=0, limit=32, smem=()):
    vmem = pl.BlockSpec(memory_space=pltpu.VMEM)
    specs = [pl.BlockSpec(memory_space=pltpu.SMEM) if i in smem else vmem for i in range(len(ins))]
    return pl.pallas_call(
        kernel,
        out_shape=outs,
        in_specs=specs,
        out_specs=jax.tree.map(lambda _: vmem, outs),
        scratch_shapes=list(scratch),
        cost_estimate=pl.CostEstimate(flops=flops, bytes_accessed=moved, transcendentals=0),
        compiler_params=pltpu.CompilerParams(vmem_limit_bytes=limit << 20),
    )(*ins)


def shape(dims, kind=BF):
    return jax.ShapeDtypeStruct(dims, kind)


def shifted(value, column, step):
    edge = 0 if step == 1 else COLS - 1
    rolled = pltpu.roll(value, step % value.shape[0], 0)
    return jnp.where(column == edge, 0.0, rolled)


def columns_of(rows, width):
    return lax.broadcasted_iota(jnp.int32, (rows, width), 0) % COLS


def window(ref, frame, start, rows, offsets):
    parts = [ref[frame, pl.ds(start + off * COLS, rows), :] for off in offsets]
    return jnp.concatenate(parts, axis=1)


CHUNK = 512


def fill(padded, block, top, bottom, frame):
    size = block.shape[1]
    padded[frame, 0:COLS, :] = top[frame]
    padded[frame, COLS : COLS + size, :] = block[frame]
    padded[frame, COLS + size :, :] = bottom[frame]


def forward_kernel(x, top, bottom, weight, act, slope, x_t, act_t, padded):
    frames, size, chans = x.shape
    for f in range(frames):
        fill(padded, x, top, bottom, f)

    @pl.loop(0, frames * (size // CHUNK))
    def _(step):
        f = step // (size // CHUNK)
        start = pl.multiple_of((step % (size // CHUNK)) * CHUNK, CHUNK)
        rows = window(padded, f, start, CHUNK, (0, 1, 2))
        column = columns_of(CHUNK, chans)
        z = [
            jnp.dot(rows, weight[:, j].reshape(3 * chans, chans), preferred_element_type=F32)
            for j in range(3)
        ]
        pre = shifted(z[0], column, 1) + z[1] + shifted(z[2], column, -1)
        sigma = 1.0 / (1.0 + jnp.exp(-pre))
        active = (pre * sigma).astype(BF)
        act[f, pl.ds(start, CHUNK), :] = active
        slope[f, pl.ds(start, CHUNK), :] = sigma * (1.0 + pre * (1.0 - sigma))
        act_t[f, :, pl.ds(start, CHUNK)] = active.T

    for f in range(frames):
        x_t[f] = padded[f].T


def early_kernel(dy, weight, act_t, partial, terms):
    frames, size, chans = dy.shape

    @pl.loop(0, size // CHUNK)
    def _(step):
        at = pl.ds(pl.multiple_of(step * CHUNK, CHUNK), CHUNK)
        second = dy[1, at, :]
        both = jnp.concatenate([dy[0, at, :], second], axis=1)
        taps = jnp.concatenate([weight[0], weight[1]], axis=1)
        partial[0, at, :] = lax.dot_general(both, taps, NT, preferred_element_type=F32)
        partial[1, at, :] = lax.dot_general(second, weight[0], NT, preferred_element_type=F32)

    left = jnp.concatenate([act_t[0], act_t[1]], axis=1)
    right = dy[...].reshape(frames * size, chans)
    terms[0] = jnp.dot(left, right, preferred_element_type=F32)
    terms[1] = jnp.dot(act_t[0], dy[1], preferred_element_type=F32)


def gradient_kernel(
    core, ahead, weight, slope, x_t, act_t, partial, early, pgrad, keep, send, wide, terms
):
    frames, size, chans = ahead.shape

    def finish(f, start, agrad):
        at = pl.ds(start, CHUNK)
        grad = (agrad.astype(BF).astype(F32) * slope[f, at, :]).astype(BF)
        pgrad[f, at, :] = grad
        full = grad.astype(F32)
        column = columns_of(CHUNK, chans)
        into = pl.ds(f * size + start, CHUNK)
        wide[0, into, :] = shifted(full, column, -1).astype(BF)
        wide[1, into, :] = grad
        wide[2, into, :] = shifted(full, column, 1).astype(BF)

    @pl.loop(0, size // CHUNK)
    def _(step):
        start = pl.multiple_of(step * CHUNK, CHUNK)
        at = pl.ds(start, CHUNK)
        first = ahead[0, at, :]
        more = lax.dot_general(first, weight[2], NT, preferred_element_type=F32)
        finish(0, start, partial[0, at, :] + more)
        both = jnp.concatenate([first, ahead[1, at, :]], axis=1)
        taps = jnp.concatenate([weight[1], weight[2]], axis=1)
        more = lax.dot_general(both, taps, NT, preferred_element_type=F32)
        finish(1, start, partial[1, at, :] + more)

    left = jnp.concatenate(
        [
            jnp.concatenate([x_t[f, :, i * COLS : i * COLS + size] for f in range(frames)], axis=1)
            for i in range(3)
        ],
        axis=0,
    )

    def put(tap, value):
        for h in range(2):
            at = (tap * 2 + h) * chans
            terms[at : at + chans, :] = value[:, h * 128 : (h + 1) * 128].astype(BF)

    for j in range(3):
        out = jnp.dot(left, wide[j], preferred_element_type=F32)
        for i in range(3):
            put(3 * i + j, out[i * chans : (i + 1) * chans])
    put(9, early[0])
    put(10, early[1] + jnp.dot(act_t[1], ahead[0], preferred_element_type=F32))
    left_t = jnp.concatenate([act_t[0], act_t[1]], axis=1)
    right = ahead[...].reshape(frames * size, chans)
    put(11, jnp.dot(left_t, right, preferred_element_type=F32))
    half = terms.shape[0] // 2
    for c in range(2):

        @pl.when(core[0] == c)
        def _():
            keep[...] = terms[c * half : (c + 1) * half, :]
            send[...] = terms[(1 - c) * half : (2 - c) * half, :]


def add_kernel(a, b, out):
    out[...] = (a[...].astype(F32) + b[...].astype(F32)).astype(BF)


def sum_kernel(parts, out):
    total = parts[0].astype(F32)
    for i in range(1, parts.shape[0]):
        total = total + parts[i].astype(F32)
    out[...] = total.astype(out.dtype)


def last_kernel(scale, a, b, out):
    total = ((a[...] + b[...]) * scale).astype(out.dtype)
    for i in range(out.shape[0]):
        out[i] = total


def spread_kernel(value, out):
    for i in range(out.shape[0]):
        out[i] = value[...]


def final_kernel(core, own, other, spatial, temporal):
    half = own.shape[0] // 2
    for c in range(2):

        @pl.when(core[0] == c)
        def _():
            for t in range(12):
                source = own if t // 6 == c else other
                at = (t % 6) * 512
                for h in range(2):
                    part = source[at + h * 256 : at + (h + 1) * 256, :].astype(F32)
                    if t < 9:
                        spatial[t, :, h * 128 : (h + 1) * 128] = part
                    else:
                        temporal[t - 9, :, h * 128 : (h + 1) * 128] = part


def back_kernel(grad, top, bottom, weight, dy, out, padded):
    frames, size, chans = dy.shape
    for f in range(frames):
        fill(padded, grad, top, bottom, f)

    @pl.loop(0, frames * (size // CHUNK))
    def _(step):
        f = step // (size // CHUNK)
        start = pl.multiple_of((step % (size // CHUNK)) * CHUNK, CHUNK)
        rows = window(padded, f, start, CHUNK, (2, 1, 0))
        column = columns_of(CHUNK, chans)
        z = [
            lax.dot_general(
                rows,
                jnp.concatenate([weight[i, j] for i in range(3)], axis=1),
                NT,
                preferred_element_type=F32,
            )
            for j in range(3)
        ]
        back = shifted(z[0], column, -1) + z[1] + shifted(z[2], column, 1)
        out[f, pl.ds(start, CHUNK), :] = (dy[f, pl.ds(start, CHUNK), :].astype(F32) + back).astype(BF)


def mix_kernel(act, behind, weight, x, out, ext):
    frames, size, chans = act.shape
    for f in range(frames):
        ext[f * size : (f + 1) * size, :] = behind[f]
        ext[(frames + f) * size : (frames + f + 1) * size, :] = act[f]

    @pl.loop(0, frames * (size // CHUNK))
    def _(step):
        start = pl.multiple_of(step * CHUNK, CHUNK)
        rows = jnp.concatenate(
            [ext[pl.ds(start + (2 - k) * size, CHUNK), :] for k in range(3)], axis=1
        )
        mixed = jnp.dot(rows, weight[...].reshape(3 * chans, chans), preferred_element_type=F32)
        own = x[pl.ds(start, CHUNK), :].astype(F32)
        out[pl.ds(start, CHUNK), :] = (own + mixed.astype(BF).astype(F32)).astype(BF)


def steps(axes, by):
    count = lax.axis_size(axes)
    return [(i, i + by) for i in range(count) if 0 <= i + by < count]


def exchange(value, axes):
    return lax.all_to_all(value, axes, split_axis=0, concat_axis=0, tiled=True)


def rims(block):
    size = block.shape[1]
    top = lax.ppermute(block[:, size - COLS :, :], SPACE, steps(SPACE, 1))
    bottom = lax.ppermute(block[:, :COLS, :], SPACE, steps(SPACE, -1))
    return top, bottom


def local(scale, frames_in, cotangent, spatial_weight, temporal_weight):
    dims = frames_in.shape
    frames, chans = dims[1], dims[4]
    size = dims[2] * dims[3]
    x = frames_in.reshape(frames, size, chans)
    dy = cotangent.reshape(frames, size, chans)
    work = 2 * frames * size * chans * chans
    core = lax.axis_index("core").astype(jnp.int32).reshape(1)
    top, bottom = rims(x)
    ahead = lax.ppermute(dy, TM, steps(TM, -1))
    act, slope, x_t, act_t = call(
        forward_kernel,
        [
            shape((frames, size, chans)),
            shape((frames, size, chans), F32),
            shape((frames, chans, size + 2 * COLS)),
            shape((frames, chans, size)),
        ],
        (x, top, bottom, spatial_weight),
        [pltpu.VMEM((frames, size + 2 * COLS, chans), BF)],
        flops=9 * work,
        moved=9 << 20,
    )
    partial, early = call(
        early_kernel,
        [shape((frames, size, chans), F32), shape((2, chans, chans), F32)],
        (dy, temporal_weight, act_t),
        flops=6 * work,
        moved=6 << 20,
    )
    act_later, ahead = lax.optimization_barrier((act, ahead))
    behind = lax.ppermute(act_later, TM, steps(TM, 1))
    flat = frames * size
    rows = 12 * chans
    pgrad, keep, send = call(
        gradient_kernel,
        [shape((frames, size, chans)), shape((rows, 128)), shape((rows, 128))],
        (core, ahead, temporal_weight, slope, x_t, act_t, partial, early),
        [pltpu.VMEM((3, flat, chans), BF), pltpu.VMEM((2 * rows, 128), BF)],
        flops=12 * work,
        moved=11 << 20,
        smem=(0,),
    )
    grad_top, grad_bottom = rims(pgrad)
    input_grad = call(
        back_kernel,
        shape((frames, size, chans)),
        (pgrad, grad_top, grad_bottom, spatial_weight, dy),
        [pltpu.VMEM((frames, size + 2 * COLS, chans), BF)],
        flops=9 * work,
        moved=5 << 20,
    )
    block_out = call(
        mix_kernel,
        shape((flat, chans)),
        (act, behind, temporal_weight, x.reshape(flat, chans)),
        [pltpu.VMEM((2 * flat, chans), BF)],
        flops=3 * work,
        moved=4 << 20,
    )
    pair = [(0, 1), (1, 0)]
    got = lax.ppermute(send, "core", pair)
    half = call(add_kernel, shape((rows, 128)), (keep, got), moved=3 << 20)
    line, ring = lax.axis_size("x"), lax.axis_size(TM)
    share, piece = rows // line, rows // line // ring
    first = exchange(half.reshape(line, share, 128), "x")
    first, input_grad = lax.optimization_barrier((first, input_grad))
    part = call(sum_kernel, shape((share, 128)), (first,), moved=1 << 20)
    second = exchange(part.reshape(ring, piece, 128), TM)
    mine = call(sum_kernel, shape((piece, 128), F32), (second,), moved=1 << 18)
    theirs = lax.ppermute(mine, "clip", pair)
    near = lax.axis_size("zl")
    spread = call(
        functools.partial(last_kernel, scale), shape((near, piece, 128)), (mine, theirs), moved=1 << 17
    )
    third = exchange(spread, "zl").reshape(near * piece, 128)
    third, block_out = lax.optimization_barrier((third, block_out))
    plane = lax.axis_size(PLANE)
    wider = call(spread_kernel, shape((plane, near * piece, 128)), (third,), moved=1 << 20)
    own = exchange(wider, PLANE).reshape(rows, 128)
    other = lax.ppermute(own, "core", pair)
    spatial, temporal = call(
        final_kernel,
        [shape((9, chans, chans), F32), shape((3, chans, chans), F32)],
        (core, own, other),
        moved=5 << 20,
        smem=(0,),
    )
    return (
        block_out.reshape(dims),
        input_grad.reshape(dims),
        spatial.reshape(3, 3, chans, chans),
        temporal,
    )


def solution(mesh):
    fine = Mesh(mesh.devices.reshape(2, 4, 4, 4, 2), ("clip", "y", "zl", "x", "core"))
    blocks = P("clip", TM, SPACE, None, None)

    def run(frames_in, cotangent, spatial_weight, temporal_weight):
        clips, frames, height, width, _ = frames_in.shape
        scale = (clips * frames * height * width) ** -0.5
        return jax.shard_map(
            functools.partial(local, scale),
            mesh=fine,
            in_specs=(blocks, blocks, P(), P()),
            out_specs=(blocks, blocks, P(), P()),
            check_vma=False,
        )(frames_in, cotangent, spatial_weight, temporal_weight)

    return run
```

```python
import functools

import jax
import jax.numpy as jnp
from jax import lax
from jax.experimental import pallas as pl
from jax.experimental.pallas import tpu as pltpu
from jax.sharding import Mesh, PartitionSpec as P

BF = jnp.bfloat16
F32 = jnp.float32
TM = ("y", "zl")
SPACE = ("x", "core")
PLANE = ("x", "y")
REST = ("y", "clip", "zl")
COLUMN = ("clip", "zl")
COLS = 128
NT = (((1,), (1,)), ((), ()))


def call(kernel, outs, ins, scratch=(), flops=0, moved=0, limit=32, smem=(), after=()):
    vmem = pl.BlockSpec(memory_space=pltpu.VMEM)
    specs = [pl.BlockSpec(memory_space=pltpu.SMEM) if i in smem else vmem for i in range(len(ins))]
    specs += [pl.BlockSpec(memory_space=pltpu.HBM)] * len(after)
    count = len(ins)

    def body(*refs):
        kernel(*refs[:count], *refs[count + len(after) :])

    return pl.pallas_call(
        body,
        out_shape=outs,
        in_specs=specs,
        out_specs=jax.tree.map(lambda _: vmem, outs),
        scratch_shapes=list(scratch),
        cost_estimate=pl.CostEstimate(flops=flops, bytes_accessed=moved, transcendentals=0),
        compiler_params=pltpu.CompilerParams(vmem_limit_bytes=limit << 20),
    )(*ins, *after)


def shape(dims, kind=BF):
    return jax.ShapeDtypeStruct(dims, kind)


def shifted(value, column, step):
    edge = 0 if step == 1 else COLS - 1
    rolled = pltpu.roll(value, step % value.shape[0], 0)
    return jnp.where(column == edge, 0.0, rolled)


def columns_of(rows, width):
    return lax.broadcasted_iota(jnp.int32, (rows, width), 0) % COLS


def window(ref, frame, start, rows, offsets):
    parts = [ref[frame, pl.ds(start + off * COLS, rows), :] for off in offsets]
    return jnp.concatenate(parts, axis=1)


CHUNK = 512


def fill(padded, block, top, bottom, frame):
    size = block.shape[1]
    padded[frame, 0:COLS, :] = top[frame]
    padded[frame, COLS : COLS + size, :] = block[frame]
    padded[frame, COLS + size :, :] = bottom[frame]


def forward_kernel(x, top, bottom, weight, act, slope, x_t, act_t, padded):
    frames, size, chans = x.shape
    for f in range(frames):
        fill(padded, x, top, bottom, f)

    @pl.loop(0, frames * (size // CHUNK))
    def _(step):
        f = step // (size // CHUNK)
        start = pl.multiple_of((step % (size // CHUNK)) * CHUNK, CHUNK)
        rows = window(padded, f, start, CHUNK, (0, 1, 2))
        column = columns_of(CHUNK, chans)
        z = [
            jnp.dot(rows, weight[:, j].reshape(3 * chans, chans), preferred_element_type=F32)
            for j in range(3)
        ]
        pre = shifted(z[0], column, 1) + z[1] + shifted(z[2], column, -1)
        sigma = 1.0 / (1.0 + jnp.exp(-pre))
        active = (pre * sigma).astype(BF)
        act[f, pl.ds(start, CHUNK), :] = active
        slope[f, pl.ds(start, CHUNK), :] = sigma * (1.0 + pre * (1.0 - sigma))
        act_t[f, :, pl.ds(start, CHUNK)] = active.T

    for f in range(frames):
        x_t[f] = padded[f].T


def early_kernel(dy, weight, act_t, partial, terms):
    frames, size, chans = dy.shape

    @pl.loop(0, size // CHUNK)
    def _(step):
        at = pl.ds(pl.multiple_of(step * CHUNK, CHUNK), CHUNK)
        second = dy[1, at, :]
        both = jnp.concatenate([dy[0, at, :], second], axis=1)
        taps = jnp.concatenate([weight[0], weight[1]], axis=1)
        partial[0, at, :] = lax.dot_general(both, taps, NT, preferred_element_type=F32)
        partial[1, at, :] = lax.dot_general(second, weight[0], NT, preferred_element_type=F32)

    left = jnp.concatenate([act_t[0], act_t[1]], axis=1)
    right = dy[...].reshape(frames * size, chans)
    terms[0] = jnp.dot(left, right, preferred_element_type=F32)
    terms[1] = jnp.dot(act_t[0], dy[1], preferred_element_type=F32)


def gradient_kernel(
    core, ahead, weight, slope, x_t, act_t, partial, early, pgrad, keep, send, wide, terms
):
    frames, size, chans = ahead.shape

    def finish(f, start, agrad):
        at = pl.ds(start, CHUNK)
        grad = (agrad.astype(BF).astype(F32) * slope[f, at, :]).astype(BF)
        pgrad[f, at, :] = grad
        full = grad.astype(F32)
        column = columns_of(CHUNK, chans)
        into = pl.ds(f * size + start, CHUNK)
        wide[0, into, :] = shifted(full, column, -1).astype(BF)
        wide[1, into, :] = grad
        wide[2, into, :] = shifted(full, column, 1).astype(BF)

    @pl.loop(0, size // CHUNK)
    def _(step):
        start = pl.multiple_of(step * CHUNK, CHUNK)
        at = pl.ds(start, CHUNK)
        first = ahead[0, at, :]
        more = lax.dot_general(first, weight[2], NT, preferred_element_type=F32)
        finish(0, start, partial[0, at, :] + more)
        both = jnp.concatenate([first, ahead[1, at, :]], axis=1)
        taps = jnp.concatenate([weight[1], weight[2]], axis=1)
        more = lax.dot_general(both, taps, NT, preferred_element_type=F32)
        finish(1, start, partial[1, at, :] + more)

    left = jnp.concatenate(
        [
            jnp.concatenate([x_t[f, :, i * COLS : i * COLS + size] for f in range(frames)], axis=1)
            for i in range(3)
        ],
        axis=0,
    )

    def put(tap, value):
        for h in range(2):
            at = (tap * 2 + h) * chans
            terms[at : at + chans, :] = value[:, h * 128 : (h + 1) * 128].astype(BF)

    for j in range(3):
        out = jnp.dot(left, wide[j], preferred_element_type=F32)
        for i in range(3):
            put(3 * i + j, out[i * chans : (i + 1) * chans])
    put(9, early[0])
    put(10, early[1] + jnp.dot(act_t[1], ahead[0], preferred_element_type=F32))
    left_t = jnp.concatenate([act_t[0], act_t[1]], axis=1)
    right = ahead[...].reshape(frames * size, chans)
    put(11, jnp.dot(left_t, right, preferred_element_type=F32))
    half = terms.shape[0] // 2
    for c in range(2):

        @pl.when(core[0] == c)
        def _():
            keep[...] = terms[c * half : (c + 1) * half, :]
            send[...] = terms[(1 - c) * half : (2 - c) * half, :]


def add_kernel(a, b, out):
    out[...] = (a[...].astype(F32) + b[...].astype(F32)).astype(BF)


def sum_kernel(parts, out):
    total = parts[0].astype(F32)
    for i in range(1, parts.shape[0]):
        total = total + parts[i].astype(F32)
    out[...] = total.astype(out.dtype)


def last_kernel(scale, parts, out):
    total = parts[0].astype(F32)
    for i in range(1, parts.shape[0]):
        total = total + parts[i].astype(F32)
    total = (total * scale).astype(out.dtype)
    for i in range(out.shape[0]):
        out[i] = total


def spread_kernel(value, out):
    for i in range(out.shape[0]):
        out[i] = value[...]


def final_kernel(core, own, other, spatial, temporal):
    half = own.shape[0] // 2
    for c in range(2):

        @pl.when(core[0] == c)
        def _():
            for t in range(12):
                source = own if t // 6 == c else other
                at = (t % 6) * 512
                for h in range(2):
                    part = source[at + h * 256 : at + (h + 1) * 256, :].astype(F32)
                    if t < 9:
                        spatial[t, :, h * 128 : (h + 1) * 128] = part
                    else:
                        temporal[t - 9, :, h * 128 : (h + 1) * 128] = part


def back_kernel(grad, top, bottom, weight, dy, out, padded):
    frames, size, chans = dy.shape
    for f in range(frames):
        fill(padded, grad, top, bottom, f)

    @pl.loop(0, frames * (size // CHUNK))
    def _(step):
        f = step // (size // CHUNK)
        start = pl.multiple_of((step % (size // CHUNK)) * CHUNK, CHUNK)
        rows = window(padded, f, start, CHUNK, (2, 1, 0))
        column = columns_of(CHUNK, chans)
        z = [
            lax.dot_general(
                rows,
                jnp.concatenate([weight[i, j] for i in range(3)], axis=1),
                NT,
                preferred_element_type=F32,
            )
            for j in range(3)
        ]
        back = shifted(z[0], column, -1) + z[1] + shifted(z[2], column, 1)
        out[f, pl.ds(start, CHUNK), :] = (dy[f, pl.ds(start, CHUNK), :].astype(F32) + back).astype(BF)


def mix_kernel(act, behind, weight, x, out, ext):
    frames, size, chans = act.shape
    for f in range(frames):
        ext[f * size : (f + 1) * size, :] = behind[f]
        ext[(frames + f) * size : (frames + f + 1) * size, :] = act[f]

    @pl.loop(0, frames * (size // CHUNK))
    def _(step):
        start = pl.multiple_of(step * CHUNK, CHUNK)
        rows = jnp.concatenate(
            [ext[pl.ds(start + (2 - k) * size, CHUNK), :] for k in range(3)], axis=1
        )
        mixed = jnp.dot(rows, weight[...].reshape(3 * chans, chans), preferred_element_type=F32)
        own = x[pl.ds(start, CHUNK), :].astype(F32)
        out[pl.ds(start, CHUNK), :] = (own + mixed.astype(BF).astype(F32)).astype(BF)


def steps(axes, by):
    count = lax.axis_size(axes)
    return [(i, i + by) for i in range(count) if 0 <= i + by < count]


def exchange(value, axes):
    return lax.all_to_all(value, axes, split_axis=0, concat_axis=0, tiled=True)


def rims(block):
    size = block.shape[1]
    top = lax.ppermute(block[:, size - COLS :, :], SPACE, steps(SPACE, 1))
    bottom = lax.ppermute(block[:, :COLS, :], SPACE, steps(SPACE, -1))
    return top, bottom


def local(scale, frames_in, cotangent, spatial_weight, temporal_weight):
    dims = frames_in.shape
    frames, chans = dims[1], dims[4]
    size = dims[2] * dims[3]
    x = frames_in.reshape(frames, size, chans)
    dy = cotangent.reshape(frames, size, chans)
    work = 2 * frames * size * chans * chans
    core = lax.axis_index("core").astype(jnp.int32).reshape(1)
    top, bottom = rims(x)
    ahead = lax.ppermute(dy, TM, steps(TM, -1))
    act, slope, x_t, act_t = call(
        forward_kernel,
        [
            shape((frames, size, chans)),
            shape((frames, size, chans), F32),
            shape((frames, chans, size + 2 * COLS)),
            shape((frames, chans, size)),
        ],
        (x, top, bottom, spatial_weight),
        [pltpu.VMEM((frames, size + 2 * COLS, chans), BF)],
        flops=9 * work,
        moved=9 << 20,
    )
    partial, early = call(
        early_kernel,
        [shape((frames, size, chans), F32), shape((2, chans, chans), F32)],
        (dy, temporal_weight, act_t),
        flops=6 * work,
        moved=6 << 20,
    )
    behind = lax.ppermute(act, TM, steps(TM, 1))
    flat = frames * size
    rows = 12 * chans
    pgrad, keep, send = call(
        gradient_kernel,
        [shape((frames, size, chans)), shape((rows, 128)), shape((rows, 128))],
        (core, ahead, temporal_weight, slope, x_t, act_t, partial, early),
        [pltpu.VMEM((3, flat, chans), BF), pltpu.VMEM((2 * rows, 128), BF)],
        flops=work // 16,
        moved=1 << 18,
        smem=(0,),
    )
    grad_top, grad_bottom = rims(pgrad)
    input_grad = call(
        back_kernel,
        shape((frames, size, chans)),
        (pgrad, grad_top, grad_bottom, spatial_weight, dy),
        [pltpu.VMEM((frames, size + 2 * COLS, chans), BF)],
        flops=9 * work,
        moved=5 << 20,
    )
    pair = [(0, 1), (1, 0)]
    got = lax.ppermute(send, "core", pair)
    half = call(add_kernel, shape((rows, 128)), (keep, got), moved=3 << 20)
    line, ring = lax.axis_size("x"), lax.axis_size(REST)
    share, piece = rows // line, rows // line // ring
    first = exchange(half.reshape(line, share, 128), "x")
    part = call(sum_kernel, shape((share, 128)), (first,), moved=1 << 18)
    second = exchange(part.reshape(ring, piece, 128), REST)
    column, plane = lax.axis_size(COLUMN), lax.axis_size(PLANE)
    spread = call(
        functools.partial(last_kernel, scale),
        shape((column, piece, 128)),
        (second,),
        moved=1 << 18,
        after=(input_grad, behind),
    )
    third = exchange(spread, COLUMN).reshape(column * piece, 128)
    wider = call(spread_kernel, shape((plane, column * piece, 128)), (third,), moved=1 << 18)
    own = exchange(wider, PLANE).reshape(rows, 128)
    block_out = call(
        mix_kernel,
        shape((flat, chans)),
        (act, behind, temporal_weight, x.reshape(flat, chans)),
        [pltpu.VMEM((2 * flat, chans), BF)],
        flops=3 * work,
        moved=4 << 20,
    )
    own, block_out = lax.optimization_barrier((own, block_out))
    other = lax.ppermute(own, "core", pair)
    spatial, temporal = call(
        final_kernel,
        [shape((9, chans, chans), F32), shape((3, chans, chans), F32)],
        (core, own, other),
        moved=5 << 20,
        smem=(0,),
    )
    return (
        block_out.reshape(dims),
        input_grad.reshape(dims),
        spatial.reshape(3, 3, chans, chans),
        temporal,
    )


def solution(mesh):
    fine = Mesh(mesh.devices.reshape(2, 4, 4, 4, 2), ("clip", "y", "zl", "x", "core"))
    blocks = P("clip", TM, SPACE, None, None)

    def run(frames_in, cotangent, spatial_weight, temporal_weight):
        clips, frames, height, width, _ = frames_in.shape
        scale = (clips * frames * height * width) ** -0.5
        return jax.shard_map(
            functools.partial(local, scale),
            mesh=fine,
            in_specs=(blocks, blocks, P(), P()),
            out_specs=(blocks, blocks, P(), P()),
            check_vma=False,
        )(frames_in, cotangent, spatial_weight, temporal_weight)

    return run
```

```python
import functools

import jax
import jax.numpy as jnp
from jax import lax
from jax.experimental import pallas as pl
from jax.experimental.pallas import tpu as pltpu
from jax.sharding import Mesh, PartitionSpec as P

BF = jnp.bfloat16
F32 = jnp.float32
TM = ("y", "zl")
SPACE = ("x", "core")
PLANE = ("x", "y")
COLUMN = ("clip", "zl")
COLS = 128
NT = (((1,), (1,)), ((), ()))


def call(kernel, outs, ins, scratch=(), flops=0, moved=0, limit=32, smem=(), after=()):
    vmem = pl.BlockSpec(memory_space=pltpu.VMEM)
    specs = [pl.BlockSpec(memory_space=pltpu.SMEM) if i in smem else vmem for i in range(len(ins))]
    specs += [pl.BlockSpec(memory_space=pltpu.HBM)] * len(after)
    count = len(ins)

    def body(*refs):
        kernel(*refs[:count], *refs[count + len(after) :])

    return pl.pallas_call(
        body,
        out_shape=outs,
        in_specs=specs,
        out_specs=jax.tree.map(lambda _: vmem, outs),
        scratch_shapes=list(scratch),
        cost_estimate=pl.CostEstimate(flops=flops, bytes_accessed=moved, transcendentals=0),
        compiler_params=pltpu.CompilerParams(vmem_limit_bytes=limit << 20),
    )(*ins, *after)


def shape(dims, kind=BF):
    return jax.ShapeDtypeStruct(dims, kind)


def shifted(value, column, step):
    edge = 0 if step == 1 else COLS - 1
    rolled = pltpu.roll(value, step % value.shape[0], 0)
    return jnp.where(column == edge, 0.0, rolled)


def columns_of(rows, width):
    return lax.broadcasted_iota(jnp.int32, (rows, width), 0) % COLS


def window(ref, frame, start, rows, offsets):
    parts = [ref[frame, pl.ds(start + off * COLS, rows), :] for off in offsets]
    return jnp.concatenate(parts, axis=1)


CHUNK = 512


def fill(padded, block, top, bottom, frame):
    size = block.shape[1]
    padded[frame, 0:COLS, :] = top[frame]
    padded[frame, COLS : COLS + size, :] = block[frame]
    padded[frame, COLS + size :, :] = bottom[frame]


def forward_kernel(x, top, bottom, weight, act, slope, x_t, act_t, padded):
    frames, size, chans = x.shape
    for f in range(frames):
        fill(padded, x, top, bottom, f)

    @pl.loop(0, frames * (size // CHUNK))
    def _(step):
        f = step // (size // CHUNK)
        start = pl.multiple_of((step % (size // CHUNK)) * CHUNK, CHUNK)
        rows = window(padded, f, start, CHUNK, (0, 1, 2))
        column = columns_of(CHUNK, chans)
        z = [
            jnp.dot(rows, weight[:, j].reshape(3 * chans, chans), preferred_element_type=F32)
            for j in range(3)
        ]
        pre = shifted(z[0], column, 1) + z[1] + shifted(z[2], column, -1)
        sigma = 1.0 / (1.0 + jnp.exp(-pre))
        active = (pre * sigma).astype(BF)
        act[f, pl.ds(start, CHUNK), :] = active
        slope[f, pl.ds(start, CHUNK), :] = sigma * (1.0 + pre * (1.0 - sigma))
        act_t[f, :, pl.ds(start, CHUNK)] = active.T

    for f in range(frames):
        x_t[f] = padded[f].T


def early_kernel(dy, weight, act_t, partial, terms):
    frames, size, chans = dy.shape

    @pl.loop(0, size // CHUNK)
    def _(step):
        at = pl.ds(pl.multiple_of(step * CHUNK, CHUNK), CHUNK)
        second = dy[1, at, :]
        both = jnp.concatenate([dy[0, at, :], second], axis=1)
        taps = jnp.concatenate([weight[0], weight[1]], axis=1)
        partial[0, at, :] = lax.dot_general(both, taps, NT, preferred_element_type=F32)
        partial[1, at, :] = lax.dot_general(second, weight[0], NT, preferred_element_type=F32)

    left = jnp.concatenate([act_t[0], act_t[1]], axis=1)
    right = dy[...].reshape(frames * size, chans)
    terms[0] = jnp.dot(left, right, preferred_element_type=F32)
    terms[1] = jnp.dot(act_t[0], dy[1], preferred_element_type=F32)


def gradient_kernel(
    core, ahead, weight, slope, x_t, act_t, partial, early, pgrad, keep, send, wide, terms
):
    frames, size, chans = ahead.shape

    def finish(f, start, agrad):
        at = pl.ds(start, CHUNK)
        grad = (agrad.astype(BF).astype(F32) * slope[f, at, :]).astype(BF)
        pgrad[f, at, :] = grad
        full = grad.astype(F32)
        column = columns_of(CHUNK, chans)
        into = pl.ds(f * size + start, CHUNK)
        wide[0, into, :] = shifted(full, column, -1).astype(BF)
        wide[1, into, :] = grad
        wide[2, into, :] = shifted(full, column, 1).astype(BF)

    @pl.loop(0, size // CHUNK)
    def _(step):
        start = pl.multiple_of(step * CHUNK, CHUNK)
        at = pl.ds(start, CHUNK)
        first = ahead[0, at, :]
        more = lax.dot_general(first, weight[2], NT, preferred_element_type=F32)
        finish(0, start, partial[0, at, :] + more)
        both = jnp.concatenate([first, ahead[1, at, :]], axis=1)
        taps = jnp.concatenate([weight[1], weight[2]], axis=1)
        more = lax.dot_general(both, taps, NT, preferred_element_type=F32)
        finish(1, start, partial[1, at, :] + more)

    left = jnp.concatenate(
        [
            jnp.concatenate([x_t[f, :, i * COLS : i * COLS + size] for f in range(frames)], axis=1)
            for i in range(3)
        ],
        axis=0,
    )

    def put(tap, value):
        for h in range(2):
            at = (tap * 2 + h) * chans
            terms[at : at + chans, :] = value[:, h * 128 : (h + 1) * 128].astype(BF)

    for j in range(3):
        out = jnp.dot(left, wide[j], preferred_element_type=F32)
        for i in range(3):
            put(3 * i + j, out[i * chans : (i + 1) * chans])
    put(9, early[0])
    put(10, early[1] + jnp.dot(act_t[1], ahead[0], preferred_element_type=F32))
    left_t = jnp.concatenate([act_t[0], act_t[1]], axis=1)
    right = ahead[...].reshape(frames * size, chans)
    put(11, jnp.dot(left_t, right, preferred_element_type=F32))
    half = terms.shape[0] // 2
    for c in range(2):

        @pl.when(core[0] == c)
        def _():
            keep[...] = terms[c * half : (c + 1) * half, :]
            send[...] = terms[(1 - c) * half : (2 - c) * half, :]


def add_kernel(a, b, out):
    out[...] = (a[...].astype(F32) + b[...].astype(F32)).astype(BF)


def sum_kernel(parts, out):
    total = parts[0].astype(F32)
    for i in range(1, parts.shape[0]):
        total = total + parts[i].astype(F32)
    out[...] = total.astype(out.dtype)


def last_kernel(scale, parts, out):
    total = parts[0].astype(F32)
    for i in range(1, parts.shape[0]):
        total = total + parts[i].astype(F32)
    total = (total * scale).astype(out.dtype)
    for i in range(out.shape[0]):
        out[i] = total


def spread_kernel(value, out):
    for i in range(out.shape[0]):
        out[i] = value[...]


def final_kernel(core, own, other, spatial, temporal):
    half = own.shape[0] // 2
    for c in range(2):

        @pl.when(core[0] == c)
        def _():
            for t in range(12):
                source = own if t // 6 == c else other
                at = (t % 6) * 512
                for h in range(2):
                    part = source[at + h * 256 : at + (h + 1) * 256, :].astype(F32)
                    if t < 9:
                        spatial[t, :, h * 128 : (h + 1) * 128] = part
                    else:
                        temporal[t - 9, :, h * 128 : (h + 1) * 128] = part


def back_kernel(grad, top, bottom, weight, dy, out, padded):
    frames, size, chans = dy.shape
    for f in range(frames):
        fill(padded, grad, top, bottom, f)

    @pl.loop(0, frames * (size // CHUNK))
    def _(step):
        f = step // (size // CHUNK)
        start = pl.multiple_of((step % (size // CHUNK)) * CHUNK, CHUNK)
        rows = window(padded, f, start, CHUNK, (2, 1, 0))
        column = columns_of(CHUNK, chans)
        z = [
            lax.dot_general(
                rows,
                jnp.concatenate([weight[i, j] for i in range(3)], axis=1),
                NT,
                preferred_element_type=F32,
            )
            for j in range(3)
        ]
        back = shifted(z[0], column, -1) + z[1] + shifted(z[2], column, 1)
        out[f, pl.ds(start, CHUNK), :] = (dy[f, pl.ds(start, CHUNK), :].astype(F32) + back).astype(BF)


def mix_kernel(act, behind, weight, x, out, ext):
    frames, size, chans = act.shape
    for f in range(frames):
        ext[f * size : (f + 1) * size, :] = behind[f]
        ext[(frames + f) * size : (frames + f + 1) * size, :] = act[f]

    @pl.loop(0, frames * (size // CHUNK))
    def _(step):
        start = pl.multiple_of(step * CHUNK, CHUNK)
        rows = jnp.concatenate(
            [ext[pl.ds(start + (2 - k) * size, CHUNK), :] for k in range(3)], axis=1
        )
        mixed = jnp.dot(rows, weight[...].reshape(3 * chans, chans), preferred_element_type=F32)
        own = x[pl.ds(start, CHUNK), :].astype(F32)
        out[pl.ds(start, CHUNK), :] = (own + mixed.astype(BF).astype(F32)).astype(BF)


def steps(axes, by):
    count = lax.axis_size(axes)
    return [(i, i + by) for i in range(count) if 0 <= i + by < count]


def exchange(value, axes):
    return lax.all_to_all(value, axes, split_axis=0, concat_axis=0, tiled=True)


def rims(block):
    size = block.shape[1]
    top = lax.ppermute(block[:, size - COLS :, :], SPACE, steps(SPACE, 1))
    bottom = lax.ppermute(block[:, :COLS, :], SPACE, steps(SPACE, -1))
    return top, bottom


def local(scale, frames_in, cotangent, spatial_weight, temporal_weight):
    dims = frames_in.shape
    frames, chans = dims[1], dims[4]
    size = dims[2] * dims[3]
    x = frames_in.reshape(frames, size, chans)
    dy = cotangent.reshape(frames, size, chans)
    work = 2 * frames * size * chans * chans
    core = lax.axis_index("core").astype(jnp.int32).reshape(1)
    top, bottom = rims(x)
    ahead = lax.ppermute(dy, TM, steps(TM, -1))
    act, slope, x_t, act_t = call(
        forward_kernel,
        [
            shape((frames, size, chans)),
            shape((frames, size, chans), F32),
            shape((frames, chans, size + 2 * COLS)),
            shape((frames, chans, size)),
        ],
        (x, top, bottom, spatial_weight),
        [pltpu.VMEM((frames, size + 2 * COLS, chans), BF)],
        flops=9 * work,
        moved=9 << 20,
    )
    partial, early = call(
        early_kernel,
        [shape((frames, size, chans), F32), shape((2, chans, chans), F32)],
        (dy, temporal_weight, act_t),
        flops=6 * work,
        moved=6 << 20,
    )
    behind = lax.ppermute(act, TM, steps(TM, 1))
    flat = frames * size
    rows = 12 * chans
    pgrad, keep, send = call(
        gradient_kernel,
        [shape((frames, size, chans)), shape((rows, 128)), shape((rows, 128))],
        (core, ahead, temporal_weight, slope, x_t, act_t, partial, early),
        [pltpu.VMEM((3, flat, chans), BF), pltpu.VMEM((2 * rows, 128), BF)],
        flops=work // 16,
        moved=1 << 18,
        smem=(0,),
    )
    grad_top, grad_bottom = rims(pgrad)
    input_grad = call(
        back_kernel,
        shape((frames, size, chans)),
        (pgrad, grad_top, grad_bottom, spatial_weight, dy),
        [pltpu.VMEM((frames, size + 2 * COLS, chans), BF)],
        flops=9 * work,
        moved=5 << 20,
    )
    pair = [(0, 1), (1, 0)]
    got = lax.ppermute(send, "core", pair)
    half = call(add_kernel, shape((rows, 128)), (keep, got), moved=3 << 20)
    line, rank = lax.axis_size("x"), lax.axis_size("y")
    column, plane = lax.axis_size(COLUMN), lax.axis_size(PLANE)
    share, piece = rows // line, rows // plane // column
    first = exchange(half.reshape(line, share, 128), "x")
    part = call(sum_kernel, shape((share, 128)), (first,), moved=1 << 18)
    second = exchange(part.reshape(rank, share // rank, 128), "y")
    part = call(
        sum_kernel, shape((share // rank, 128), F32), (second,), moved=1 << 18, after=(behind,)
    )
    third = exchange(part.reshape(column, piece, 128), COLUMN)
    spread = call(
        functools.partial(last_kernel, scale),
        shape((column, piece, 128)),
        (third,),
        moved=1 << 18,
        after=(grad_top, grad_bottom),
    )
    fourth = exchange(spread, COLUMN).reshape(column * piece, 128)
    wider = call(spread_kernel, shape((plane, column * piece, 128)), (fourth,), moved=1 << 18)
    own = exchange(wider, PLANE).reshape(rows, 128)
    block_out = call(
        mix_kernel,
        shape((flat, chans)),
        (act, behind, temporal_weight, x.reshape(flat, chans)),
        [pltpu.VMEM((2 * flat, chans), BF)],
        flops=3 * work,
        moved=4 << 20,
    )
    own, block_out, input_grad = lax.optimization_barrier((own, block_out, input_grad))
    other = lax.ppermute(own, "core", pair)
    spatial, temporal = call(
        final_kernel,
        [shape((9, chans, chans), F32), shape((3, chans, chans), F32)],
        (core, own, other),
        moved=5 << 20,
        smem=(0,),
    )
    return (
        block_out.reshape(dims),
        input_grad.reshape(dims),
        spatial.reshape(3, 3, chans, chans),
        temporal,
    )


def solution(mesh):
    fine = Mesh(mesh.devices.reshape(2, 4, 4, 4, 2), ("clip", "y", "zl", "x", "core"))
    blocks = P("clip", TM, SPACE, None, None)

    def run(frames_in, cotangent, spatial_weight, temporal_weight):
        clips, frames, height, width, _ = frames_in.shape
        scale = (clips * frames * height * width) ** -0.5
        return jax.shard_map(
            functools.partial(local, scale),
            mesh=fine,
            in_specs=(blocks, blocks, P(), P()),
            out_specs=(blocks, blocks, P(), P()),
            check_vma=False,
        )(frames_in, cotangent, spatial_weight, temporal_weight)

    return run
```

```python
import functools

import jax
import jax.numpy as jnp
from jax import lax
from jax.experimental import pallas as pl
from jax.experimental.pallas import tpu as pltpu
from jax.sharding import Mesh, PartitionSpec as P

BF = jnp.bfloat16
F32 = jnp.float32
TM = ("y", "zl")
SPACE = ("x", "core")
PLANE = ("x", "y")
COLUMN = ("clip", "zl")
COLS = 128
NT = (((1,), (1,)), ((), ()))


def call(kernel, outs, ins, scratch=(), flops=0, moved=0, limit=20, smem=(), after=(), hbm=(), out_hbm=False, alias=None):
    vmem = pl.BlockSpec(memory_space=pltpu.VMEM)
    specs = [pl.BlockSpec(memory_space=pltpu.SMEM) if i in smem else vmem for i in range(len(ins))]
    specs = [pl.BlockSpec(memory_space=pltpu.HBM) if i in hbm else p for i, p in enumerate(specs)]
    specs += [pl.BlockSpec(memory_space=pltpu.HBM)] * len(after)
    placed = pl.BlockSpec(memory_space=pltpu.HBM) if out_hbm else vmem
    count = len(ins)

    def body(*refs):
        kernel(*refs[:count], *refs[count + len(after) :])

    return pl.pallas_call(
        body,
        out_shape=outs,
        in_specs=specs,
        out_specs=jax.tree.map(lambda _: placed, outs),
        input_output_aliases=alias or {},
        scratch_shapes=list(scratch),
        cost_estimate=pl.CostEstimate(flops=flops, bytes_accessed=moved, transcendentals=0),
        compiler_params=pltpu.CompilerParams(vmem_limit_bytes=limit << 20),
    )(*ins, *after)


def shape(dims, kind=BF):
    return jax.ShapeDtypeStruct(dims, kind)


def shifted(value, column, step):
    edge = 0 if step == 1 else COLS - 1
    rolled = pltpu.roll(value, step % value.shape[0], 0)
    return jnp.where(column == edge, 0.0, rolled)


def columns_of(rows, width):
    return lax.broadcasted_iota(jnp.int32, (rows, width), 0) % COLS


def window(ref, frame, start, rows, offsets):
    parts = [ref[frame, pl.ds(start + off * COLS, rows), :] for off in offsets]
    return jnp.concatenate(parts, axis=1)


CHUNK = 512


def fill(padded, block, top, bottom, frame):
    size = block.shape[1]
    padded[frame, 0:COLS, :] = top[frame]
    padded[frame, COLS : COLS + size, :] = block[frame]
    padded[frame, COLS + size :, :] = bottom[frame]


def forward_kernel(x, top, bottom, weight, act, slope, x_t, act_t, padded):
    frames, size, chans = x.shape
    for f in range(frames):
        fill(padded, x, top, bottom, f)

    @pl.loop(0, frames * (size // CHUNK))
    def _(step):
        f = step // (size // CHUNK)
        start = pl.multiple_of((step % (size // CHUNK)) * CHUNK, CHUNK)
        rows = window(padded, f, start, CHUNK, (0, 1, 2))
        column = columns_of(CHUNK, chans)
        z = [
            jnp.dot(rows, weight[:, j].reshape(3 * chans, chans), preferred_element_type=F32)
            for j in range(3)
        ]
        pre = shifted(z[0], column, 1) + z[1] + shifted(z[2], column, -1)
        sigma = 1.0 / (1.0 + jnp.exp(-pre))
        active = (pre * sigma).astype(BF)
        act[f, pl.ds(start, CHUNK), :] = active
        slope[f, pl.ds(start, CHUNK), :] = sigma * (1.0 + pre * (1.0 - sigma))
        act_t[f, :, pl.ds(start, CHUNK)] = active.T

    for f in range(frames):
        x_t[f] = padded[f].T


def early_kernel(dy, weight, act_t, partial, terms):
    frames, size, chans = dy.shape

    @pl.loop(0, size // CHUNK)
    def _(step):
        at = pl.ds(pl.multiple_of(step * CHUNK, CHUNK), CHUNK)
        second = dy[1, at, :]
        both = jnp.concatenate([dy[0, at, :], second], axis=1)
        taps = jnp.concatenate([weight[0], weight[1]], axis=1)
        partial[0, at, :] = lax.dot_general(both, taps, NT, preferred_element_type=F32)
        partial[1, at, :] = lax.dot_general(second, weight[0], NT, preferred_element_type=F32)

    left = jnp.concatenate([act_t[0], act_t[1]], axis=1)
    right = dy[...].reshape(frames * size, chans)
    terms[0] = jnp.dot(left, right, preferred_element_type=F32)
    terms[1] = jnp.dot(act_t[0], dy[1], preferred_element_type=F32)


def finish(f, start, agrad, slope, pgrad, wide):
    at = pl.ds(start, CHUNK)
    grad = (agrad.astype(BF).astype(F32) * slope[f, at, :]).astype(BF)
    pgrad[at, :] = grad
    full = grad.astype(F32)
    column = columns_of(CHUNK, full.shape[1])
    wide[0, at, :] = shifted(full, column, -1).astype(BF)
    wide[1, at, :] = grad
    wide[2, at, :] = shifted(full, column, 1).astype(BF)


def windows_of(x_t, f, size):
    return jnp.concatenate([x_t[f, :, i * COLS : i * COLS + size] for i in range(3)], axis=0)


def first_kernel(
    ahead, weight, slope, x_t, act_t, partial, early, pgrad, rest, spatial, temporal, last, first, wide
):
    size = ahead.shape[0]

    @pl.loop(0, size // CHUNK)
    def _(step):
        start = pl.multiple_of(step * CHUNK, CHUNK)
        at = pl.ds(start, CHUNK)
        block = ahead[at, :]
        more = lax.dot_general(block, weight[2], NT, preferred_element_type=F32)
        finish(0, start, partial[0, at, :] + more, slope, pgrad, wide)
        more = lax.dot_general(block, weight[1], NT, preferred_element_type=F32)
        rest[at, :] = partial[1, at, :] + more

    last[...] = pgrad[size - COLS :, :]
    first[...] = pgrad[:COLS, :]
    left = windows_of(x_t, 0, size)
    for j in range(3):
        spatial[j] = jnp.dot(left, wide[j], preferred_element_type=F32)
    temporal[0] = early[1] + jnp.dot(act_t[1], ahead[...], preferred_element_type=F32)
    temporal[1] = jnp.dot(act_t[0], ahead[...], preferred_element_type=F32)


def second_kernel(
    core,
    ahead,
    weight,
    slope,
    x_t,
    act_t,
    rest,
    early,
    spatial,
    temporal,
    last_0,
    first_0,
    pgrad,
    keep,
    send,
    last,
    first,
    wide,
    terms,
):
    size, chans = ahead.shape

    @pl.loop(0, size // CHUNK)
    def _(step):
        start = pl.multiple_of(step * CHUNK, CHUNK)
        at = pl.ds(start, CHUNK)
        more = lax.dot_general(ahead[at, :], weight[2], NT, preferred_element_type=F32)
        finish(1, start, rest[at, :] + more, slope, pgrad, wide)

    last[0] = last_0[...]
    first[0] = first_0[...]
    last[1] = pgrad[size - COLS :, :]
    first[1] = pgrad[:COLS, :]

    def put(tap, value):
        for h in range(2):
            at = (tap * 2 + h) * chans
            terms[at : at + chans, :] = value[:, h * 128 : (h + 1) * 128].astype(BF)

    left = windows_of(x_t, 1, size)
    for j in range(3):
        out = spatial[j] + jnp.dot(left, wide[j], preferred_element_type=F32)
        for i in range(3):
            put(3 * i + j, out[i * chans : (i + 1) * chans])
    put(9, early[0])
    put(10, temporal[0])
    put(11, temporal[1] + jnp.dot(act_t[1], ahead[...], preferred_element_type=F32))
    half = terms.shape[0] // 2
    for c in range(2):

        @pl.when(core[0] == c)
        def _():
            keep[...] = terms[c * half : (c + 1) * half, :]
            send[...] = terms[(1 - c) * half : (2 - c) * half, :]


def add_kernel(a, b, out):
    out[...] = (a[...].astype(F32) + b[...].astype(F32)).astype(BF)


def sum_kernel(parts, out):
    total = parts[0].astype(F32)
    for i in range(1, parts.shape[0]):
        total = total + parts[i].astype(F32)
    out[...] = total.astype(out.dtype)


def last_kernel(scale, parts, out):
    total = parts[0].astype(F32)
    for i in range(1, parts.shape[0]):
        total = total + parts[i].astype(F32)
    total = (total * scale).astype(out.dtype)
    for i in range(out.shape[0]):
        out[i] = total


def spread_kernel(value, out):
    for i in range(out.shape[0]):
        out[i] = value[...]


def write_half(first, source, spatial, temporal, wide, sems):
    copies = []
    for n in range(6):
        t = n if first else n + 6
        for h in range(2):
            at = (n * 2 + h) * 256
            wide[n, :, h * 128 : (h + 1) * 128] = source[at : at + 256, :].astype(F32)
        target = spatial.at[t] if t < 9 else temporal.at[t - 9]
        copy = pltpu.make_async_copy(wide.at[n], target, sems.at[n])
        copy.start()
        copies.append(copy)
    for copy in copies:
        copy.wait()


def own_kernel(core, own, spatial, temporal, wide, sems):
    for c in range(2):

        @pl.when(core[0] == c)
        def _():
            write_half(c == 0, own, spatial, temporal, wide, sems)


def other_kernel(core, other, spatial_in, temporal_in, spatial, temporal, wide, sems):
    for c in range(2):

        @pl.when(core[0] == c)
        def _():
            write_half(c == 1, other, spatial, temporal, wide, sems)


def back_kernel(grad_0, grad_1, top, bottom, weight, dy, out, padded):
    frames, size, chans = dy.shape
    for f, grad in enumerate((grad_0, grad_1)):
        padded[f, 0:COLS, :] = top[f]
        padded[f, COLS : COLS + size, :] = grad[...]
        padded[f, COLS + size :, :] = bottom[f]

    @pl.loop(0, frames * (size // CHUNK))
    def _(step):
        f = step // (size // CHUNK)
        start = pl.multiple_of((step % (size // CHUNK)) * CHUNK, CHUNK)
        rows = window(padded, f, start, CHUNK, (2, 1, 0))
        column = columns_of(CHUNK, chans)
        z = [
            lax.dot_general(
                rows,
                jnp.concatenate([weight[i, j] for i in range(3)], axis=1),
                NT,
                preferred_element_type=F32,
            )
            for j in range(3)
        ]
        back = shifted(z[0], column, -1) + z[1] + shifted(z[2], column, 1)
        out[f, pl.ds(start, CHUNK), :] = (dy[f, pl.ds(start, CHUNK), :].astype(F32) + back).astype(BF)


def mix_kernel(act, behind, weight, x, out, ext):
    frames, size, chans = act.shape
    for f in range(frames):
        ext[f * size : (f + 1) * size, :] = behind[f]
        ext[(frames + f) * size : (frames + f + 1) * size, :] = act[f]

    @pl.loop(0, frames * (size // CHUNK))
    def _(step):
        start = pl.multiple_of(step * CHUNK, CHUNK)
        rows = jnp.concatenate(
            [ext[pl.ds(start + (2 - k) * size, CHUNK), :] for k in range(3)], axis=1
        )
        mixed = jnp.dot(rows, weight[...].reshape(3 * chans, chans), preferred_element_type=F32)
        own = x[pl.ds(start, CHUNK), :].astype(F32)
        out[pl.ds(start, CHUNK), :] = (own + mixed.astype(BF).astype(F32)).astype(BF)


def steps(axes, by):
    count = lax.axis_size(axes)
    return [(i, i + by) for i in range(count) if 0 <= i + by < count]


def exchange(value, axes):
    return lax.all_to_all(value, axes, split_axis=0, concat_axis=0, tiled=True)


def swap_rims(last, first):
    return lax.ppermute(last, SPACE, steps(SPACE, 1)), lax.ppermute(first, SPACE, steps(SPACE, -1))


def local(scale, frames_in, cotangent, spatial_weight, temporal_weight):
    dims = frames_in.shape
    frames, chans = dims[1], dims[4]
    size = dims[2] * dims[3]
    x = frames_in.reshape(frames, size, chans)
    dy = cotangent.reshape(frames, size, chans)
    work = 2 * frames * size * chans * chans
    core = lax.axis_index("core").astype(jnp.int32).reshape(1)
    ahead = [lax.ppermute(dy[f], TM, steps(TM, -1)) for f in range(frames)]
    top, bottom = swap_rims(x[:, size - COLS :, :], x[:, :COLS, :])
    act, slope, x_t, act_t = call(
        forward_kernel,
        [
            shape((frames, size, chans)),
            shape((frames, size, chans), F32),
            shape((frames, chans, size + 2 * COLS)),
            shape((frames, chans, size)),
        ],
        (x, top, bottom, spatial_weight),
        [pltpu.VMEM((frames, size + 2 * COLS, chans), BF)],
        flops=9 * work,
        moved=9 << 20,
    )
    partial, early = call(
        early_kernel,
        [shape((frames, size, chans), F32), shape((2, chans, chans), F32)],
        (dy, temporal_weight, act_t),
        flops=6 * work,
        moved=6 << 20,
    )
    behind = lax.ppermute(act, TM, steps(TM, 1))
    flat = frames * size
    rows = 12 * chans
    wide = pltpu.VMEM((3, size, chans), BF)
    edge = shape((COLS, chans))
    pgrad_0, rest, spatial, temporal, last_0, first_0 = call(
        first_kernel,
        [
            shape((size, chans)),
            shape((size, chans), F32),
            shape((3, 3 * chans, chans), F32),
            shape((2, chans, chans), F32),
            edge,
            edge,
        ],
        (ahead[0], temporal_weight, slope, x_t, act_t, partial, early),
        [wide],
        flops=work // 16,
        moved=1 << 18,
    )
    edges = shape((frames, COLS, chans))
    pgrad_1, keep, send, last, first = call(
        second_kernel,
        [shape((size, chans)), shape((rows, 128)), shape((rows, 128)), edges, edges],
        (
            core,
            ahead[1],
            temporal_weight,
            slope,
            x_t,
            act_t,
            rest,
            early,
            spatial,
            temporal,
            last_0,
            first_0,
        ),
        [wide, pltpu.VMEM((2 * rows, 128), BF)],
        flops=work // 16,
        moved=1 << 18,
        smem=(0,),
    )
    grad_top, grad_bottom = swap_rims(last, first)
    input_grad = call(
        back_kernel,
        shape((frames, size, chans)),
        (pgrad_0, pgrad_1, grad_top, grad_bottom, spatial_weight, dy),
        [pltpu.VMEM((frames, size + 2 * COLS, chans), BF)],
        flops=9 * work,
        moved=5 << 20,
    )
    pair = [(0, 1), (1, 0)]
    got = lax.ppermute(send, "core", pair)
    half = call(add_kernel, shape((rows, 128)), (keep, got), moved=3 << 20)
    line, rank = lax.axis_size("x"), lax.axis_size("y")
    column, plane = lax.axis_size(COLUMN), lax.axis_size(PLANE)
    share, piece = rows // line, rows // plane // column
    first = exchange(half.reshape(line, share, 128), "x")
    part = call(sum_kernel, shape((share, 128)), (first,), moved=1 << 18)
    second = exchange(part.reshape(rank, share // rank, 128), "y")
    part = call(
        sum_kernel, shape((share // rank, 128), F32), (second,), moved=1 << 18, after=(behind, grad_top, grad_bottom)
    )
    third = exchange(part.reshape(column, piece, 128), COLUMN)
    block_out = call(
        mix_kernel,
        shape((flat, chans)),
        (act, behind, temporal_weight, x.reshape(flat, chans)),
        [pltpu.VMEM((2 * flat, chans), BF)],
        flops=3 * work,
        moved=4 << 20,
    )
    spread = call(
        functools.partial(last_kernel, scale),
        shape((column, piece, 128)),
        (third,),
        moved=1 << 18,
    )
    fourth = exchange(spread, COLUMN).reshape(column * piece, 128)
    wider = call(spread_kernel, shape((plane, column * piece, 128)), (fourth,), moved=1 << 18)
    own = exchange(wider, PLANE).reshape(rows, 128)
    own, block_out, input_grad = lax.optimization_barrier((own, block_out, input_grad))
    other = lax.ppermute(own, "core", pair)
    grads = [shape((9, chans, chans), F32), shape((3, chans, chans), F32)]
    room = [pltpu.VMEM((6, chans, chans), F32), pltpu.SemaphoreType.DMA((6,))]
    spatial, temporal = call(
        own_kernel, grads, (core, own), room, moved=3 << 20, smem=(0,), out_hbm=True
    )
    spatial, temporal = call(
        other_kernel,
        grads,
        (core, other, spatial, temporal),
        room,
        moved=3 << 20,
        smem=(0,),
        hbm=(2, 3),
        out_hbm=True,
        alias={2: 0, 3: 1},
    )
    return (
        block_out.reshape(dims),
        input_grad.reshape(dims),
        spatial.reshape(3, 3, chans, chans),
        temporal,
    )


def solution(mesh):
    fine = Mesh(mesh.devices.reshape(2, 4, 4, 4, 2), ("clip", "y", "zl", "x", "core"))
    blocks = P("clip", TM, SPACE, None, None)

    def run(frames_in, cotangent, spatial_weight, temporal_weight):
        clips, frames, height, width, _ = frames_in.shape
        scale = (clips * frames * height * width) ** -0.5
        return jax.shard_map(
            functools.partial(local, scale),
            mesh=fine,
            in_specs=(blocks, blocks, P(), P()),
            out_specs=(blocks, blocks, P(), P()),
            check_vma=False,
        )(frames_in, cotangent, spatial_weight, temporal_weight)

    return run
```

```python
import functools

import jax
import jax.numpy as jnp
from jax import lax
from jax.experimental import pallas as pl
from jax.experimental.pallas import tpu as pltpu
from jax.sharding import Mesh, PartitionSpec as P

BF = jnp.bfloat16
F32 = jnp.float32
TM = ("y", "zl")
SPACE = ("x", "core")
PLANE = ("x", "y")
COLUMN = ("clip", "zl")
COLS = 128
NT = (((1,), (1,)), ((), ()))


def call(kernel, outs, ins, scratch=(), flops=0, moved=0, limit=20, smem=(), after=(), hbm=(), out_hbm=False, alias=None):
    vmem = pl.BlockSpec(memory_space=pltpu.VMEM)
    specs = [pl.BlockSpec(memory_space=pltpu.SMEM) if i in smem else vmem for i in range(len(ins))]
    specs = [pl.BlockSpec(memory_space=pl.ANY) if i in hbm else p for i, p in enumerate(specs)]
    specs += [pl.BlockSpec(memory_space=pltpu.HBM)] * len(after)
    many = isinstance(outs, list)
    placed = [
        pl.BlockSpec(memory_space=pltpu.HBM) if out_hbm is True or i in (out_hbm or ()) else vmem
        for i in range(len(outs) if many else 1)
    ]
    count = len(ins)

    def body(*refs):
        kernel(*refs[:count], *refs[count + len(after) :])

    return pl.pallas_call(
        body,
        out_shape=outs,
        in_specs=specs,
        out_specs=placed if many else placed[0],
        input_output_aliases=alias or {},
        scratch_shapes=list(scratch),
        cost_estimate=pl.CostEstimate(flops=flops, bytes_accessed=moved, transcendentals=0),
        compiler_params=pltpu.CompilerParams(vmem_limit_bytes=limit << 20),
    )(*ins, *after)


def shape(dims, kind=BF):
    return jax.ShapeDtypeStruct(dims, kind)


def shifted(value, column, step):
    edge = 0 if step == 1 else COLS - 1
    rolled = pltpu.roll(value, step % value.shape[0], 0)
    return jnp.where(column == edge, 0.0, rolled)


def columns_of(rows, width):
    return lax.broadcasted_iota(jnp.int32, (rows, width), 0) % COLS


def window(ref, frame, start, rows, offsets):
    parts = [ref[frame, pl.ds(start + off * COLS, rows), :] for off in offsets]
    return jnp.concatenate(parts, axis=1)


CHUNK = 512


def fill(padded, block, top, bottom, frame):
    size = block.shape[1]
    padded[frame, 0:COLS, :] = top[frame]
    padded[frame, COLS : COLS + size, :] = block[frame]
    padded[frame, COLS + size :, :] = bottom[frame]


def forward_kernel(x, top, bottom, weight, act, slope, x_t, act_t, padded):
    frames, size, chans = x.shape
    for f in range(frames):
        fill(padded, x, top, bottom, f)

    @pl.loop(0, frames * (size // CHUNK))
    def _(step):
        f = step // (size // CHUNK)
        start = pl.multiple_of((step % (size // CHUNK)) * CHUNK, CHUNK)
        rows = window(padded, f, start, CHUNK, (0, 1, 2))
        column = columns_of(CHUNK, chans)
        z = [
            jnp.dot(rows, weight[:, j].reshape(3 * chans, chans), preferred_element_type=F32)
            for j in range(3)
        ]
        pre = shifted(z[0], column, 1) + z[1] + shifted(z[2], column, -1)
        sigma = 1.0 / (1.0 + jnp.exp(-pre))
        active = (pre * sigma).astype(BF)
        act[f, pl.ds(start, CHUNK), :] = active
        slope[f, pl.ds(start, CHUNK), :] = sigma * (1.0 + pre * (1.0 - sigma))
        act_t[f, :, pl.ds(start, CHUNK)] = active.T

    for f in range(frames):
        x_t[f] = padded[f].T


def early_kernel(dy, weight, act_t, partial, terms):
    frames, size, chans = dy.shape

    @pl.loop(0, size // CHUNK)
    def _(step):
        at = pl.ds(pl.multiple_of(step * CHUNK, CHUNK), CHUNK)
        second = dy[1, at, :]
        both = jnp.concatenate([dy[0, at, :], second], axis=1)
        taps = jnp.concatenate([weight[0], weight[1]], axis=1)
        partial[0, at, :] = lax.dot_general(both, taps, NT, preferred_element_type=F32)
        partial[1, at, :] = lax.dot_general(second, weight[0], NT, preferred_element_type=F32)

    left = jnp.concatenate([act_t[0], act_t[1]], axis=1)
    right = dy[...].reshape(frames * size, chans)
    terms[0] = jnp.dot(left, right, preferred_element_type=F32)
    terms[1] = jnp.dot(act_t[0], dy[1], preferred_element_type=F32)


def finish(f, start, agrad, slope, wide):
    at = pl.ds(start, CHUNK)
    grad = (agrad.astype(BF).astype(F32) * slope[f, at, :]).astype(BF)
    full = grad.astype(F32)
    column = columns_of(CHUNK, full.shape[1])
    wide[0, at, :] = shifted(full, column, -1).astype(BF)
    wide[1, at, :] = grad
    wide[2, at, :] = shifted(full, column, 1).astype(BF)


def windows_of(x_t, f, size):
    return jnp.concatenate([x_t[f, :, i * COLS : i * COLS + size] for i in range(3)], axis=0)


def first_kernel(
    ahead, weight, slope, x_t, act_t, partial, early, pgrad, rest, spatial, temporal, last, first, wide, sem
):
    size = ahead.shape[0]

    @pl.loop(0, size // CHUNK)
    def _(step):
        start = pl.multiple_of(step * CHUNK, CHUNK)
        at = pl.ds(start, CHUNK)
        block = ahead[at, :]
        more = lax.dot_general(block, weight[2], NT, preferred_element_type=F32)
        finish(0, start, partial[0, at, :] + more, slope, wide)
        more = lax.dot_general(block, weight[1], NT, preferred_element_type=F32)
        rest[at, :] = partial[1, at, :] + more

    store = pltpu.make_async_copy(wide.at[1], pgrad, sem)
    store.start()
    last[...] = wide[1, size - COLS :, :]
    first[...] = wide[1, :COLS, :]
    left = windows_of(x_t, 0, size)
    for j in range(3):
        spatial[j] = jnp.dot(left, wide[j], preferred_element_type=F32)
    temporal[0] = early[1] + jnp.dot(act_t[1], ahead[...], preferred_element_type=F32)
    temporal[1] = jnp.dot(act_t[0], ahead[...], preferred_element_type=F32)
    store.wait()


def second_kernel(
    core,
    ahead,
    weight,
    slope,
    x_t,
    act_t,
    rest,
    early,
    spatial,
    temporal,
    last_0,
    first_0,
    pgrad,
    keep,
    send,
    last,
    first,
    wide,
    terms,
    sem,
):
    size, chans = ahead.shape

    @pl.loop(0, size // CHUNK)
    def _(step):
        start = pl.multiple_of(step * CHUNK, CHUNK)
        at = pl.ds(start, CHUNK)
        more = lax.dot_general(ahead[at, :], weight[2], NT, preferred_element_type=F32)
        finish(1, start, rest[at, :] + more, slope, wide)

    store = pltpu.make_async_copy(wide.at[1], pgrad, sem)
    store.start()
    last[0] = last_0[...]
    first[0] = first_0[...]
    last[1] = wide[1, size - COLS :, :]
    first[1] = wide[1, :COLS, :]

    def put(tap, value):
        for h in range(2):
            at = (tap * 2 + h) * chans
            terms[at : at + chans, :] = value[:, h * 128 : (h + 1) * 128].astype(BF)

    left = windows_of(x_t, 1, size)
    for j in range(3):
        out = spatial[j] + jnp.dot(left, wide[j], preferred_element_type=F32)
        for i in range(3):
            put(3 * i + j, out[i * chans : (i + 1) * chans])
    put(9, early[0])
    put(10, temporal[0])
    put(11, temporal[1] + jnp.dot(act_t[1], ahead[...], preferred_element_type=F32))
    half = terms.shape[0] // 2
    for c in range(2):

        @pl.when(core[0] == c)
        def _():
            keep[...] = terms[c * half : (c + 1) * half, :]
            send[...] = terms[(1 - c) * half : (2 - c) * half, :]

    store.wait()


def add_kernel(a, b, out):
    out[...] = (a[...].astype(F32) + b[...].astype(F32)).astype(BF)


def sum_kernel(parts, out):
    total = parts[0].astype(F32)
    for i in range(1, parts.shape[0]):
        total = total + parts[i].astype(F32)
    out[...] = total.astype(out.dtype)


def spread_sum_kernel(scale, parts, out):
    total = parts[0].astype(F32)
    for i in range(1, parts.shape[0]):
        total = total + parts[i].astype(F32)
    total = (total * scale).astype(out.dtype)
    for i in range(out.shape[0]):
        out[i] = total


def write_half(first, source, spatial, temporal, wide, sems):
    copies = []
    for n in range(6):
        t = n if first else n + 6
        for h in range(2):
            at = (n * 2 + h) * 256
            wide[n, :, h * 128 : (h + 1) * 128] = source[at : at + 256, :].astype(F32)
        target = spatial.at[t] if t < 9 else temporal.at[t - 9]
        copy = pltpu.make_async_copy(wide.at[n], target, sems.at[n])
        copy.start()
        copies.append(copy)
    for copy in copies:
        copy.wait()


def own_kernel(core, own, spatial, temporal, wide, sems):
    for c in range(2):

        @pl.when(core[0] == c)
        def _():
            write_half(c == 0, own, spatial, temporal, wide, sems)


def other_kernel(core, other, spatial_in, temporal_in, spatial, temporal, wide, sems):
    for c in range(2):

        @pl.when(core[0] == c)
        def _():
            write_half(c == 1, other, spatial, temporal, wide, sems)


def back_kernel(
    grad_0, grad_1, top, bottom, weight, dy, out, padded, taps, own, result, sems
):
    frames, size, chans = own.shape
    whole = pltpu.make_async_copy(weight, taps, sems.at[0])
    whole.start()
    loads = []
    for f, grad in enumerate((grad_0, grad_1)):
        base = 1 + 5 * f
        loads.append(
            [
                pltpu.make_async_copy(top.at[f], padded.at[f, pl.ds(0, COLS)], sems.at[base]),
                pltpu.make_async_copy(grad, padded.at[f, pl.ds(COLS, size)], sems.at[base + 1]),
                pltpu.make_async_copy(
                    bottom.at[f], padded.at[f, pl.ds(COLS + size, COLS)], sems.at[base + 2]
                ),
                pltpu.make_async_copy(dy.at[f], own.at[f], sems.at[base + 3]),
            ]
        )
        for load in loads[f]:
            load.start()
    whole.wait()
    stores = []
    for f in range(frames):
        for load in loads[f]:
            load.wait()

        @pl.loop(0, size // CHUNK)
        def _(step):
            start = pl.multiple_of(step * CHUNK, CHUNK)
            at = pl.ds(start, CHUNK)
            rows = window(padded, f, start, CHUNK, (2, 1, 0))
            column = columns_of(CHUNK, chans)
            z = [
                lax.dot_general(
                    rows,
                    jnp.concatenate([taps[i, j] for i in range(3)], axis=1),
                    NT,
                    preferred_element_type=F32,
                )
                for j in range(3)
            ]
            back = shifted(z[0], column, -1) + z[1] + shifted(z[2], column, 1)
            result[f, at, :] = (own[f, at, :].astype(F32) + back).astype(BF)

        store = pltpu.make_async_copy(result.at[f], out.at[f], sems.at[5 + 5 * f])
        store.start()
        stores.append(store)
    for store in stores:
        store.wait()


def mix_kernel(act, behind, weight, x, out, ext, own, result, sems):
    frames, size, chans = own.shape
    loads = []
    for f in range(frames):
        loads.append(pltpu.make_async_copy(behind.at[f], ext.at[f], sems.at[f]))
        loads.append(pltpu.make_async_copy(act.at[f], ext.at[frames + f], sems.at[frames + f]))
        loads.append(pltpu.make_async_copy(x.at[f], own.at[f], sems.at[2 * frames + f]))
    for load in loads:
        load.start()
    for load in loads:
        load.wait()
    stores = []
    for f in range(frames):

        @pl.loop(0, size // CHUNK)
        def _(step):
            at = pl.ds(pl.multiple_of(step * CHUNK, CHUNK), CHUNK)
            rows = jnp.concatenate([ext[f + 2 - k, at, :] for k in range(3)], axis=1)
            taps = weight[...].reshape(3 * chans, chans)
            mixed = jnp.dot(rows, taps, preferred_element_type=F32).astype(BF)
            result[f, at, :] = (own[f, at, :].astype(F32) + mixed.astype(F32)).astype(BF)

        store = pltpu.make_async_copy(result.at[f], out.at[f], sems.at[3 * frames + f])
        store.start()
        stores.append(store)
    for store in stores:
        store.wait()


def steps(axes, by):
    count = lax.axis_size(axes)
    return [(i, i + by) for i in range(count) if 0 <= i + by < count]


def exchange(value, axes):
    return lax.all_to_all(value, axes, split_axis=0, concat_axis=0, tiled=True)


def swap_rims(last, first):
    return lax.ppermute(last, SPACE, steps(SPACE, 1)), lax.ppermute(first, SPACE, steps(SPACE, -1))


def local(scale, frames_in, cotangent, spatial_weight, temporal_weight):
    dims = frames_in.shape
    frames, chans = dims[1], dims[4]
    size = dims[2] * dims[3]
    x = frames_in.reshape(frames, size, chans)
    dy = cotangent.reshape(frames, size, chans)
    work = 2 * frames * size * chans * chans
    core = lax.axis_index("core").astype(jnp.int32).reshape(1)
    dy_0, later = lax.optimization_barrier((dy[0], dy))
    ahead = [lax.ppermute(frame, TM, steps(TM, -1)) for frame in (dy_0, later[1])]
    top, bottom = swap_rims(x[:, size - COLS :, :], x[:, :COLS, :])
    act, slope, x_t, act_t = call(
        forward_kernel,
        [
            shape((frames, size, chans)),
            shape((frames, size, chans), F32),
            shape((frames, chans, size + 2 * COLS)),
            shape((frames, chans, size)),
        ],
        (x, top, bottom, spatial_weight),
        [pltpu.VMEM((frames, size + 2 * COLS, chans), BF)],
        flops=9 * work,
        moved=9 << 20,
    )
    partial, early = call(
        early_kernel,
        [shape((frames, size, chans), F32), shape((2, chans, chans), F32)],
        (dy, temporal_weight, act_t),
        flops=6 * work,
        moved=6 << 20,
    )
    behind = lax.ppermute(act, TM, steps(TM, 1))
    flat = frames * size
    rows = 12 * chans
    wide = pltpu.VMEM((3, size, chans), BF)
    edge = shape((COLS, chans))
    pgrad_0, rest, spatial, temporal, last_0, first_0 = call(
        first_kernel,
        [
            shape((size, chans)),
            shape((size, chans), F32),
            shape((3, 3 * chans, chans), F32),
            shape((2, chans, chans), F32),
            edge,
            edge,
        ],
        (ahead[0], temporal_weight, slope, x_t, act_t, partial, early),
        [wide, pltpu.SemaphoreType.DMA],
        flops=work // 16,
        moved=1 << 18,
        out_hbm=(0,),
    )
    edges = shape((frames, COLS, chans))
    pgrad_1, keep, send, last, first = call(
        second_kernel,
        [shape((size, chans)), shape((rows, 128)), shape((rows, 128)), edges, edges],
        (
            core,
            ahead[1],
            temporal_weight,
            slope,
            x_t,
            act_t,
            rest,
            early,
            spatial,
            temporal,
            last_0,
            first_0,
        ),
        [wide, pltpu.VMEM((2 * rows, 128), BF), pltpu.SemaphoreType.DMA],
        flops=work // 16,
        moved=1 << 18,
        out_hbm=(0,),
        smem=(0,),
    )
    grad_top, grad_bottom = swap_rims(last, first)
    pair = [(0, 1), (1, 0)]
    got = lax.ppermute(send, "core", pair)
    half = call(add_kernel, shape((rows, 128)), (keep, got), moved=3 << 20)
    block = pltpu.VMEM((frames, size, chans), BF)
    line, rank = lax.axis_size("x"), lax.axis_size("y")
    column, plane = lax.axis_size(COLUMN), lax.axis_size(PLANE)
    share = rows // line
    first = exchange(half.reshape(line, share, 128), "x")
    part = call(sum_kernel, shape((share, 128)), (first,), moved=1 << 18)
    second = exchange(part.reshape(rank, share // rank, 128), "y")
    spread = call(
        functools.partial(spread_sum_kernel, 1.0),
        shape((column, share // rank, 128)),
        (second,),
        moved=1 << 18,
        after=(behind,),
    )
    third = exchange(spread, COLUMN)
    block_out = call(
        mix_kernel,
        shape((frames, size, chans)),
        (act, behind, temporal_weight, x),
        [
            pltpu.VMEM((2 * frames, size, chans), BF),
            block,
            block,
            pltpu.SemaphoreType.DMA((4 * frames,)),
        ],
        flops=3 * work,
        moved=4 << 20,
        hbm=(0, 1, 3),
        out_hbm=True,
        limit=58,
    )
    third, grad_top, grad_bottom = lax.optimization_barrier((third, grad_top, grad_bottom))
    input_grad = call(
        back_kernel,
        shape((frames, size, chans)),
        (pgrad_0, pgrad_1, grad_top, grad_bottom, spatial_weight, dy),
        [
            pltpu.VMEM((frames, size + 2 * COLS, chans), BF),
            pltpu.VMEM((3, 3, chans, chans), BF),
            block,
            block,
            pltpu.SemaphoreType.DMA((11,)),
        ],
        flops=9 * work,
        moved=5 << 20,
        hbm=range(6),
        out_hbm=True,
        limit=58,
    )
    wider = call(
        functools.partial(spread_sum_kernel, scale),
        shape((plane, share // rank, 128)),
        (third,),
        moved=1 << 18,
    )
    own = exchange(wider, PLANE).reshape(rows, 128)
    own, block_out, input_grad = lax.optimization_barrier((own, block_out, input_grad))
    other = lax.ppermute(own, "core", pair)
    grads = [shape((9, chans, chans), F32), shape((3, chans, chans), F32)]
    room = [pltpu.VMEM((6, chans, chans), F32), pltpu.SemaphoreType.DMA((6,))]
    spatial, temporal = call(
        own_kernel, grads, (core, own), room, moved=3 << 20, smem=(0,), out_hbm=True
    )
    spatial, temporal = call(
        other_kernel,
        grads,
        (core, other, spatial, temporal),
        room,
        moved=3 << 20,
        smem=(0,),
        hbm=(2, 3),
        out_hbm=True,
        alias={2: 0, 3: 1},
    )
    return (
        block_out.reshape(dims),
        input_grad.reshape(dims),
        spatial.reshape(3, 3, chans, chans),
        temporal,
    )


def solution(mesh):
    fine = Mesh(mesh.devices.reshape(2, 4, 4, 4, 2), ("clip", "y", "zl", "x", "core"))
    blocks = P("clip", TM, SPACE, None, None)

    def run(frames_in, cotangent, spatial_weight, temporal_weight):
        clips, frames, height, width, _ = frames_in.shape
        scale = (clips * frames * height * width) ** -0.5
        return jax.shard_map(
            functools.partial(local, scale),
            mesh=fine,
            in_specs=(blocks, blocks, P(), P()),
            out_specs=(blocks, blocks, P(), P()),
            check_vma=False,
        )(frames_in, cotangent, spatial_weight, temporal_weight)

    return run
```

```python
import functools

import jax
import jax.numpy as jnp
from jax import lax
from jax.experimental import pallas as pl
from jax.experimental.pallas import tpu as pltpu
from jax.sharding import Mesh, PartitionSpec as P

BF = jnp.bfloat16
F32 = jnp.float32
TM = ("y", "zl")
SPACE = ("x", "core")
PLANE = ("x", "y")
COLUMN = ("clip", "zl")
COLS = 128
NT = (((1,), (1,)), ((), ()))


def call(kernel, outs, ins, scratch=(), flops=0, moved=0, limit=20, smem=(), after=(), hbm=(), out_hbm=False, alias=None):
    vmem = pl.BlockSpec(memory_space=pltpu.VMEM)
    specs = [pl.BlockSpec(memory_space=pltpu.SMEM) if i in smem else vmem for i in range(len(ins))]
    specs = [pl.BlockSpec(memory_space=pl.ANY) if i in hbm else p for i, p in enumerate(specs)]
    specs += [pl.BlockSpec(memory_space=pltpu.HBM)] * len(after)
    many = isinstance(outs, list)
    placed = [
        pl.BlockSpec(memory_space=pltpu.HBM) if out_hbm is True or i in (out_hbm or ()) else vmem
        for i in range(len(outs) if many else 1)
    ]
    count = len(ins)

    def body(*refs):
        kernel(*refs[:count], *refs[count + len(after) :])

    return pl.pallas_call(
        body,
        out_shape=outs,
        in_specs=specs,
        out_specs=placed if many else placed[0],
        input_output_aliases=alias or {},
        scratch_shapes=list(scratch),
        cost_estimate=pl.CostEstimate(flops=flops, bytes_accessed=moved, transcendentals=0),
        compiler_params=pltpu.CompilerParams(vmem_limit_bytes=limit << 20),
    )(*ins, *after)


def shape(dims, kind=BF):
    return jax.ShapeDtypeStruct(dims, kind)


def shifted(value, column, step):
    edge = 0 if step == 1 else COLS - 1
    rolled = pltpu.roll(value, step % value.shape[0], 0)
    return jnp.where(column == edge, 0.0, rolled)


def columns_of(rows, width):
    return lax.broadcasted_iota(jnp.int32, (rows, width), 0) % COLS


def window(ref, frame, start, rows, offsets):
    parts = [ref[frame, pl.ds(start + off * COLS, rows), :] for off in offsets]
    return jnp.concatenate(parts, axis=1)


CHUNK = 512


def fill(padded, block, top, bottom, frame):
    size = block.shape[1]
    padded[frame, 0:COLS, :] = top[frame]
    padded[frame, COLS : COLS + size, :] = block[frame]
    padded[frame, COLS + size :, :] = bottom[frame]


def forward_kernel(x, top, bottom, weight, act, slope, x_t, act_t, padded):
    frames, size, chans = x.shape
    for f in range(frames):
        fill(padded, x, top, bottom, f)

    @pl.loop(0, frames * (size // CHUNK))
    def _(step):
        f = step // (size // CHUNK)
        start = pl.multiple_of((step % (size // CHUNK)) * CHUNK, CHUNK)
        rows = window(padded, f, start, CHUNK, (0, 1, 2))
        column = columns_of(CHUNK, chans)
        z = [
            jnp.dot(rows, weight[:, j].reshape(3 * chans, chans), preferred_element_type=F32)
            for j in range(3)
        ]
        pre = shifted(z[0], column, 1) + z[1] + shifted(z[2], column, -1)
        sigma = 1.0 / (1.0 + jnp.exp(-pre))
        active = (pre * sigma).astype(BF)
        act[f, pl.ds(start, CHUNK), :] = active
        slope[f, pl.ds(start, CHUNK), :] = sigma * (1.0 + pre * (1.0 - sigma))
        act_t[f, :, pl.ds(start, CHUNK)] = active.T

    for f in range(frames):
        x_t[f] = padded[f].T


def early_kernel(dy, weight, act_t, partial, terms):
    frames, size, chans = dy.shape

    @pl.loop(0, size // CHUNK)
    def _(step):
        at = pl.ds(pl.multiple_of(step * CHUNK, CHUNK), CHUNK)
        second = dy[1, at, :]
        both = jnp.concatenate([dy[0, at, :], second], axis=1)
        taps = jnp.concatenate([weight[0], weight[1]], axis=1)
        partial[0, at, :] = lax.dot_general(both, taps, NT, preferred_element_type=F32)
        partial[1, at, :] = lax.dot_general(second, weight[0], NT, preferred_element_type=F32)

    left = jnp.concatenate([act_t[0], act_t[1]], axis=1)
    right = dy[...].reshape(frames * size, chans)
    terms[0] = jnp.dot(left, right, preferred_element_type=F32)
    terms[1] = jnp.dot(act_t[0], dy[1], preferred_element_type=F32)


def finish(f, start, agrad, slope, wide):
    at = pl.ds(start, CHUNK)
    grad = (agrad.astype(BF).astype(F32) * slope[f, at, :]).astype(BF)
    full = grad.astype(F32)
    column = columns_of(CHUNK, full.shape[1])
    into = pl.ds(f * slope.shape[1] + start, CHUNK)
    wide[0, into, :] = shifted(full, column, -1).astype(BF)
    wide[1, into, :] = grad
    wide[2, into, :] = shifted(full, column, 1).astype(BF)


def windows_of(x_t, f, size):
    return jnp.concatenate([x_t[f, :, i * COLS : i * COLS + size] for i in range(3)], axis=0)


def gradient_kernel(
    core,
    ahead,
    weight,
    slope,
    x_t,
    act_t,
    partial,
    early,
    pgrad,
    keep,
    send,
    last,
    first,
    wide,
    terms,
    sems,
):
    frames, size, chans = ahead.shape

    @pl.loop(0, size // CHUNK)
    def _(step):
        start = pl.multiple_of(step * CHUNK, CHUNK)
        at = pl.ds(start, CHUNK)
        block = ahead[0, at, :]
        more = lax.dot_general(block, weight[2], NT, preferred_element_type=F32)
        finish(0, start, partial[0, at, :] + more, slope, wide)
        both = jnp.concatenate([block, ahead[1, at, :]], axis=1)
        taps = jnp.concatenate([weight[1], weight[2]], axis=1)
        more = lax.dot_general(both, taps, NT, preferred_element_type=F32)
        finish(1, start, partial[1, at, :] + more, slope, wide)

    stores = []
    for f in range(frames):
        rows = pl.ds(f * size, size)
        stores.append(pltpu.make_async_copy(wide.at[1, rows], pgrad.at[f], sems.at[f]))
        stores[f].start()
        last[f] = wide[1, (f + 1) * size - COLS : (f + 1) * size, :]
        first[f] = wide[1, f * size : f * size + COLS, :]

    def put(tap, value):
        for h in range(2):
            at = (tap * 2 + h) * chans
            terms[at : at + chans, :] = value[:, h * 128 : (h + 1) * 128].astype(BF)

    left = jnp.concatenate([windows_of(x_t, f, size) for f in range(frames)], axis=1)
    for j in range(3):
        out = jnp.dot(left, wide[j], preferred_element_type=F32)
        for i in range(3):
            put(3 * i + j, out[i * chans : (i + 1) * chans])
    put(9, early[0])
    put(10, early[1] + jnp.dot(act_t[1], ahead[0], preferred_element_type=F32))
    left_t = jnp.concatenate([act_t[0], act_t[1]], axis=1)
    right = ahead[...].reshape(frames * size, chans)
    put(11, jnp.dot(left_t, right, preferred_element_type=F32))
    half = terms.shape[0] // 2
    for c in range(2):

        @pl.when(core[0] == c)
        def _():
            keep[...] = terms[c * half : (c + 1) * half, :]
            send[...] = terms[(1 - c) * half : (2 - c) * half, :]

    for store in stores:
        store.wait()


def add_kernel(a, b, out):
    out[...] = (a[...].astype(F32) + b[...].astype(F32)).astype(BF)


def sum_kernel(parts, out):
    total = parts[0].astype(F32)
    for i in range(1, parts.shape[0]):
        total = total + parts[i].astype(F32)
    out[...] = total.astype(out.dtype)


def spread_sum_kernel(scale, parts, out):
    total = parts[0].astype(F32)
    for i in range(1, parts.shape[0]):
        total = total + parts[i].astype(F32)
    total = (total * scale).astype(out.dtype)
    for i in range(out.shape[0]):
        out[i] = total


def write_half(first, source, spatial, temporal, wide, sems):
    copies = []
    for n in range(6):
        t = n if first else n + 6
        for h in range(2):
            at = (n * 2 + h) * 256
            wide[n, :, h * 128 : (h + 1) * 128] = source[at : at + 256, :].astype(F32)
        target = spatial.at[t] if t < 9 else temporal.at[t - 9]
        copy = pltpu.make_async_copy(wide.at[n], target, sems.at[n])
        copy.start()
        copies.append(copy)
    for copy in copies:
        copy.wait()


def own_kernel(core, own, spatial, temporal, wide, sems):
    for c in range(2):

        @pl.when(core[0] == c)
        def _():
            write_half(c == 0, own, spatial, temporal, wide, sems)


def other_kernel(core, other, spatial_in, temporal_in, spatial, temporal, wide, sems):
    for c in range(2):

        @pl.when(core[0] == c)
        def _():
            write_half(c == 1, other, spatial, temporal, wide, sems)


def back_taps(taps, j):
    return jnp.concatenate([taps[i, j] for i in range(3)], axis=1)


def back_kernel(grad, weight, dy, out, edge, padded, taps, own, result, sems):
    frames, size, chans = own.shape
    whole = pltpu.make_async_copy(weight, taps, sems.at[0])
    whole.start()
    loads = []
    for f in range(frames):
        base = 1 + 3 * f
        loads.append(
            [
                pltpu.make_async_copy(
                    grad.at[f], padded.at[f, pl.ds(COLS, size)], sems.at[base]
                ),
                pltpu.make_async_copy(dy.at[f], own.at[f], sems.at[base + 1]),
            ]
        )
        for load in loads[f]:
            load.start()
        blank = jnp.zeros((COLS, chans), BF)
        padded[f, 0:COLS, :] = blank
        padded[f, COLS + size :, :] = blank
    whole.wait()
    stores = []
    for f in range(frames):
        for load in loads[f]:
            load.wait()

        @pl.loop(0, size // CHUNK)
        def _(step):
            start = pl.multiple_of(step * CHUNK, CHUNK)
            at = pl.ds(start, CHUNK)
            rows = window(padded, f, start, CHUNK, (2, 1, 0))
            column = columns_of(CHUNK, chans)
            z = [
                lax.dot_general(rows, back_taps(taps, j), NT, preferred_element_type=F32)
                for j in range(3)
            ]
            back = shifted(z[0], column, -1) + z[1] + shifted(z[2], column, 1)
            total = own[f, at, :].astype(F32) + back
            result[f, at, :] = total.astype(BF)

            @pl.when(step == 0)
            def _():
                edge[f, 0] = total[:COLS]

            @pl.when(step == size // CHUNK - 1)
            def _():
                edge[f, 1] = total[CHUNK - COLS :]

        store = pltpu.make_async_copy(result.at[f], out.at[f], sems.at[3 + 3 * f])
        store.start()
        stores.append(store)
    for store in stores:
        store.wait()


def edge_kernel(top, bottom, weight, edge, part, out, result, sems):
    frames, size = part.shape[0], part.shape[1]
    chans = part.shape[2]
    column = columns_of(frames * COLS, chans)
    stores = []
    for e, (rim, i) in enumerate(((top, 2), (bottom, 0))):
        rows = rim[...].reshape(frames * COLS, chans)
        z = [
            lax.dot_general(rows, weight[i, j], NT, preferred_element_type=F32) for j in range(3)
        ]
        more = shifted(z[0], column, -1) + z[1] + shifted(z[2], column, 1)
        for f in range(frames):
            total = edge[f, e] + more[f * COLS : (f + 1) * COLS]
            result[f, e] = total.astype(BF)
            target = out.at[f, pl.ds(e * (size - COLS), COLS)]
            store = pltpu.make_async_copy(result.at[f, e], target, sems.at[2 * f + e])
            store.start()
            stores.append(store)
    for store in stores:
        store.wait()


def mix_kernel(act, behind, weight, x, out, ext, own, result, sems):
    frames, size, chans = own.shape
    loads = [pltpu.make_async_copy(behind.at[f], ext.at[f], sems.at[f]) for f in range(frames)]
    for f in range(frames):
        loads.append(pltpu.make_async_copy(act.at[f], ext.at[frames + f], sems.at[frames + 2 * f]))
        loads.append(pltpu.make_async_copy(x.at[f], own.at[f], sems.at[frames + 2 * f + 1]))
    for load in loads:
        load.start()
    for load in loads[:frames]:
        load.wait()
    stores = []
    for f in range(frames):
        for load in loads[frames + 2 * f : frames + 2 * f + 2]:
            load.wait()
        rows = jnp.concatenate([ext[f + 2 - k] for k in range(3)], axis=1)
        taps = weight[...].reshape(3 * chans, chans)
        mixed = jnp.dot(rows, taps, preferred_element_type=F32).astype(BF)
        result[f] = (own[f].astype(F32) + mixed.astype(F32)).astype(BF)
        store = pltpu.make_async_copy(result.at[f], out.at[f], sems.at[3 * frames + f])
        store.start()
        stores.append(store)
    for store in stores:
        store.wait()


def steps(axes, by):
    count = lax.axis_size(axes)
    return [(i, i + by) for i in range(count) if 0 <= i + by < count]


def exchange(value, axes):
    return lax.all_to_all(value, axes, split_axis=0, concat_axis=0, tiled=True)


def swap_rims(last, first):
    return lax.ppermute(last, SPACE, steps(SPACE, 1)), lax.ppermute(first, SPACE, steps(SPACE, -1))


def local(scale, frames_in, cotangent, spatial_weight, temporal_weight):
    dims = frames_in.shape
    frames, chans = dims[1], dims[4]
    size = dims[2] * dims[3]
    x = frames_in.reshape(frames, size, chans)
    dy = cotangent.reshape(frames, size, chans)
    work = 2 * frames * size * chans * chans
    core = lax.axis_index("core").astype(jnp.int32).reshape(1)
    ahead = lax.ppermute(dy, TM, steps(TM, -1))
    top, bottom = swap_rims(x[:, size - COLS :, :], x[:, :COLS, :])
    act, slope, x_t, act_t = call(
        forward_kernel,
        [
            shape((frames, size, chans)),
            shape((frames, size, chans), F32),
            shape((frames, chans, size + 2 * COLS)),
            shape((frames, chans, size)),
        ],
        (x, top, bottom, spatial_weight),
        [pltpu.VMEM((frames, size + 2 * COLS, chans), BF)],
        flops=9 * work,
        moved=9 << 20,
    )
    partial, early = call(
        early_kernel,
        [shape((frames, size, chans), F32), shape((2, chans, chans), F32)],
        (dy, temporal_weight, act_t),
        flops=6 * work,
        moved=6 << 20,
    )
    behind = lax.ppermute(act, TM, steps(TM, 1))
    flat = frames * size
    rows = 12 * chans
    edges = shape((frames, COLS, chans))
    pgrad, keep, send, last, first = call(
        gradient_kernel,
        [shape((frames, size, chans)), shape((rows, 128)), shape((rows, 128)), edges, edges],
        (core, ahead, temporal_weight, slope, x_t, act_t, partial, early),
        [
            pltpu.VMEM((3, flat, chans), BF),
            pltpu.VMEM((2 * rows, 128), BF),
            pltpu.SemaphoreType.DMA((frames,)),
        ],
        flops=work // 16,
        moved=1 << 18,
        smem=(0,),
        out_hbm=(0,),
    )
    grad_top, grad_bottom = swap_rims(last, first)
    pair = [(0, 1), (1, 0)]
    got = lax.ppermute(send, "core", pair)
    half = call(add_kernel, shape((rows, 128)), (keep, got), moved=3 << 20)
    block = pltpu.VMEM((frames, size, chans), BF)
    line, rank = lax.axis_size("x"), lax.axis_size("y")
    column, plane = lax.axis_size(COLUMN), lax.axis_size(PLANE)
    share = rows // line
    first = exchange(half.reshape(line, share, 128), "x")
    part = call(sum_kernel, shape((share, 128)), (first,), moved=1 << 18)
    second = exchange(part.reshape(rank, share // rank, 128), "y")
    inner, edge = call(
        back_kernel,
        [shape((frames, size, chans)), shape((frames, 2, COLS, chans), F32)],
        (pgrad, spatial_weight, dy),
        [
            pltpu.VMEM((frames, size + 2 * COLS, chans), BF),
            pltpu.VMEM((3, 3, chans, chans), BF),
            block,
            block,
            pltpu.SemaphoreType.DMA((7,)),
        ],
        flops=9 * work,
        moved=5 << 20,
        hbm=range(3),
        out_hbm=(0,),
        limit=58,
    )
    second, edge = lax.optimization_barrier((second, edge))
    spread = call(
        functools.partial(spread_sum_kernel, 1.0),
        shape((column, share // rank, 128)),
        (second,),
        moved=1 << 18,
        after=(behind,),
    )
    third = exchange(spread, COLUMN)
    block_out = call(
        mix_kernel,
        shape((frames, size, chans)),
        (act, behind, temporal_weight, x),
        [
            pltpu.VMEM((2 * frames, size, chans), BF),
            block,
            block,
            pltpu.SemaphoreType.DMA((4 * frames,)),
        ],
        flops=3 * work,
        moved=4 << 20,
        hbm=(0, 1, 3),
        out_hbm=True,
        limit=58,
    )
    third, grad_top, grad_bottom = lax.optimization_barrier((third, grad_top, grad_bottom))
    input_grad = call(
        edge_kernel,
        shape((frames, size, chans)),
        (grad_top, grad_bottom, spatial_weight, edge, inner),
        [pltpu.VMEM((frames, 2, COLS, chans), BF), pltpu.SemaphoreType.DMA((2 * frames,))],
        flops=work,
        moved=1 << 20,
        hbm=(4,),
        out_hbm=True,
        alias={4: 0},
    )
    wider = call(
        functools.partial(spread_sum_kernel, scale),
        shape((plane, share // rank, 128)),
        (third,),
        moved=1 << 18,
    )
    own = exchange(wider, PLANE).reshape(rows, 128)
    own, block_out, input_grad = lax.optimization_barrier((own, block_out, input_grad))
    other = lax.ppermute(own, "core", pair)
    grads = [shape((9, chans, chans), F32), shape((3, chans, chans), F32)]
    room = [pltpu.VMEM((6, chans, chans), F32), pltpu.SemaphoreType.DMA((6,))]
    spatial, temporal = call(
        own_kernel, grads, (core, own), room, moved=3 << 20, smem=(0,), out_hbm=True
    )
    spatial, temporal = call(
        other_kernel,
        grads,
        (core, other, spatial, temporal),
        room,
        moved=3 << 20,
        smem=(0,),
        hbm=(2, 3),
        out_hbm=True,
        alias={2: 0, 3: 1},
    )
    return (
        block_out.reshape(dims),
        input_grad.reshape(dims),
        spatial.reshape(3, 3, chans, chans),
        temporal,
    )


def solution(mesh):
    fine = Mesh(mesh.devices.reshape(2, 4, 4, 4, 2), ("clip", "y", "zl", "x", "core"))
    blocks = P("clip", TM, SPACE, None, None)

    def run(frames_in, cotangent, spatial_weight, temporal_weight):
        clips, frames, height, width, _ = frames_in.shape
        scale = (clips * frames * height * width) ** -0.5
        return jax.shard_map(
            functools.partial(local, scale),
            mesh=fine,
            in_specs=(blocks, blocks, P(), P()),
            out_specs=(blocks, blocks, P(), P()),
            check_vma=False,
        )(frames_in, cotangent, spatial_weight, temporal_weight)

    return run
```

```python
import functools

import jax
import jax.numpy as jnp
from jax import lax
from jax.experimental import pallas as pl
from jax.experimental.pallas import tpu as pltpu
from jax.sharding import Mesh, PartitionSpec as P

BF = jnp.bfloat16
F32 = jnp.float32
TM = ("y", "zl")
SPACE = ("x", "core")
PLANE = ("x", "y")
COLUMN = ("clip", "zl")
COLS = 128
NT = (((1,), (1,)), ((), ()))


def call(kernel, outs, ins, scratch=(), flops=0, moved=0, limit=20, smem=(), after=(), hbm=(), out_hbm=False, alias=None):
    vmem = pl.BlockSpec(memory_space=pltpu.VMEM)
    specs = [pl.BlockSpec(memory_space=pltpu.SMEM) if i in smem else vmem for i in range(len(ins))]
    specs = [pl.BlockSpec(memory_space=pl.ANY) if i in hbm else p for i, p in enumerate(specs)]
    specs += [pl.BlockSpec(memory_space=pltpu.HBM)] * len(after)
    many = isinstance(outs, list)
    placed = [
        pl.BlockSpec(memory_space=pltpu.HBM) if out_hbm is True or i in (out_hbm or ()) else vmem
        for i in range(len(outs) if many else 1)
    ]
    count = len(ins)

    def body(*refs):
        kernel(*refs[:count], *refs[count + len(after) :])

    return pl.pallas_call(
        body,
        out_shape=outs,
        in_specs=specs,
        out_specs=placed if many else placed[0],
        input_output_aliases=alias or {},
        scratch_shapes=list(scratch),
        cost_estimate=pl.CostEstimate(flops=flops, bytes_accessed=moved, transcendentals=0),
        compiler_params=pltpu.CompilerParams(vmem_limit_bytes=limit << 20),
    )(*ins, *after)


def shape(dims, kind=BF):
    return jax.ShapeDtypeStruct(dims, kind)


def shifted(value, column, step):
    edge = 0 if step == 1 else COLS - 1
    rolled = pltpu.roll(value, step % value.shape[0], 0)
    return jnp.where(column == edge, 0.0, rolled)


def columns_of(rows, width):
    return lax.broadcasted_iota(jnp.int32, (rows, width), 0) % COLS


def window(ref, frame, start, rows, offsets):
    parts = [ref[frame, pl.ds(start + off * COLS, rows), :] for off in offsets]
    return jnp.concatenate(parts, axis=1)


CHUNK = 512
SWAPS = 4


def fill(padded, block, top, bottom, frame):
    size = block.shape[1]
    padded[frame, 0:COLS, :] = top[frame]
    padded[frame, COLS : COLS + size, :] = block[frame]
    padded[frame, COLS + size :, :] = bottom[frame]


def forward_kernel(x, top, bottom, weight, act, slope, x_t, act_t, padded):
    frames, size, chans = x.shape
    for f in range(frames):
        fill(padded, x, top, bottom, f)

    @pl.loop(0, frames * (size // CHUNK))
    def _(step):
        f = step // (size // CHUNK)
        start = pl.multiple_of((step % (size // CHUNK)) * CHUNK, CHUNK)
        rows = window(padded, f, start, CHUNK, (0, 1, 2))
        column = columns_of(CHUNK, chans)
        z = [
            jnp.dot(rows, weight[:, j].reshape(3 * chans, chans), preferred_element_type=F32)
            for j in range(3)
        ]
        pre = shifted(z[0], column, 1) + z[1] + shifted(z[2], column, -1)
        sigma = 1.0 / (1.0 + jnp.exp(-pre))
        active = (pre * sigma).astype(BF)
        act[f, pl.ds(start, CHUNK), :] = active
        slope[f, pl.ds(start, CHUNK), :] = sigma * (1.0 + pre * (1.0 - sigma))
        act_t[f, :, pl.ds(start, CHUNK)] = active.T

    for f in range(frames):
        x_t[f] = padded[f].T


def early_kernel(dy, weight, act_t, partial, terms):
    frames, size, chans = dy.shape

    @pl.loop(0, size // CHUNK)
    def _(step):
        at = pl.ds(pl.multiple_of(step * CHUNK, CHUNK), CHUNK)
        second = dy[1, at, :]
        both = jnp.concatenate([dy[0, at, :], second], axis=1)
        taps = jnp.concatenate([weight[0], weight[1]], axis=1)
        partial[0, at, :] = lax.dot_general(both, taps, NT, preferred_element_type=F32)
        partial[1, at, :] = lax.dot_general(second, weight[0], NT, preferred_element_type=F32)

    left = jnp.concatenate([act_t[0], act_t[1]], axis=1)
    right = dy[...].reshape(frames * size, chans)
    terms[0] = jnp.dot(left, right, preferred_element_type=F32)
    terms[1] = jnp.dot(act_t[0], dy[1], preferred_element_type=F32)


def finish(f, start, agrad, slope, wide):
    at = pl.ds(start, CHUNK)
    grad = (agrad.astype(BF).astype(F32) * slope[f, at, :]).astype(BF)
    full = grad.astype(F32)
    column = columns_of(CHUNK, full.shape[1])
    into = pl.ds(f * slope.shape[1] + start, CHUNK)
    wide[0, into, :] = shifted(full, column, -1).astype(BF)
    wide[1, into, :] = grad
    wide[2, into, :] = shifted(full, column, 1).astype(BF)


def windows_of(x_t, f, size):
    return jnp.concatenate([x_t[f, :, i * COLS : i * COLS + size] for i in range(3)], axis=0)


def gradient_kernel(
    core,
    ahead,
    weight,
    slope,
    x_t,
    act_t,
    partial,
    early,
    pgrad,
    keep,
    last,
    first,
    *rest,
):
    *sends, wide, terms, sems = rest
    frames, size, chans = ahead.shape

    @pl.loop(0, size // CHUNK)
    def _(step):
        start = pl.multiple_of(step * CHUNK, CHUNK)
        at = pl.ds(start, CHUNK)
        block = ahead[0, at, :]
        more = lax.dot_general(block, weight[2], NT, preferred_element_type=F32)
        finish(0, start, partial[0, at, :] + more, slope, wide)
        both = jnp.concatenate([block, ahead[1, at, :]], axis=1)
        taps = jnp.concatenate([weight[1], weight[2]], axis=1)
        more = lax.dot_general(both, taps, NT, preferred_element_type=F32)
        finish(1, start, partial[1, at, :] + more, slope, wide)

    stores = []
    for f in range(frames):
        rows = pl.ds(f * size, size)
        stores.append(pltpu.make_async_copy(wide.at[1, rows], pgrad.at[f], sems.at[f]))
        stores[f].start()
        last[f] = wide[1, (f + 1) * size - COLS : (f + 1) * size, :]
        first[f] = wide[1, f * size : f * size + COLS, :]

    def put(tap, value):
        for h in range(2):
            at = (tap * 2 + h) * chans
            terms[at : at + chans, :] = value[:, h * 128 : (h + 1) * 128].astype(BF)

    left = jnp.concatenate([windows_of(x_t, f, size) for f in range(frames)], axis=1)
    for j in range(3):
        out = jnp.dot(left, wide[j], preferred_element_type=F32)
        for i in range(3):
            put(3 * i + j, out[i * chans : (i + 1) * chans])
    put(9, early[0])
    put(10, early[1] + jnp.dot(act_t[1], ahead[0], preferred_element_type=F32))
    left_t = jnp.concatenate([act_t[0], act_t[1]], axis=1)
    right = ahead[...].reshape(frames * size, chans)
    put(11, jnp.dot(left_t, right, preferred_element_type=F32))
    half = terms.shape[0] // 2
    for c in range(2):

        @pl.when(core[0] == c)
        def _():
            keep[...] = terms[c * half : (c + 1) * half, :]
            cut = sends[0].shape[0]
            for n, send in enumerate(sends):
                at = (1 - c) * half + n * cut
                send[...] = terms[at : at + cut, :]

    for store in stores:
        store.wait()


def add_kernel(a, *refs):
    out = refs[-1]
    cut = refs[0].shape[0]
    for n, b in enumerate(refs[:-1]):
        rows = pl.ds(n * cut, cut)
        out[rows, :] = (a[rows, :].astype(F32) + b[...].astype(F32)).astype(BF)


def sum_kernel(parts, out):
    total = parts[0].astype(F32)
    for i in range(1, parts.shape[0]):
        total = total + parts[i].astype(F32)
    out[...] = total.astype(out.dtype)


def spread_sum_kernel(scale, parts, out):
    total = parts[0].astype(F32)
    for i in range(1, parts.shape[0]):
        total = total + parts[i].astype(F32)
    total = (total * scale).astype(out.dtype)
    for i in range(out.shape[0]):
        out[i] = total


def write_half(first, source, spatial, temporal, wide, sems):
    copies = []
    for n in range(6):
        t = n if first else n + 6
        for h in range(2):
            at = (n * 2 + h) * 256
            wide[n, :, h * 128 : (h + 1) * 128] = source[at : at + 256, :].astype(F32)
        target = spatial.at[t] if t < 9 else temporal.at[t - 9]
        copy = pltpu.make_async_copy(wide.at[n], target, sems.at[n])
        copy.start()
        copies.append(copy)
    for copy in copies:
        copy.wait()


def own_kernel(core, own, spatial, temporal, wide, sems):
    for c in range(2):

        @pl.when(core[0] == c)
        def _():
            write_half(c == 0, own, spatial, temporal, wide, sems)


def other_kernel(core, other, spatial_in, temporal_in, spatial, temporal, wide, sems):
    for c in range(2):

        @pl.when(core[0] == c)
        def _():
            write_half(c == 1, other, spatial, temporal, wide, sems)


def back_taps(taps, j):
    return jnp.concatenate([taps[i, j] for i in range(3)], axis=1)


def back_kernel(grad, weight, dy, out, edge, padded, taps, own, result, sems):
    frames, size, chans = own.shape
    whole = pltpu.make_async_copy(weight, taps, sems.at[0])
    whole.start()
    loads = []
    for f in range(frames):
        base = 1 + 3 * f
        loads.append(
            [
                pltpu.make_async_copy(
                    grad.at[f], padded.at[f, pl.ds(COLS, size)], sems.at[base]
                ),
                pltpu.make_async_copy(dy.at[f], own.at[f], sems.at[base + 1]),
            ]
        )
        for load in loads[f]:
            load.start()
        blank = jnp.zeros((COLS, chans), BF)
        padded[f, 0:COLS, :] = blank
        padded[f, COLS + size :, :] = blank
    whole.wait()
    stores = []
    for f in range(frames):
        for load in loads[f]:
            load.wait()

        @pl.loop(0, size // CHUNK)
        def _(step):
            start = pl.multiple_of(step * CHUNK, CHUNK)
            at = pl.ds(start, CHUNK)
            rows = window(padded, f, start, CHUNK, (2, 1, 0))
            column = columns_of(CHUNK, chans)
            z = [
                lax.dot_general(rows, back_taps(taps, j), NT, preferred_element_type=F32)
                for j in range(3)
            ]
            back = shifted(z[0], column, -1) + z[1] + shifted(z[2], column, 1)
            total = own[f, at, :].astype(F32) + back
            result[f, at, :] = total.astype(BF)

            @pl.when(step == 0)
            def _():
                edge[f, 0] = total[:COLS]

            @pl.when(step == size // CHUNK - 1)
            def _():
                edge[f, 1] = total[CHUNK - COLS :]

        store = pltpu.make_async_copy(result.at[f], out.at[f], sems.at[3 + 3 * f])
        store.start()
        stores.append(store)
    for store in stores:
        store.wait()


def edge_kernel(top, bottom, weight, edge, part, out, result, sems):
    frames, size = part.shape[0], part.shape[1]
    chans = part.shape[2]
    column = columns_of(frames * COLS, chans)
    stores = []
    for e, (rim, i) in enumerate(((top, 2), (bottom, 0))):
        rows = rim[...].reshape(frames * COLS, chans)
        z = [
            lax.dot_general(rows, weight[i, j], NT, preferred_element_type=F32) for j in range(3)
        ]
        more = shifted(z[0], column, -1) + z[1] + shifted(z[2], column, 1)
        for f in range(frames):
            total = edge[f, e] + more[f * COLS : (f + 1) * COLS]
            result[f, e] = total.astype(BF)
            target = out.at[f, pl.ds(e * (size - COLS), COLS)]
            store = pltpu.make_async_copy(result.at[f, e], target, sems.at[2 * f + e])
            store.start()
            stores.append(store)
    for store in stores:
        store.wait()


def mix_kernel(act, behind, weight, x, out, ext, own, result, sems):
    frames, size, chans = own.shape
    loads = [pltpu.make_async_copy(behind.at[f], ext.at[f], sems.at[f]) for f in range(frames)]
    for f in range(frames):
        loads.append(pltpu.make_async_copy(act.at[f], ext.at[frames + f], sems.at[frames + 2 * f]))
        loads.append(pltpu.make_async_copy(x.at[f], own.at[f], sems.at[frames + 2 * f + 1]))
    for load in loads:
        load.start()
    for load in loads[:frames]:
        load.wait()
    stores = []
    for f in range(frames):
        for load in loads[frames + 2 * f : frames + 2 * f + 2]:
            load.wait()
        rows = jnp.concatenate([ext[f + 2 - k] for k in range(3)], axis=1)
        taps = weight[...].reshape(3 * chans, chans)
        mixed = jnp.dot(rows, taps, preferred_element_type=F32).astype(BF)
        result[f] = (own[f].astype(F32) + mixed.astype(F32)).astype(BF)
        store = pltpu.make_async_copy(result.at[f], out.at[f], sems.at[3 * frames + f])
        store.start()
        stores.append(store)
    for store in stores:
        store.wait()


def steps(axes, by):
    count = lax.axis_size(axes)
    return [(i, i + by) for i in range(count) if 0 <= i + by < count]


def exchange(value, axes):
    return lax.all_to_all(value, axes, split_axis=0, concat_axis=0, tiled=True)


def swap_rims(last, first):
    return lax.ppermute(last, SPACE, steps(SPACE, 1)), lax.ppermute(first, SPACE, steps(SPACE, -1))


def local(scale, frames_in, cotangent, spatial_weight, temporal_weight):
    dims = frames_in.shape
    frames, chans = dims[1], dims[4]
    size = dims[2] * dims[3]
    x = frames_in.reshape(frames, size, chans)
    dy = cotangent.reshape(frames, size, chans)
    work = 2 * frames * size * chans * chans
    core = lax.axis_index("core").astype(jnp.int32).reshape(1)
    ahead = lax.ppermute(dy, TM, steps(TM, -1))
    top, bottom = swap_rims(x[:, size - COLS :, :], x[:, :COLS, :])
    act, slope, x_t, act_t = call(
        forward_kernel,
        [
            shape((frames, size, chans)),
            shape((frames, size, chans), F32),
            shape((frames, chans, size + 2 * COLS)),
            shape((frames, chans, size)),
        ],
        (x, top, bottom, spatial_weight),
        [pltpu.VMEM((frames, size + 2 * COLS, chans), BF)],
        flops=9 * work,
        moved=9 << 20,
    )
    partial, early = call(
        early_kernel,
        [shape((frames, size, chans), F32), shape((2, chans, chans), F32)],
        (dy, temporal_weight, act_t),
        flops=6 * work,
        moved=6 << 20,
    )
    act, ahead = lax.optimization_barrier((act, ahead))
    behind = lax.ppermute(act, TM, steps(TM, 1))
    flat = frames * size
    rows = 12 * chans
    edges = shape((frames, COLS, chans))
    pgrad, keep, last, first, *send = call(
        gradient_kernel,
        [shape((frames, size, chans)), shape((rows, 128)), edges, edges]
        + [shape((rows // SWAPS, 128))] * SWAPS,
        (core, ahead, temporal_weight, slope, x_t, act_t, partial, early),
        [
            pltpu.VMEM((3, flat, chans), BF),
            pltpu.VMEM((2 * rows, 128), BF),
            pltpu.SemaphoreType.DMA((frames,)),
        ],
        flops=1 << 10,
        moved=1 << 12,
        smem=(0,),
        out_hbm=(0,),
    )
    grad_top, grad_bottom = swap_rims(last, first)
    pair = [(0, 1), (1, 0)]
    got = [lax.ppermute(part, "core", pair) for part in send]
    half = call(add_kernel, shape((rows, 128)), (keep, *got), moved=1 << 12)
    block = pltpu.VMEM((frames, size, chans), BF)
    column, plane = lax.axis_size(COLUMN), lax.axis_size(PLANE)
    share = rows // plane
    first = exchange(half.reshape(plane, share, 128), PLANE)
    inner, edge = call(
        back_kernel,
        [shape((frames, size, chans)), shape((frames, 2, COLS, chans), F32)],
        (pgrad, spatial_weight, dy),
        [
            pltpu.VMEM((frames, size + 2 * COLS, chans), BF),
            pltpu.VMEM((3, 3, chans, chans), BF),
            block,
            block,
            pltpu.SemaphoreType.DMA((7,)),
        ],
        flops=9 * work,
        moved=5 << 20,
        hbm=range(3),
        out_hbm=(0,),
        limit=58,
    )
    first, edge = lax.optimization_barrier((first, edge))
    spread = call(
        functools.partial(spread_sum_kernel, 1.0),
        shape((column, share, 128)),
        (first,),
        moved=1 << 12,
        after=(behind,),
    )
    third = exchange(spread, COLUMN)
    block_out = call(
        mix_kernel,
        shape((frames, size, chans)),
        (act, behind, temporal_weight, x),
        [
            pltpu.VMEM((2 * frames, size, chans), BF),
            block,
            block,
            pltpu.SemaphoreType.DMA((4 * frames,)),
        ],
        flops=3 * work,
        moved=4 << 20,
        hbm=(0, 1, 3),
        out_hbm=True,
        limit=58,
    )
    third, grad_top, grad_bottom = lax.optimization_barrier((third, grad_top, grad_bottom))
    input_grad = call(
        edge_kernel,
        shape((frames, size, chans)),
        (grad_top, grad_bottom, spatial_weight, edge, inner),
        [pltpu.VMEM((frames, 2, COLS, chans), BF), pltpu.SemaphoreType.DMA((2 * frames,))],
        flops=work,
        moved=1 << 20,
        hbm=(4,),
        out_hbm=True,
        alias={4: 0},
    )
    wider = call(
        functools.partial(spread_sum_kernel, scale),
        shape((plane, share, 128)),
        (third,),
        moved=1 << 12,
    )
    own = exchange(wider, PLANE).reshape(rows, 128)
    own, block_out, input_grad = lax.optimization_barrier((own, block_out, input_grad))
    other = lax.ppermute(own, "core", pair)
    grads = [shape((9, chans, chans), F32), shape((3, chans, chans), F32)]
    room = [pltpu.VMEM((6, chans, chans), F32), pltpu.SemaphoreType.DMA((6,))]
    spatial, temporal = call(
        own_kernel, grads, (core, own), room, moved=3 << 20, smem=(0,), out_hbm=True
    )
    spatial, temporal = call(
        other_kernel,
        grads,
        (core, other, spatial, temporal),
        room,
        moved=3 << 20,
        smem=(0,),
        hbm=(2, 3),
        out_hbm=True,
        alias={2: 0, 3: 1},
    )
    return (
        block_out.reshape(dims),
        input_grad.reshape(dims),
        spatial.reshape(3, 3, chans, chans),
        temporal,
    )


def solution(mesh):
    fine = Mesh(mesh.devices.reshape(2, 4, 4, 4, 2), ("clip", "y", "zl", "x", "core"))
    blocks = P("clip", TM, SPACE, None, None)

    def run(frames_in, cotangent, spatial_weight, temporal_weight):
        clips, frames, height, width, _ = frames_in.shape
        scale = (clips * frames * height * width) ** -0.5
        return jax.shard_map(
            functools.partial(local, scale),
            mesh=fine,
            in_specs=(blocks, blocks, P(), P()),
            out_specs=(blocks, blocks, P(), P()),
            check_vma=False,
        )(frames_in, cotangent, spatial_weight, temporal_weight)

    return run
```

```python
import functools

import jax
import jax.numpy as jnp
from jax import lax
from jax.experimental import pallas as pl
from jax.experimental.pallas import tpu as pltpu
from jax.sharding import Mesh, PartitionSpec as P

BF = jnp.bfloat16
F32 = jnp.float32
TM = ("y", "zl")
SPACE = ("x", "core")
PLANE = ("x", "y")
COLUMN = ("clip", "zl")
COLS = 128
NT = (((1,), (1,)), ((), ()))


def call(kernel, outs, ins, scratch=(), flops=0, moved=0, limit=20, smem=(), after=(), hbm=(), out_hbm=False, alias=None):
    vmem = pl.BlockSpec(memory_space=pltpu.VMEM)
    specs = [pl.BlockSpec(memory_space=pltpu.SMEM) if i in smem else vmem for i in range(len(ins))]
    specs = [pl.BlockSpec(memory_space=pl.ANY) if i in hbm else p for i, p in enumerate(specs)]
    specs += [pl.BlockSpec(memory_space=pltpu.HBM)] * len(after)
    many = isinstance(outs, list)
    placed = [
        pl.BlockSpec(memory_space=pltpu.HBM) if out_hbm is True or i in (out_hbm or ()) else vmem
        for i in range(len(outs) if many else 1)
    ]
    count = len(ins)

    def body(*refs):
        kernel(*refs[:count], *refs[count + len(after) :])

    return pl.pallas_call(
        body,
        out_shape=outs,
        in_specs=specs,
        out_specs=placed if many else placed[0],
        input_output_aliases=alias or {},
        scratch_shapes=list(scratch),
        cost_estimate=pl.CostEstimate(flops=flops, bytes_accessed=moved, transcendentals=0),
        compiler_params=pltpu.CompilerParams(vmem_limit_bytes=limit << 20),
    )(*ins, *after)


def shape(dims, kind=BF):
    return jax.ShapeDtypeStruct(dims, kind)


def shifted(value, column, step):
    edge = 0 if step == 1 else COLS - 1
    rolled = pltpu.roll(value, step % value.shape[0], 0)
    return jnp.where(column == edge, 0.0, rolled)


def columns_of(rows, width):
    return lax.broadcasted_iota(jnp.int32, (rows, width), 0) % COLS


def window(ref, frame, start, rows, offsets):
    parts = [ref[frame, pl.ds(start + off * COLS, rows), :] for off in offsets]
    return jnp.concatenate(parts, axis=1)


CHUNK = 512
SWAPS = 4


def fill(padded, block, top, bottom, frame):
    size = block.shape[1]
    padded[frame, 0:COLS, :] = top[frame]
    padded[frame, COLS : COLS + size, :] = block[frame]
    padded[frame, COLS + size :, :] = bottom[frame]


def forward_kernel(x, top, bottom, weight, act, slope, x_t, act_t, padded):
    frames, size, chans = x.shape
    for f in range(frames):
        fill(padded, x, top, bottom, f)

    @pl.loop(0, frames * (size // CHUNK))
    def _(step):
        f = step // (size // CHUNK)
        start = pl.multiple_of((step % (size // CHUNK)) * CHUNK, CHUNK)
        rows = window(padded, f, start, CHUNK, (0, 1, 2))
        column = columns_of(CHUNK, chans)
        z = [
            jnp.dot(rows, weight[:, j].reshape(3 * chans, chans), preferred_element_type=F32)
            for j in range(3)
        ]
        pre = shifted(z[0], column, 1) + z[1] + shifted(z[2], column, -1)
        sigma = 1.0 / (1.0 + jnp.exp(-pre))
        active = (pre * sigma).astype(BF)
        act[f, pl.ds(start, CHUNK), :] = active
        slope[f, pl.ds(start, CHUNK), :] = sigma * (1.0 + pre * (1.0 - sigma))
        act_t[f, :, pl.ds(start, CHUNK)] = active.T

    for f in range(frames):
        x_t[f] = padded[f].T


def early_kernel(dy, weight, act_t, partial, terms):
    frames, size, chans = dy.shape

    @pl.loop(0, size // CHUNK)
    def _(step):
        at = pl.ds(pl.multiple_of(step * CHUNK, CHUNK), CHUNK)
        second = dy[1, at, :]
        both = jnp.concatenate([dy[0, at, :], second], axis=1)
        taps = jnp.concatenate([weight[0], weight[1]], axis=1)
        partial[0, at, :] = lax.dot_general(both, taps, NT, preferred_element_type=F32)
        partial[1, at, :] = lax.dot_general(second, weight[0], NT, preferred_element_type=F32)

    left = jnp.concatenate([act_t[0], act_t[1]], axis=1)
    right = dy[...].reshape(frames * size, chans)
    terms[0] = jnp.dot(left, right, preferred_element_type=F32)
    terms[1] = jnp.dot(act_t[0], dy[1], preferred_element_type=F32)


def finish(f, start, agrad, slope, wide):
    at = pl.ds(start, CHUNK)
    grad = (agrad.astype(BF).astype(F32) * slope[f, at, :]).astype(BF)
    full = grad.astype(F32)
    column = columns_of(CHUNK, full.shape[1])
    into = pl.ds(f * slope.shape[1] + start, CHUNK)
    wide[0, into, :] = shifted(full, column, -1).astype(BF)
    wide[1, into, :] = grad
    wide[2, into, :] = shifted(full, column, 1).astype(BF)


def windows_of(x_t, f, size):
    return jnp.concatenate([x_t[f, :, i * COLS : i * COLS + size] for i in range(3)], axis=0)


def gradient_kernel(
    core,
    ahead,
    weight,
    slope,
    x_t,
    act_t,
    partial,
    early,
    pgrad,
    keep,
    last,
    first,
    *rest,
):
    *sends, wide, terms, sems = rest
    frames, size, chans = ahead.shape

    @pl.loop(0, size // CHUNK)
    def _(step):
        start = pl.multiple_of(step * CHUNK, CHUNK)
        at = pl.ds(start, CHUNK)
        block = ahead[0, at, :]
        more = lax.dot_general(block, weight[2], NT, preferred_element_type=F32)
        finish(0, start, partial[0, at, :] + more, slope, wide)
        both = jnp.concatenate([block, ahead[1, at, :]], axis=1)
        taps = jnp.concatenate([weight[1], weight[2]], axis=1)
        more = lax.dot_general(both, taps, NT, preferred_element_type=F32)
        finish(1, start, partial[1, at, :] + more, slope, wide)

    stores = []
    for f in range(frames):
        rows = pl.ds(f * size, size)
        stores.append(pltpu.make_async_copy(wide.at[1, rows], pgrad.at[f], sems.at[f]))
        stores[f].start()
        last[f] = wide[1, (f + 1) * size - COLS : (f + 1) * size, :]
        first[f] = wide[1, f * size : f * size + COLS, :]

    def put(tap, value):
        for h in range(2):
            at = (tap * 2 + h) * chans
            terms[at : at + chans, :] = value[:, h * 128 : (h + 1) * 128].astype(BF)

    left = jnp.concatenate([windows_of(x_t, f, size) for f in range(frames)], axis=1)
    for j in range(3):
        out = jnp.dot(left, wide[j], preferred_element_type=F32)
        for i in range(3):
            put(3 * i + j, out[i * chans : (i + 1) * chans])
    put(9, early[0])
    put(10, early[1] + jnp.dot(act_t[1], ahead[0], preferred_element_type=F32))
    left_t = jnp.concatenate([act_t[0], act_t[1]], axis=1)
    right = ahead[...].reshape(frames * size, chans)
    put(11, jnp.dot(left_t, right, preferred_element_type=F32))
    half = terms.shape[0] // 2
    for c in range(2):

        @pl.when(core[0] == c)
        def _():
            keep[...] = terms[c * half : (c + 1) * half, :]
            cut = sends[0].shape[0]
            for n, send in enumerate(sends):
                at = (1 - c) * half + n * cut
                send[...] = terms[at : at + cut, :]

    for store in stores:
        store.wait()


def add_kernel(a, *refs):
    out = refs[-1]
    cut = refs[0].shape[0]
    for n, b in enumerate(refs[:-1]):
        rows = pl.ds(n * cut, cut)
        out[rows, :] = (a[rows, :].astype(F32) + b[...].astype(F32)).astype(BF)


def sum_kernel(parts, out):
    total = parts[0].astype(F32)
    for i in range(1, parts.shape[0]):
        total = total + parts[i].astype(F32)
    out[...] = total.astype(out.dtype)


def spread_sum_kernel(scale, parts, out):
    total = parts[0].astype(F32)
    for i in range(1, parts.shape[0]):
        total = total + parts[i].astype(F32)
    total = (total * scale).astype(out.dtype)
    for i in range(out.shape[0]):
        out[i] = total


def write_half(first, source, spatial, temporal, wide, sems):
    copies = []
    for n in range(6):
        t = n if first else n + 6
        for h in range(2):
            at = (n * 2 + h) * 256
            wide[n, :, h * 128 : (h + 1) * 128] = source[at : at + 256, :].astype(F32)
        target = spatial.at[t] if t < 9 else temporal.at[t - 9]
        copy = pltpu.make_async_copy(wide.at[n], target, sems.at[n])
        copy.start()
        copies.append(copy)
    for copy in copies:
        copy.wait()


def own_kernel(core, own, spatial, temporal, wide, sems):
    for c in range(2):

        @pl.when(core[0] == c)
        def _():
            write_half(c == 0, own, spatial, temporal, wide, sems)


def other_kernel(core, other, spatial_in, temporal_in, spatial, temporal, wide, sems):
    for c in range(2):

        @pl.when(core[0] == c)
        def _():
            write_half(c == 1, other, spatial, temporal, wide, sems)


def back_taps(taps, j):
    return jnp.concatenate([taps[i, j] for i in range(3)], axis=1)


def back_kernel(grad, weight, dy, out, edge, padded, taps, own, result, sems):
    frames, size, chans = own.shape
    whole = pltpu.make_async_copy(weight, taps, sems.at[0])
    whole.start()
    loads = []
    for f in range(frames):
        base = 1 + 3 * f
        loads.append(
            [
                pltpu.make_async_copy(
                    grad.at[f], padded.at[f, pl.ds(COLS, size)], sems.at[base]
                ),
                pltpu.make_async_copy(dy.at[f], own.at[f], sems.at[base + 1]),
            ]
        )
        for load in loads[f]:
            load.start()
        blank = jnp.zeros((COLS, chans), BF)
        padded[f, 0:COLS, :] = blank
        padded[f, COLS + size :, :] = blank
    whole.wait()
    stores = []
    for f in range(frames):
        for load in loads[f]:
            load.wait()

        @pl.loop(0, size // CHUNK)
        def _(step):
            start = pl.multiple_of(step * CHUNK, CHUNK)
            at = pl.ds(start, CHUNK)
            rows = window(padded, f, start, CHUNK, (2, 1, 0))
            column = columns_of(CHUNK, chans)
            z = [
                lax.dot_general(rows, back_taps(taps, j), NT, preferred_element_type=F32)
                for j in range(3)
            ]
            back = shifted(z[0], column, -1) + z[1] + shifted(z[2], column, 1)
            total = own[f, at, :].astype(F32) + back
            result[f, at, :] = total.astype(BF)

            @pl.when(step == 0)
            def _():
                edge[f, 0] = total[:COLS]

            @pl.when(step == size // CHUNK - 1)
            def _():
                edge[f, 1] = total[CHUNK - COLS :]

        store = pltpu.make_async_copy(result.at[f], out.at[f], sems.at[3 + 3 * f])
        store.start()
        stores.append(store)
    for store in stores:
        store.wait()


def edge_kernel(top, bottom, weight, edge, part, out, result, sems):
    frames, size = part.shape[0], part.shape[1]
    chans = part.shape[2]
    column = columns_of(frames * COLS, chans)
    stores = []
    for e, (rim, i) in enumerate(((top, 2), (bottom, 0))):
        rows = rim[...].reshape(frames * COLS, chans)
        z = [
            lax.dot_general(rows, weight[i, j], NT, preferred_element_type=F32) for j in range(3)
        ]
        more = shifted(z[0], column, -1) + z[1] + shifted(z[2], column, 1)
        for f in range(frames):
            total = edge[f, e] + more[f * COLS : (f + 1) * COLS]
            result[f, e] = total.astype(BF)
            target = out.at[f, pl.ds(e * (size - COLS), COLS)]
            store = pltpu.make_async_copy(result.at[f, e], target, sems.at[2 * f + e])
            store.start()
            stores.append(store)
    for store in stores:
        store.wait()


def mix_kernel(act, behind, weight, x, out, ext, own, result, sems):
    frames, size, chans = own.shape
    loads = [pltpu.make_async_copy(behind.at[f], ext.at[f], sems.at[f]) for f in range(frames)]
    for f in range(frames):
        loads.append(pltpu.make_async_copy(act.at[f], ext.at[frames + f], sems.at[frames + 2 * f]))
        loads.append(pltpu.make_async_copy(x.at[f], own.at[f], sems.at[frames + 2 * f + 1]))
    for load in loads:
        load.start()
    for load in loads[:frames]:
        load.wait()
    stores = []
    for f in range(frames):
        for load in loads[frames + 2 * f : frames + 2 * f + 2]:
            load.wait()
        rows = jnp.concatenate([ext[f + 2 - k] for k in range(3)], axis=1)
        taps = weight[...].reshape(3 * chans, chans)
        mixed = jnp.dot(rows, taps, preferred_element_type=F32).astype(BF)
        result[f] = (own[f].astype(F32) + mixed.astype(F32)).astype(BF)
        store = pltpu.make_async_copy(result.at[f], out.at[f], sems.at[3 * frames + f])
        store.start()
        stores.append(store)
    for store in stores:
        store.wait()


def steps(axes, by):
    count = lax.axis_size(axes)
    return [(i, i + by) for i in range(count) if 0 <= i + by < count]


def exchange(value, axes):
    return lax.all_to_all(value, axes, split_axis=0, concat_axis=0, tiled=True)


def swap_rims(last, first):
    return lax.ppermute(last, SPACE, steps(SPACE, 1)), lax.ppermute(first, SPACE, steps(SPACE, -1))


def local(scale, frames_in, cotangent, spatial_weight, temporal_weight):
    dims = frames_in.shape
    frames, chans = dims[1], dims[4]
    size = dims[2] * dims[3]
    x = frames_in.reshape(frames, size, chans)
    dy = cotangent.reshape(frames, size, chans)
    work = 2 * frames * size * chans * chans
    core = lax.axis_index("core").astype(jnp.int32).reshape(1)
    ahead = lax.ppermute(dy, TM, steps(TM, -1))
    top, bottom = swap_rims(x[:, size - COLS :, :], x[:, :COLS, :])
    act, slope, x_t, act_t = call(
        forward_kernel,
        [
            shape((frames, size, chans)),
            shape((frames, size, chans), F32),
            shape((frames, chans, size + 2 * COLS)),
            shape((frames, chans, size)),
        ],
        (x, top, bottom, spatial_weight),
        [pltpu.VMEM((frames, size + 2 * COLS, chans), BF)],
        flops=9 * work,
        moved=9 << 20,
    )
    partial, early = call(
        early_kernel,
        [shape((frames, size, chans), F32), shape((2, chans, chans), F32)],
        (dy, temporal_weight, act_t),
        flops=6 * work,
        moved=6 << 20,
    )
    behind = lax.ppermute(act, TM, steps(TM, 1))
    flat = frames * size
    rows = 12 * chans
    edges = shape((frames, COLS, chans))
    pgrad, keep, last, first, *send = call(
        gradient_kernel,
        [shape((frames, size, chans)), shape((rows, 128)), edges, edges]
        + [shape((rows // SWAPS, 128))] * SWAPS,
        (core, ahead, temporal_weight, slope, x_t, act_t, partial, early),
        [
            pltpu.VMEM((3, flat, chans), BF),
            pltpu.VMEM((2 * rows, 128), BF),
            pltpu.SemaphoreType.DMA((frames,)),
        ],
        flops=1 << 10,
        moved=1 << 12,
        smem=(0,),
        out_hbm=(0,),
    )
    grad_top, grad_bottom = swap_rims(last, first)
    pair = [(0, 1), (1, 0)]
    got = [lax.ppermute(part, "core", pair) for part in send]
    half = call(add_kernel, shape((rows, 128)), (keep, *got), moved=1 << 12)
    block = pltpu.VMEM((frames, size, chans), BF)
    column, plane = lax.axis_size(COLUMN), lax.axis_size(PLANE)
    share = rows // plane
    first = exchange(half.reshape(plane, share, 128), PLANE)
    inner, edge = call(
        back_kernel,
        [shape((frames, size, chans)), shape((frames, 2, COLS, chans), F32)],
        (pgrad, spatial_weight, dy),
        [
            pltpu.VMEM((frames, size + 2 * COLS, chans), BF),
            pltpu.VMEM((3, 3, chans, chans), BF),
            block,
            block,
            pltpu.SemaphoreType.DMA((7,)),
        ],
        flops=9 * work,
        moved=5 << 20,
        hbm=range(3),
        out_hbm=(0,),
        limit=58,
    )
    first, edge = lax.optimization_barrier((first, edge))
    spread = call(
        functools.partial(spread_sum_kernel, 1.0),
        shape((column, share, 128)),
        (first,),
        moved=1 << 12,
        after=(behind,),
    )
    third = exchange(spread, COLUMN)
    block_out = call(
        mix_kernel,
        shape((frames, size, chans)),
        (act, behind, temporal_weight, x),
        [
            pltpu.VMEM((2 * frames, size, chans), BF),
            block,
            block,
            pltpu.SemaphoreType.DMA((4 * frames,)),
        ],
        flops=3 * work,
        moved=4 << 20,
        hbm=(0, 1, 3),
        out_hbm=True,
        limit=58,
    )
    third, grad_top, grad_bottom = lax.optimization_barrier((third, grad_top, grad_bottom))
    input_grad = call(
        edge_kernel,
        shape((frames, size, chans)),
        (grad_top, grad_bottom, spatial_weight, edge, inner),
        [pltpu.VMEM((frames, 2, COLS, chans), BF), pltpu.SemaphoreType.DMA((2 * frames,))],
        flops=work,
        moved=1 << 20,
        hbm=(4,),
        out_hbm=True,
        alias={4: 0},
    )
    wider = call(
        functools.partial(spread_sum_kernel, scale),
        shape((plane, share, 128)),
        (third,),
        moved=1 << 12,
    )
    own = exchange(wider, PLANE).reshape(rows, 128)
    own, block_out, input_grad = lax.optimization_barrier((own, block_out, input_grad))
    other = lax.ppermute(own, "core", pair)
    grads = [shape((9, chans, chans), F32), shape((3, chans, chans), F32)]
    room = [pltpu.VMEM((6, chans, chans), F32), pltpu.SemaphoreType.DMA((6,))]
    spatial, temporal = call(
        own_kernel, grads, (core, own), room, moved=3 << 20, smem=(0,), out_hbm=True
    )
    spatial, temporal = call(
        other_kernel,
        grads,
        (core, other, spatial, temporal),
        room,
        moved=3 << 20,
        smem=(0,),
        hbm=(2, 3),
        out_hbm=True,
        alias={2: 0, 3: 1},
    )
    return (
        block_out.reshape(dims),
        input_grad.reshape(dims),
        spatial.reshape(3, 3, chans, chans),
        temporal,
    )


def solution(mesh):
    fine = Mesh(mesh.devices.reshape(2, 4, 4, 4, 2), ("clip", "y", "zl", "x", "core"))
    blocks = P("clip", TM, SPACE, None, None)

    def run(frames_in, cotangent, spatial_weight, temporal_weight):
        clips, frames, height, width, _ = frames_in.shape
        scale = (clips * frames * height * width) ** -0.5
        return jax.shard_map(
            functools.partial(local, scale),
            mesh=fine,
            in_specs=(blocks, blocks, P(), P()),
            out_specs=(blocks, blocks, P(), P()),
            check_vma=False,
        )(frames_in, cotangent, spatial_weight, temporal_weight)

    return run
```

```python
import functools

import jax
import jax.numpy as jnp
from jax import lax
from jax.experimental import pallas as pl
from jax.experimental.pallas import tpu as pltpu
from jax.sharding import Mesh, PartitionSpec as P

BF = jnp.bfloat16
F32 = jnp.float32
TM = ("y", "zl")
SPACE = ("x", "core")
PLANE = ("x", "y")
COLUMN = ("clip", "zl")
COLS = 128
NT = (((1,), (1,)), ((), ()))


def call(kernel, outs, ins, scratch=(), flops=0, moved=0, limit=20, smem=(), after=(), hbm=(), out_hbm=False, alias=None):
    vmem = pl.BlockSpec(memory_space=pltpu.VMEM)
    specs = [pl.BlockSpec(memory_space=pltpu.SMEM) if i in smem else vmem for i in range(len(ins))]
    specs = [pl.BlockSpec(memory_space=pl.ANY) if i in hbm else p for i, p in enumerate(specs)]
    specs += [pl.BlockSpec(memory_space=pltpu.HBM)] * len(after)
    many = isinstance(outs, list)
    placed = [
        pl.BlockSpec(memory_space=pltpu.HBM) if out_hbm is True or i in (out_hbm or ()) else vmem
        for i in range(len(outs) if many else 1)
    ]
    count = len(ins)

    def body(*refs):
        kernel(*refs[:count], *refs[count + len(after) :])

    return pl.pallas_call(
        body,
        out_shape=outs,
        in_specs=specs,
        out_specs=placed if many else placed[0],
        input_output_aliases=alias or {},
        scratch_shapes=list(scratch),
        cost_estimate=pl.CostEstimate(flops=flops, bytes_accessed=moved, transcendentals=0),
        compiler_params=pltpu.CompilerParams(vmem_limit_bytes=limit << 20),
    )(*ins, *after)


def shape(dims, kind=BF):
    return jax.ShapeDtypeStruct(dims, kind)


def shifted(value, column, step):
    edge = 0 if step == 1 else COLS - 1
    rolled = pltpu.roll(value, step % value.shape[0], 0)
    return jnp.where(column == edge, 0.0, rolled)


def columns_of(rows, width):
    return lax.broadcasted_iota(jnp.int32, (rows, width), 0) % COLS


def window(ref, frame, start, rows, offsets):
    parts = [ref[frame, pl.ds(start + off * COLS, rows), :] for off in offsets]
    return jnp.concatenate(parts, axis=1)


CHUNK = 512
SWAPS = 4


def fill(padded, block, top, bottom, frame):
    size = block.shape[1]
    padded[frame, 0:COLS, :] = top[frame]
    padded[frame, COLS : COLS + size, :] = block[frame]
    padded[frame, COLS + size :, :] = bottom[frame]


def turn_kernel(x, weight, x_t):
    for f in range(x.shape[0]):
        x_t[f] = x[f].T


def forward_kernel(x, top, bottom, weight, act, slope, top_t, bottom_t, act_t, padded):
    frames, size, chans = x.shape
    for f in range(frames):
        fill(padded, x, top, bottom, f)

    @pl.loop(0, frames * (size // CHUNK))
    def _(step):
        f = step // (size // CHUNK)
        start = pl.multiple_of((step % (size // CHUNK)) * CHUNK, CHUNK)
        rows = window(padded, f, start, CHUNK, (0, 1, 2))
        column = columns_of(CHUNK, chans)
        z = [
            jnp.dot(rows, weight[:, j].reshape(3 * chans, chans), preferred_element_type=F32)
            for j in range(3)
        ]
        pre = shifted(z[0], column, 1) + z[1] + shifted(z[2], column, -1)
        sigma = 1.0 / (1.0 + jnp.exp(-pre))
        active = (pre * sigma).astype(BF)
        act[f, pl.ds(start, CHUNK), :] = active
        slope[f, pl.ds(start, CHUNK), :] = sigma * (1.0 + pre * (1.0 - sigma))
        act_t[f, :, pl.ds(start, CHUNK)] = active.T

    for f in range(frames):
        top_t[f] = top[f].T
        bottom_t[f] = bottom[f].T


def early_kernel(dy, weight, act_t, partial, terms):
    frames, size, chans = dy.shape

    @pl.loop(0, size // CHUNK)
    def _(step):
        at = pl.ds(pl.multiple_of(step * CHUNK, CHUNK), CHUNK)
        second = dy[1, at, :]
        both = jnp.concatenate([dy[0, at, :], second], axis=1)
        taps = jnp.concatenate([weight[0], weight[1]], axis=1)
        partial[0, at, :] = lax.dot_general(both, taps, NT, preferred_element_type=F32)
        partial[1, at, :] = lax.dot_general(second, weight[0], NT, preferred_element_type=F32)

    left = jnp.concatenate([act_t[0], act_t[1]], axis=1)
    right = dy[...].reshape(frames * size, chans)
    terms[0] = jnp.dot(left, right, preferred_element_type=F32)
    terms[1] = jnp.dot(act_t[0], dy[1], preferred_element_type=F32)


def finish(f, start, agrad, slope, wide):
    at = pl.ds(start, CHUNK)
    grad = (agrad.astype(BF).astype(F32) * slope[f, at, :]).astype(BF)
    full = grad.astype(F32)
    column = columns_of(CHUNK, full.shape[1])
    into = pl.ds(f * slope.shape[1] + start, CHUNK)
    wide[0, into, :] = shifted(full, column, -1).astype(BF)
    wide[1, into, :] = grad
    wide[2, into, :] = shifted(full, column, 1).astype(BF)


def windows_of(x_t, top_t, bottom_t, f, size):
    above = jnp.concatenate([top_t[f], x_t[f, :, : size - COLS]], axis=1)
    below = jnp.concatenate([x_t[f, :, COLS:], bottom_t[f]], axis=1)
    return jnp.concatenate([above, x_t[f], below], axis=0)


def gradient_kernel(
    core,
    ahead,
    weight,
    slope,
    x_t,
    top_t,
    bottom_t,
    act_t,
    partial,
    early,
    pgrad,
    keep,
    last,
    first,
    *rest,
):
    *sends, wide, terms, sems = rest
    frames, size, chans = ahead.shape

    @pl.loop(0, size // CHUNK)
    def _(step):
        start = pl.multiple_of(step * CHUNK, CHUNK)
        at = pl.ds(start, CHUNK)
        block = ahead[0, at, :]
        more = lax.dot_general(block, weight[2], NT, preferred_element_type=F32)
        finish(0, start, partial[0, at, :] + more, slope, wide)
        both = jnp.concatenate([block, ahead[1, at, :]], axis=1)
        taps = jnp.concatenate([weight[1], weight[2]], axis=1)
        more = lax.dot_general(both, taps, NT, preferred_element_type=F32)
        finish(1, start, partial[1, at, :] + more, slope, wide)

    stores = []
    for f in range(frames):
        rows = pl.ds(f * size, size)
        stores.append(pltpu.make_async_copy(wide.at[1, rows], pgrad.at[f], sems.at[f]))
        stores[f].start()
        last[f] = wide[1, (f + 1) * size - COLS : (f + 1) * size, :]
        first[f] = wide[1, f * size : f * size + COLS, :]

    def put(tap, value):
        for h in range(2):
            at = (tap * 2 + h) * chans
            terms[at : at + chans, :] = value[:, h * 128 : (h + 1) * 128].astype(BF)

    left = jnp.concatenate([windows_of(x_t, top_t, bottom_t, f, size) for f in range(frames)], axis=1)
    for j in range(3):
        out = jnp.dot(left, wide[j], preferred_element_type=F32)
        for i in range(3):
            put(3 * i + j, out[i * chans : (i + 1) * chans])
    put(9, early[0])
    put(10, early[1] + jnp.dot(act_t[1], ahead[0], preferred_element_type=F32))
    left_t = jnp.concatenate([act_t[0], act_t[1]], axis=1)
    right = ahead[...].reshape(frames * size, chans)
    put(11, jnp.dot(left_t, right, preferred_element_type=F32))
    half = terms.shape[0] // 2
    for c in range(2):

        @pl.when(core[0] == c)
        def _():
            keep[...] = terms[c * half : (c + 1) * half, :]
            cut = sends[0].shape[0]
            for n, send in enumerate(sends):
                at = (1 - c) * half + n * cut
                send[...] = terms[at : at + cut, :]

    for store in stores:
        store.wait()


def add_kernel(a, *refs):
    out = refs[-1]
    cut = refs[0].shape[0]
    for n, b in enumerate(refs[:-1]):
        rows = pl.ds(n * cut, cut)
        out[rows, :] = (a[rows, :].astype(F32) + b[...].astype(F32)).astype(BF)


def sum_kernel(parts, out):
    total = parts[0].astype(F32)
    for i in range(1, parts.shape[0]):
        total = total + parts[i].astype(F32)
    out[...] = total.astype(out.dtype)


def spread_sum_kernel(scale, parts, out, sent, sems):
    total = parts[0].astype(F32)
    for i in range(1, parts.shape[0]):
        total = total + parts[i].astype(F32)
    sent[...] = (total * scale).astype(sent.dtype)
    copies = [
        pltpu.make_async_copy(sent, out.at[i], sems.at[i]) for i in range(out.shape[0])
    ]
    for copy in copies:
        copy.start()
    for copy in copies:
        copy.wait()


def write_half(first, source, spatial, temporal, wide, sems):
    copies = []
    for n in range(6):
        t = n if first else n + 6
        for h in range(2):
            at = (n * 2 + h) * 256
            wide[n, :, h * 128 : (h + 1) * 128] = source[at : at + 256, :].astype(F32)
        target = spatial.at[t] if t < 9 else temporal.at[t - 9]
        copy = pltpu.make_async_copy(wide.at[n], target, sems.at[n])
        copy.start()
        copies.append(copy)
    for copy in copies:
        copy.wait()


def own_kernel(core, own, spatial, temporal, wide, sems):
    for c in range(2):

        @pl.when(core[0] == c)
        def _():
            write_half(c == 0, own, spatial, temporal, wide, sems)


def other_kernel(core, other, spatial_in, temporal_in, spatial, temporal, wide, sems):
    for c in range(2):

        @pl.when(core[0] == c)
        def _():
            write_half(c == 1, other, spatial, temporal, wide, sems)


def back_taps(taps, j):
    return jnp.concatenate([taps[i, j] for i in range(3)], axis=1)


def back_kernel(grad, weight, dy, out, edge, padded, taps, own, result, sems):
    frames, size, chans = own.shape
    whole = pltpu.make_async_copy(weight, taps, sems.at[0])
    whole.start()
    loads = []
    for f in range(frames):
        base = 1 + 3 * f
        loads.append(
            [
                pltpu.make_async_copy(
                    grad.at[f], padded.at[f, pl.ds(COLS, size)], sems.at[base]
                ),
                pltpu.make_async_copy(dy.at[f], own.at[f], sems.at[base + 1]),
            ]
        )
        for load in loads[f]:
            load.start()
        blank = jnp.zeros((COLS, chans), BF)
        padded[f, 0:COLS, :] = blank
        padded[f, COLS + size :, :] = blank
    whole.wait()
    stores = []
    for f in range(frames):
        for load in loads[f]:
            load.wait()

        @pl.loop(0, size // CHUNK)
        def _(step):
            start = pl.multiple_of(step * CHUNK, CHUNK)
            at = pl.ds(start, CHUNK)
            rows = window(padded, f, start, CHUNK, (2, 1, 0))
            column = columns_of(CHUNK, chans)
            z = [
                lax.dot_general(rows, back_taps(taps, j), NT, preferred_element_type=F32)
                for j in range(3)
            ]
            back = shifted(z[0], column, -1) + z[1] + shifted(z[2], column, 1)
            total = own[f, at, :].astype(F32) + back
            result[f, at, :] = total.astype(BF)

            @pl.when(step == 0)
            def _():
                edge[f, 0] = total[:COLS]

            @pl.when(step == size // CHUNK - 1)
            def _():
                edge[f, 1] = total[CHUNK - COLS :]

        store = pltpu.make_async_copy(result.at[f], out.at[f], sems.at[3 + 3 * f])
        store.start()
        stores.append(store)
    for store in stores:
        store.wait()


def edge_kernel(top, bottom, weight, edge, part, out, result, sems):
    frames, size = part.shape[0], part.shape[1]
    chans = part.shape[2]
    column = columns_of(frames * COLS, chans)
    stores = []
    for e, (rim, i) in enumerate(((top, 2), (bottom, 0))):
        rows = rim[...].reshape(frames * COLS, chans)
        z = [
            lax.dot_general(rows, weight[i, j], NT, preferred_element_type=F32) for j in range(3)
        ]
        more = shifted(z[0], column, -1) + z[1] + shifted(z[2], column, 1)
        for f in range(frames):
            total = edge[f, e] + more[f * COLS : (f + 1) * COLS]
            result[f, e] = total.astype(BF)
            target = out.at[f, pl.ds(e * (size - COLS), COLS)]
            store = pltpu.make_async_copy(result.at[f, e], target, sems.at[2 * f + e])
            store.start()
            stores.append(store)
    for store in stores:
        store.wait()


def mix_kernel(act, behind, weight, x, out, ext, own, result, sems):
    frames, size, chans = own.shape
    loads = [pltpu.make_async_copy(behind.at[f], ext.at[f], sems.at[f]) for f in range(frames)]
    for f in range(frames):
        loads.append(pltpu.make_async_copy(act.at[f], ext.at[frames + f], sems.at[frames + 2 * f]))
        loads.append(pltpu.make_async_copy(x.at[f], own.at[f], sems.at[frames + 2 * f + 1]))
    for load in loads:
        load.start()
    for load in loads[:frames]:
        load.wait()
    stores = []
    for f in range(frames):
        for load in loads[frames + 2 * f : frames + 2 * f + 2]:
            load.wait()
        rows = jnp.concatenate([ext[f + 2 - k] for k in range(3)], axis=1)
        taps = weight[...].reshape(3 * chans, chans)
        mixed = jnp.dot(rows, taps, preferred_element_type=F32).astype(BF)
        result[f] = (own[f].astype(F32) + mixed.astype(F32)).astype(BF)
        store = pltpu.make_async_copy(result.at[f], out.at[f], sems.at[3 * frames + f])
        store.start()
        stores.append(store)
    for store in stores:
        store.wait()


def steps(axes, by):
    count = lax.axis_size(axes)
    return [(i, i + by) for i in range(count) if 0 <= i + by < count]


def exchange(value, axes):
    return lax.all_to_all(value, axes, split_axis=0, concat_axis=0, tiled=True)


def swap_rims(last, first):
    return lax.ppermute(last, SPACE, steps(SPACE, 1)), lax.ppermute(first, SPACE, steps(SPACE, -1))


def local(scale, frames_in, cotangent, spatial_weight, temporal_weight):
    dims = frames_in.shape
    frames, chans = dims[1], dims[4]
    size = dims[2] * dims[3]
    x = frames_in.reshape(frames, size, chans)
    dy = cotangent.reshape(frames, size, chans)
    work = 2 * frames * size * chans * chans
    core = lax.axis_index("core").astype(jnp.int32).reshape(1)
    ahead = lax.ppermute(dy, TM, steps(TM, -1))
    top, bottom = swap_rims(x[:, size - COLS :, :], x[:, :COLS, :])
    x_t = call(
        turn_kernel,
        shape((frames, chans, size)),
        (x, spatial_weight),
        flops=1 << 20,
        moved=2 << 20,
    )
    act, slope, top_t, bottom_t, act_t = call(
        forward_kernel,
        [
            shape((frames, size, chans)),
            shape((frames, size, chans), F32),
            shape((frames, chans, COLS)),
            shape((frames, chans, COLS)),
            shape((frames, chans, size)),
        ],
        (x, top, bottom, spatial_weight),
        [pltpu.VMEM((frames, size + 2 * COLS, chans), BF)],
        flops=9 * work,
        moved=9 << 20,
    )
    partial, early = call(
        early_kernel,
        [shape((frames, size, chans), F32), shape((2, chans, chans), F32)],
        (dy, temporal_weight, act_t),
        flops=6 * work,
        moved=6 << 20,
    )
    behind = lax.ppermute(act, TM, steps(TM, 1))
    flat = frames * size
    rows = 12 * chans
    edges = shape((frames, COLS, chans))
    pgrad, keep, last, first, *send = call(
        gradient_kernel,
        [shape((frames, size, chans)), shape((rows, 128)), edges, edges]
        + [shape((rows // SWAPS, 128))] * SWAPS,
        (
            core,
            ahead,
            temporal_weight,
            slope,
            x_t,
            top_t,
            bottom_t,
            act_t,
            partial,
            early,
        ),
        [
            pltpu.VMEM((3, flat, chans), BF),
            pltpu.VMEM((2 * rows, 128), BF),
            pltpu.SemaphoreType.DMA((frames,)),
        ],
        flops=1 << 10,
        moved=1 << 12,
        smem=(0,),
        out_hbm=(0,),
    )
    grad_top, grad_bottom = swap_rims(last, first)
    pair = [(0, 1), (1, 0)]
    got = [lax.ppermute(part, "core", pair) for part in send]
    half = call(add_kernel, shape((rows, 128)), (keep, *got), moved=1 << 12)
    block = pltpu.VMEM((frames, size, chans), BF)
    column, plane = lax.axis_size(COLUMN), lax.axis_size(PLANE)
    share = rows // plane
    first = exchange(half.reshape(plane, share, 128), PLANE)
    inner, edge = call(
        back_kernel,
        [shape((frames, size, chans)), shape((frames, 2, COLS, chans), F32)],
        (pgrad, spatial_weight, dy),
        [
            pltpu.VMEM((frames, size + 2 * COLS, chans), BF),
            pltpu.VMEM((3, 3, chans, chans), BF),
            block,
            block,
            pltpu.SemaphoreType.DMA((7,)),
        ],
        flops=9 * work,
        moved=5 << 20,
        hbm=range(3),
        out_hbm=(0,),
        limit=58,
    )
    first, edge = lax.optimization_barrier((first, edge))
    spread = call(
        functools.partial(spread_sum_kernel, 1.0),
        shape((column, share, 128)),
        (first,),
        [pltpu.VMEM((share, 128), BF), pltpu.SemaphoreType.DMA((column,))],
        moved=1 << 12,
        out_hbm=(0,),
        after=(behind,),
    )
    third = exchange(spread, COLUMN)
    block_out = call(
        mix_kernel,
        shape((frames, size, chans)),
        (act, behind, temporal_weight, x),
        [
            pltpu.VMEM((2 * frames, size, chans), BF),
            block,
            block,
            pltpu.SemaphoreType.DMA((4 * frames,)),
        ],
        flops=3 * work,
        moved=4 << 20,
        hbm=(0, 1, 3),
        out_hbm=True,
        limit=58,
    )
    third, grad_top, grad_bottom = lax.optimization_barrier((third, grad_top, grad_bottom))
    input_grad = call(
        edge_kernel,
        shape((frames, size, chans)),
        (grad_top, grad_bottom, spatial_weight, edge, inner),
        [pltpu.VMEM((frames, 2, COLS, chans), BF), pltpu.SemaphoreType.DMA((2 * frames,))],
        flops=work,
        moved=1 << 20,
        hbm=(4,),
        out_hbm=True,
        alias={4: 0},
    )
    wider = call(
        functools.partial(spread_sum_kernel, scale),
        shape((plane, share, 128)),
        (third,),
        [pltpu.VMEM((share, 128), BF), pltpu.SemaphoreType.DMA((plane,))],
        moved=1 << 12,
        out_hbm=(0,),
    )
    own = exchange(wider, PLANE).reshape(rows, 128)
    own, block_out, input_grad = lax.optimization_barrier((own, block_out, input_grad))
    other = lax.ppermute(own, "core", pair)
    grads = [shape((9, chans, chans), F32), shape((3, chans, chans), F32)]
    room = [pltpu.VMEM((6, chans, chans), F32), pltpu.SemaphoreType.DMA((6,))]
    spatial, temporal = call(
        own_kernel, grads, (core, own), room, moved=3 << 20, smem=(0,), out_hbm=True
    )
    spatial, temporal = call(
        other_kernel,
        grads,
        (core, other, spatial, temporal),
        room,
        moved=3 << 20,
        smem=(0,),
        hbm=(2, 3),
        out_hbm=True,
        alias={2: 0, 3: 1},
    )
    return (
        block_out.reshape(dims),
        input_grad.reshape(dims),
        spatial.reshape(3, 3, chans, chans),
        temporal,
    )


def solution(mesh):
    fine = Mesh(mesh.devices.reshape(2, 4, 4, 4, 2), ("clip", "y", "zl", "x", "core"))
    blocks = P("clip", TM, SPACE, None, None)

    def run(frames_in, cotangent, spatial_weight, temporal_weight):
        clips, frames, height, width, _ = frames_in.shape
        scale = (clips * frames * height * width) ** -0.5
        return jax.shard_map(
            functools.partial(local, scale),
            mesh=fine,
            in_specs=(blocks, blocks, P(), P()),
            out_specs=(blocks, blocks, P(), P()),
            check_vma=False,
        )(frames_in, cotangent, spatial_weight, temporal_weight)

    return run
```

```python
import functools

import jax
import jax.numpy as jnp
from jax import lax
from jax.experimental import pallas as pl
from jax.experimental.pallas import tpu as pltpu
from jax.sharding import Mesh, PartitionSpec as P

BF = jnp.bfloat16
F32 = jnp.float32
TM = ("y", "zl")
SPACE = ("x", "core")
COLUMN = ("clip", "zl")
COLS = 128
NT = (((1,), (1,)), ((), ()))


def call(kernel, outs, ins, scratch=(), flops=0, moved=0, limit=20, smem=(), after=(), hbm=(), out_hbm=False, alias=None):
    vmem = pl.BlockSpec(memory_space=pltpu.VMEM)
    specs = [pl.BlockSpec(memory_space=pltpu.SMEM) if i in smem else vmem for i in range(len(ins))]
    specs = [pl.BlockSpec(memory_space=pl.ANY) if i in hbm else p for i, p in enumerate(specs)]
    specs += [pl.BlockSpec(memory_space=pltpu.HBM)] * len(after)
    many = isinstance(outs, list)
    placed = [
        pl.BlockSpec(memory_space=pltpu.HBM) if out_hbm is True or i in (out_hbm or ()) else vmem
        for i in range(len(outs) if many else 1)
    ]
    count = len(ins)

    def body(*refs):
        kernel(*refs[:count], *refs[count + len(after) :])

    return pl.pallas_call(
        body,
        out_shape=outs,
        in_specs=specs,
        out_specs=placed if many else placed[0],
        input_output_aliases=alias or {},
        scratch_shapes=list(scratch),
        cost_estimate=pl.CostEstimate(flops=flops, bytes_accessed=moved, transcendentals=0),
        compiler_params=pltpu.CompilerParams(vmem_limit_bytes=limit << 20),
    )(*ins, *after)


def shape(dims, kind=BF):
    return jax.ShapeDtypeStruct(dims, kind)


def shifted(value, column, step):
    edge = 0 if step == 1 else COLS - 1
    rolled = pltpu.roll(value, step % value.shape[0], 0)
    return jnp.where(column == edge, 0.0, rolled)


def columns_of(rows, width):
    return lax.broadcasted_iota(jnp.int32, (rows, width), 0) % COLS


def window(ref, frame, start, rows, offsets):
    parts = [ref[frame, pl.ds(start + off * COLS, rows), :] for off in offsets]
    return jnp.concatenate(parts, axis=1)


CHUNK = 512
SWAPS = 4


def fill(padded, block, top, bottom, frame):
    size = block.shape[1]
    padded[frame, 0:COLS, :] = top[frame]
    padded[frame, COLS : COLS + size, :] = block[frame]
    padded[frame, COLS + size :, :] = bottom[frame]


def turn_kernel(x, x_t):
    for f in range(x.shape[0]):
        x_t[f] = x[f].T


def forward_kernel(x, top, bottom, weight, act, slope, top_t, bottom_t, act_t, padded):
    frames, size, chans = x.shape
    for f in range(frames):
        fill(padded, x, top, bottom, f)

    @pl.loop(0, frames * (size // CHUNK))
    def _(step):
        f = step // (size // CHUNK)
        start = pl.multiple_of((step % (size // CHUNK)) * CHUNK, CHUNK)
        rows = window(padded, f, start, CHUNK, (0, 1, 2))
        column = columns_of(CHUNK, chans)
        z = [
            jnp.dot(rows, weight[:, j].reshape(3 * chans, chans), preferred_element_type=F32)
            for j in range(3)
        ]
        pre = shifted(z[0], column, 1) + z[1] + shifted(z[2], column, -1)
        sigma = 1.0 / (1.0 + jnp.exp(-pre))
        active = (pre * sigma).astype(BF)
        act[f, pl.ds(start, CHUNK), :] = active
        slope[f, pl.ds(start, CHUNK), :] = sigma * (1.0 + pre * (1.0 - sigma))
        act_t[f, :, pl.ds(start, CHUNK)] = active.T

    for f in range(frames):
        top_t[f] = top[f].T
        bottom_t[f] = bottom[f].T


def early_kernel(dy, weight, act_t, partial, terms):
    frames, size, chans = dy.shape

    @pl.loop(0, size // CHUNK)
    def _(step):
        at = pl.ds(pl.multiple_of(step * CHUNK, CHUNK), CHUNK)
        second = dy[1, at, :]
        both = jnp.concatenate([dy[0, at, :], second], axis=1)
        taps = jnp.concatenate([weight[0], weight[1]], axis=1)
        partial[0, at, :] = lax.dot_general(both, taps, NT, preferred_element_type=F32)
        partial[1, at, :] = lax.dot_general(second, weight[0], NT, preferred_element_type=F32)

    left = jnp.concatenate([act_t[0], act_t[1]], axis=1)
    right = dy[...].reshape(frames * size, chans)
    terms[0] = jnp.dot(left, right, preferred_element_type=F32)
    terms[1] = jnp.dot(act_t[0], dy[1], preferred_element_type=F32)


def finish(f, start, agrad, slope, wide):
    at = pl.ds(start, CHUNK)
    grad = (agrad.astype(BF).astype(F32) * slope[f, at, :]).astype(BF)
    full = grad.astype(F32)
    column = columns_of(CHUNK, full.shape[1])
    into = pl.ds(f * slope.shape[1] + start, CHUNK)
    wide[0, into, :] = shifted(full, column, -1).astype(BF)
    wide[1, into, :] = grad
    wide[2, into, :] = shifted(full, column, 1).astype(BF)


def windows_of(x_t, top_t, bottom_t, f, size):
    above = jnp.concatenate([top_t[f], x_t[f, :, : size - COLS]], axis=1)
    below = jnp.concatenate([x_t[f, :, COLS:], bottom_t[f]], axis=1)
    return jnp.concatenate([above, x_t[f], below], axis=0)


def gradient_kernel(
    core,
    ahead,
    weight,
    slope,
    x_t,
    top_t,
    bottom_t,
    act_t,
    partial,
    early,
    pgrad,
    keep,
    last,
    first,
    *rest,
):
    *sends, wide, terms, sems = rest
    frames, size, chans = ahead.shape

    @pl.loop(0, size // CHUNK)
    def _(step):
        start = pl.multiple_of(step * CHUNK, CHUNK)
        at = pl.ds(start, CHUNK)
        block = ahead[0, at, :]
        more = lax.dot_general(block, weight[2], NT, preferred_element_type=F32)
        finish(0, start, partial[0, at, :] + more, slope, wide)
        both = jnp.concatenate([block, ahead[1, at, :]], axis=1)
        taps = jnp.concatenate([weight[1], weight[2]], axis=1)
        more = lax.dot_general(both, taps, NT, preferred_element_type=F32)
        finish(1, start, partial[1, at, :] + more, slope, wide)

    stores = []
    for f in range(frames):
        rows = pl.ds(f * size, size)
        stores.append(pltpu.make_async_copy(wide.at[1, rows], pgrad.at[f], sems.at[f]))
        stores[f].start()
        last[f] = wide[1, (f + 1) * size - COLS : (f + 1) * size, :]
        first[f] = wide[1, f * size : f * size + COLS, :]

    def put(tap, value):
        for h in range(2):
            at = (tap * 2 + h) * chans
            terms[at : at + chans, :] = value[:, h * 128 : (h + 1) * 128].astype(BF)

    left = jnp.concatenate([windows_of(x_t, top_t, bottom_t, f, size) for f in range(frames)], axis=1)
    for j in range(3):
        out = jnp.dot(left, wide[j], preferred_element_type=F32)
        for i in range(3):
            put(3 * i + j, out[i * chans : (i + 1) * chans])
    put(9, early[0])
    put(10, early[1] + jnp.dot(act_t[1], ahead[0], preferred_element_type=F32))
    left_t = jnp.concatenate([act_t[0], act_t[1]], axis=1)
    right = ahead[...].reshape(frames * size, chans)
    put(11, jnp.dot(left_t, right, preferred_element_type=F32))
    half = terms.shape[0] // 2
    for c in range(2):

        @pl.when(core[0] == c)
        def _():
            keep[...] = terms[c * half : (c + 1) * half, :]
            cut = sends[0].shape[0]
            for n, send in enumerate(sends):
                at = (1 - c) * half + n * cut
                send[...] = terms[at : at + cut, :]

    for store in stores:
        store.wait()


def deal(place, total, own, outs):
    size = own.shape[0]
    count = len(outs) + 1
    for d in range(count):
        at = pl.multiple_of(lax.rem(place[0] + d, count) * size, size)
        block = total[pl.ds(at, size), :]
        if d:
            outs[d - 1][...] = block.astype(BF)
        else:
            own[...] = block


def add_kernel(place, a, *refs):
    parts, (own, *outs), total = refs[:SWAPS], refs[SWAPS:-1], refs[-1]
    cut = parts[0].shape[0]
    for n, b in enumerate(parts):
        rows = pl.ds(n * cut, cut)
        total[rows, :] = a[rows, :].astype(F32) + b[...].astype(F32)
    deal(place, total, own, outs)


def sum_deal_kernel(place, a, b, c, d, own, *refs):
    outs, total = refs[:-1], refs[-1]
    total[...] = a[...] + b[...].astype(F32) + c[...].astype(F32) + d[...].astype(F32)
    deal(place, total, own, outs)


def sum_spread_kernel(a, b, c, d, out):
    total = a[...] + b[...].astype(F32) + c[...].astype(F32) + d[...].astype(F32)
    total = total.astype(BF)
    for i in range(out.shape[0]):
        out[i] = total


def sum_kernel(scale, parts, out):
    total = parts[0].astype(F32)
    for i in range(1, parts.shape[0]):
        total = total + parts[i].astype(F32)
    out[...] = (total * scale).astype(out.dtype)


def collect_kernel(place, *refs):
    blocks, out = refs[:-1], refs[-1]
    size = blocks[0].shape[0]
    count = len(blocks)
    for d, block in enumerate(blocks):
        at = pl.multiple_of(lax.rem(place[0] + count - d, count) * size, size)
        out[pl.ds(at, size), :] = block[...]


def write_half(first, source, spatial, temporal, wide, sems):
    copies = []
    for n in range(6):
        t = n if first else n + 6
        for h in range(2):
            at = (n * 2 + h) * 256
            wide[n, :, h * 128 : (h + 1) * 128] = source[at : at + 256, :].astype(F32)
        target = spatial.at[t] if t < 9 else temporal.at[t - 9]
        copy = pltpu.make_async_copy(wide.at[n], target, sems.at[n])
        copy.start()
        copies.append(copy)
    for copy in copies:
        copy.wait()


def own_kernel(core, own, spatial, temporal, wide, sems):
    for c in range(2):

        @pl.when(core[0] == c)
        def _():
            write_half(c == 0, own, spatial, temporal, wide, sems)


def other_kernel(core, other, spatial_in, temporal_in, spatial, temporal, wide, sems):
    for c in range(2):

        @pl.when(core[0] == c)
        def _():
            write_half(c == 1, other, spatial, temporal, wide, sems)


def back_taps(taps, j):
    return jnp.concatenate([taps[i, j] for i in range(3)], axis=1)


def back_kernel(grad, weight, dy, out, edge, padded, taps, own, result, sems):
    frames, size, chans = own.shape
    whole = pltpu.make_async_copy(weight, taps, sems.at[0])
    whole.start()
    loads = []
    for f in range(frames):
        base = 1 + 3 * f
        loads.append(
            [
                pltpu.make_async_copy(
                    grad.at[f], padded.at[f, pl.ds(COLS, size)], sems.at[base]
                ),
                pltpu.make_async_copy(dy.at[f], own.at[f], sems.at[base + 1]),
            ]
        )
        for load in loads[f]:
            load.start()
        blank = jnp.zeros((COLS, chans), BF)
        padded[f, 0:COLS, :] = blank
        padded[f, COLS + size :, :] = blank
    whole.wait()
    stores = []
    for f in range(frames):
        for load in loads[f]:
            load.wait()

        @pl.loop(0, size // CHUNK)
        def _(step):
            start = pl.multiple_of(step * CHUNK, CHUNK)
            at = pl.ds(start, CHUNK)
            rows = window(padded, f, start, CHUNK, (2, 1, 0))
            column = columns_of(CHUNK, chans)
            z = [
                lax.dot_general(rows, back_taps(taps, j), NT, preferred_element_type=F32)
                for j in range(3)
            ]
            back = shifted(z[0], column, -1) + z[1] + shifted(z[2], column, 1)
            total = own[f, at, :].astype(F32) + back
            result[f, at, :] = total.astype(BF)

            @pl.when(step == 0)
            def _():
                edge[f, 0] = total[:COLS]

            @pl.when(step == size // CHUNK - 1)
            def _():
                edge[f, 1] = total[CHUNK - COLS :]

        store = pltpu.make_async_copy(result.at[f], out.at[f], sems.at[3 + 3 * f])
        store.start()
        stores.append(store)
    for store in stores:
        store.wait()


def edge_kernel(top, bottom, weight, edge, part, out, result, sems):
    frames, size = part.shape[0], part.shape[1]
    chans = part.shape[2]
    column = columns_of(frames * COLS, chans)
    stores = []
    for e, (rim, i) in enumerate(((top, 2), (bottom, 0))):
        rows = rim[...].reshape(frames * COLS, chans)
        z = [
            lax.dot_general(rows, weight[i, j], NT, preferred_element_type=F32) for j in range(3)
        ]
        more = shifted(z[0], column, -1) + z[1] + shifted(z[2], column, 1)
        for f in range(frames):
            total = edge[f, e] + more[f * COLS : (f + 1) * COLS]
            result[f, e] = total.astype(BF)
            target = out.at[f, pl.ds(e * (size - COLS), COLS)]
            store = pltpu.make_async_copy(result.at[f, e], target, sems.at[2 * f + e])
            store.start()
            stores.append(store)
    for store in stores:
        store.wait()


def mix_kernel(act, behind, weight, x, out, ext, own, result, sems):
    frames, size, chans = own.shape
    loads = [pltpu.make_async_copy(behind.at[f], ext.at[f], sems.at[f]) for f in range(frames)]
    for f in range(frames):
        loads.append(pltpu.make_async_copy(act.at[f], ext.at[frames + f], sems.at[frames + 2 * f]))
        loads.append(pltpu.make_async_copy(x.at[f], own.at[f], sems.at[frames + 2 * f + 1]))
    for load in loads:
        load.start()
    for load in loads[:frames]:
        load.wait()
    stores = []
    for f in range(frames):
        for load in loads[frames + 2 * f : frames + 2 * f + 2]:
            load.wait()
        rows = jnp.concatenate([ext[f + 2 - k] for k in range(3)], axis=1)
        taps = weight[...].reshape(3 * chans, chans)
        mixed = jnp.dot(rows, taps, preferred_element_type=F32).astype(BF)
        result[f] = (own[f].astype(F32) + mixed.astype(F32)).astype(BF)
        store = pltpu.make_async_copy(result.at[f], out.at[f], sems.at[3 * frames + f])
        store.start()
        stores.append(store)
    for store in stores:
        store.wait()


def steps(axes, by):
    count = lax.axis_size(axes)
    return [(i, i + by) for i in range(count) if 0 <= i + by < count]


def ring(value, axis):
    count = lax.axis_size(axis)
    values = value if isinstance(value, list) else [value] * (count - 1)
    return [
        lax.ppermute(part, axis, [(i, (i + d) % count) for i in range(count)])
        for d, part in enumerate(values, 1)
    ]


def exchange(value, axes):
    return lax.all_to_all(value, axes, split_axis=0, concat_axis=0, tiled=True)


def swap_rims(last, first):
    return lax.ppermute(last, SPACE, steps(SPACE, 1)), lax.ppermute(first, SPACE, steps(SPACE, -1))


def local(scale, frames_in, cotangent, spatial_weight, temporal_weight):
    dims = frames_in.shape
    frames, chans = dims[1], dims[4]
    size = dims[2] * dims[3]
    x = frames_in.reshape(frames, size, chans)
    dy = cotangent.reshape(frames, size, chans)
    work = 2 * frames * size * chans * chans
    core = lax.axis_index("core").astype(jnp.int32).reshape(1)
    ahead = lax.ppermute(dy, TM, steps(TM, -1))
    top, bottom = swap_rims(x[:, size - COLS :, :], x[:, :COLS, :])
    x_t = call(turn_kernel, shape((frames, chans, size)), (x,), flops=1 << 20, moved=2 << 20)
    act, slope, top_t, bottom_t, act_t = call(
        forward_kernel,
        [
            shape((frames, size, chans)),
            shape((frames, size, chans), F32),
            shape((frames, chans, COLS)),
            shape((frames, chans, COLS)),
            shape((frames, chans, size)),
        ],
        (x, top, bottom, spatial_weight),
        [pltpu.VMEM((frames, size + 2 * COLS, chans), BF)],
        flops=9 * work,
        moved=9 << 20,
    )
    partial, early = call(
        early_kernel,
        [shape((frames, size, chans), F32), shape((2, chans, chans), F32)],
        (dy, temporal_weight, act_t),
        flops=6 * work,
        moved=6 << 20,
    )
    behind = lax.ppermute(act, TM, steps(TM, 1))
    flat = frames * size
    rows = 12 * chans
    edges = shape((frames, COLS, chans))
    pgrad, keep, last, first, *send = call(
        gradient_kernel,
        [shape((frames, size, chans)), shape((rows, 128)), edges, edges]
        + [shape((rows // SWAPS, 128))] * SWAPS,
        (
            core,
            ahead,
            temporal_weight,
            slope,
            x_t,
            top_t,
            bottom_t,
            act_t,
            partial,
            early,
        ),
        [
            pltpu.VMEM((3, flat, chans), BF),
            pltpu.VMEM((2 * rows, 128), BF),
            pltpu.SemaphoreType.DMA((frames,)),
        ],
        flops=1 << 10,
        moved=1 << 12,
        smem=(0,),
        out_hbm=(0,),
    )
    grad_top, grad_bottom = swap_rims(last, first)
    pair = [(0, 1), (1, 0)]
    got = [lax.ppermute(part, "core", pair) for part in send]
    at_x = lax.axis_index("x").astype(jnp.int32).reshape(1)
    at_y = lax.axis_index("y").astype(jnp.int32).reshape(1)
    block = pltpu.VMEM((frames, size, chans), BF)
    column = lax.axis_size(COLUMN)
    quarter = rows // lax.axis_size("x")
    share = quarter // lax.axis_size("y")
    dealt = [shape((quarter, 128), F32)] + [shape((quarter, 128))] * 3
    own, *out = call(
        add_kernel, dealt, (at_x, keep, *got), [pltpu.VMEM((rows, 128), F32)], moved=1 << 12, smem=(0,)
    )
    first = ring(out, "x")
    inner, edge = call(
        back_kernel,
        [shape((frames, size, chans)), shape((frames, 2, COLS, chans), F32)],
        (pgrad, spatial_weight, dy),
        [
            pltpu.VMEM((frames, size + 2 * COLS, chans), BF),
            pltpu.VMEM((3, 3, chans, chans), BF),
            block,
            block,
            pltpu.SemaphoreType.DMA((7,)),
        ],
        flops=1 << 10,
        moved=1 << 12,
        hbm=range(3),
        out_hbm=(0,),
        limit=58,
    )
    first[0], edge = lax.optimization_barrier((first[0], edge))
    dealt = [shape((share, 128), F32)] + [shape((share, 128))] * 3
    own, *out = call(
        sum_deal_kernel,
        dealt,
        (at_y, own, *first),
        [pltpu.VMEM((quarter, 128), F32)],
        moved=1 << 12,
        smem=(0,),
    )
    second = ring(out, "y")
    second[0], grad_top, grad_bottom = lax.optimization_barrier((second[0], grad_top, grad_bottom))
    spread = call(
        sum_spread_kernel,
        shape((column, share, 128)),
        (own, *second),
        moved=1 << 12,
        after=(behind,),
    )
    third = exchange(spread, COLUMN)
    total = call(functools.partial(sum_kernel, scale), shape((share, 128)), (third,), moved=1 << 12)
    fourth = ring(total, "y")
    wider = call(
        collect_kernel, shape((quarter, 128)), (at_y, total, *fourth), moved=1 << 12, smem=(0,)
    )
    fifth = ring(wider, "x")
    block_out = call(
        mix_kernel,
        shape((frames, size, chans)),
        (act, behind, temporal_weight, x),
        [
            pltpu.VMEM((2 * frames, size, chans), BF),
            block,
            block,
            pltpu.SemaphoreType.DMA((4 * frames,)),
        ],
        flops=3 * work,
        moved=4 << 20,
        hbm=(0, 1, 3),
        out_hbm=True,
        limit=58,
    )
    input_grad = call(
        edge_kernel,
        shape((frames, size, chans)),
        (grad_top, grad_bottom, spatial_weight, edge, inner),
        [pltpu.VMEM((frames, 2, COLS, chans), BF), pltpu.SemaphoreType.DMA((2 * frames,))],
        flops=work,
        moved=1 << 20,
        hbm=(4,),
        out_hbm=True,
        alias={4: 0},
    )
    fifth[0], block_out, input_grad = lax.optimization_barrier((fifth[0], block_out, input_grad))
    own = call(
        collect_kernel, shape((rows, 128)), (at_x, wider, *fifth), moved=1 << 12, smem=(0,)
    )
    other = lax.ppermute(own, "core", pair)
    grads = [shape((9, chans, chans), F32), shape((3, chans, chans), F32)]
    room = [pltpu.VMEM((6, chans, chans), F32), pltpu.SemaphoreType.DMA((6,))]
    spatial, temporal = call(
        own_kernel, grads, (core, own), room, moved=3 << 20, smem=(0,), out_hbm=True
    )
    spatial, temporal = call(
        other_kernel,
        grads,
        (core, other, spatial, temporal),
        room,
        moved=3 << 20,
        smem=(0,),
        hbm=(2, 3),
        out_hbm=True,
        alias={2: 0, 3: 1},
    )
    return (
        block_out.reshape(dims),
        input_grad.reshape(dims),
        spatial.reshape(3, 3, chans, chans),
        temporal,
    )


def solution(mesh):
    fine = Mesh(mesh.devices.reshape(2, 4, 4, 4, 2), ("clip", "y", "zl", "x", "core"))
    blocks = P("clip", TM, SPACE, None, None)

    def run(frames_in, cotangent, spatial_weight, temporal_weight):
        clips, frames, height, width, _ = frames_in.shape
        scale = (clips * frames * height * width) ** -0.5
        return jax.shard_map(
            functools.partial(local, scale),
            mesh=fine,
            in_specs=(blocks, blocks, P(), P()),
            out_specs=(blocks, blocks, P(), P()),
            check_vma=False,
        )(frames_in, cotangent, spatial_weight, temporal_weight)

    return run
```

```python
import functools

import jax
import jax.numpy as jnp
from jax import lax
from jax.experimental import pallas as pl
from jax.experimental.pallas import tpu as pltpu
from jax.sharding import Mesh, PartitionSpec as P

BF = jnp.bfloat16
F32 = jnp.float32
TM = ("y", "zl")
SPACE = ("x", "core")
PLANE = ("x", "y")
COLUMN = ("clip", "zl")
COLS = 128
NT = (((1,), (1,)), ((), ()))


def call(kernel, outs, ins, scratch=(), flops=0, moved=0, limit=20, smem=(), after=(), hbm=(), out_hbm=False, alias=None):
    vmem = pl.BlockSpec(memory_space=pltpu.VMEM)
    specs = [pl.BlockSpec(memory_space=pltpu.SMEM) if i in smem else vmem for i in range(len(ins))]
    specs = [pl.BlockSpec(memory_space=pl.ANY) if i in hbm else p for i, p in enumerate(specs)]
    specs += [pl.BlockSpec(memory_space=pltpu.HBM)] * len(after)
    many = isinstance(outs, list)
    placed = [
        pl.BlockSpec(memory_space=pltpu.HBM) if out_hbm is True or i in (out_hbm or ()) else vmem
        for i in range(len(outs) if many else 1)
    ]
    count = len(ins)

    def body(*refs):
        kernel(*refs[:count], *refs[count + len(after) :])

    return pl.pallas_call(
        body,
        out_shape=outs,
        in_specs=specs,
        out_specs=placed if many else placed[0],
        input_output_aliases=alias or {},
        scratch_shapes=list(scratch),
        cost_estimate=pl.CostEstimate(flops=flops, bytes_accessed=moved, transcendentals=0),
        compiler_params=pltpu.CompilerParams(vmem_limit_bytes=limit << 20),
    )(*ins, *after)


def shape(dims, kind=BF):
    return jax.ShapeDtypeStruct(dims, kind)


def shifted(value, column, step):
    edge = 0 if step == 1 else COLS - 1
    rolled = pltpu.roll(value, step % value.shape[0], 0)
    return jnp.where(column == edge, 0.0, rolled)


def columns_of(rows, width):
    return lax.broadcasted_iota(jnp.int32, (rows, width), 0) % COLS


def window(ref, frame, start, rows, offsets):
    parts = [ref[frame, pl.ds(start + off * COLS, rows), :] for off in offsets]
    return jnp.concatenate(parts, axis=1)


CHUNK = 512
SWAPS = 4


def fill(padded, block, top, bottom, frame):
    size = block.shape[1]
    padded[frame, 0:COLS, :] = top[frame]
    padded[frame, COLS : COLS + size, :] = block[frame]
    padded[frame, COLS + size :, :] = bottom[frame]


def forward_kernel(x, top, bottom, weight, act, slope, x_t, act_t, padded):
    frames, size, chans = x.shape
    for f in range(frames):
        fill(padded, x, top, bottom, f)

    @pl.loop(0, frames * (size // CHUNK))
    def _(step):
        f = step // (size // CHUNK)
        start = pl.multiple_of((step % (size // CHUNK)) * CHUNK, CHUNK)
        rows = window(padded, f, start, CHUNK, (0, 1, 2))
        column = columns_of(CHUNK, chans)
        z = [
            jnp.dot(rows, weight[:, j].reshape(3 * chans, chans), preferred_element_type=F32)
            for j in range(3)
        ]
        pre = shifted(z[0], column, 1) + z[1] + shifted(z[2], column, -1)
        sigma = 1.0 / (1.0 + jnp.exp(-pre))
        active = (pre * sigma).astype(BF)
        act[f, pl.ds(start, CHUNK), :] = active
        slope[f, pl.ds(start, CHUNK), :] = sigma * (1.0 + pre * (1.0 - sigma))
        act_t[f, :, pl.ds(start, CHUNK)] = active.T

    for f in range(frames):
        x_t[f] = padded[f].T


def early_kernel(dy, weight, act_t, partial, terms):
    frames, size, chans = dy.shape

    @pl.loop(0, size // CHUNK)
    def _(step):
        at = pl.ds(pl.multiple_of(step * CHUNK, CHUNK), CHUNK)
        second = dy[1, at, :]
        both = jnp.concatenate([dy[0, at, :], second], axis=1)
        taps = jnp.concatenate([weight[0], weight[1]], axis=1)
        partial[0, at, :] = lax.dot_general(both, taps, NT, preferred_element_type=F32)
        partial[1, at, :] = lax.dot_general(second, weight[0], NT, preferred_element_type=F32)

    left = jnp.concatenate([act_t[0], act_t[1]], axis=1)
    right = dy[...].reshape(frames * size, chans)
    terms[0] = jnp.dot(left, right, preferred_element_type=F32)
    terms[1] = jnp.dot(act_t[0], dy[1], preferred_element_type=F32)


def finish(f, start, agrad, slope, wide):
    at = pl.ds(start, CHUNK)
    grad = (agrad.astype(BF).astype(F32) * slope[f, at, :]).astype(BF)
    full = grad.astype(F32)
    column = columns_of(CHUNK, full.shape[1])
    into = pl.ds(f * slope.shape[1] + start, CHUNK)
    wide[0, into, :] = shifted(full, column, -1).astype(BF)
    wide[1, into, :] = grad
    wide[2, into, :] = shifted(full, column, 1).astype(BF)


def windows_of(x_t, f, size):
    return jnp.concatenate([x_t[f, :, i * COLS : i * COLS + size] for i in range(3)], axis=0)


def gradient_kernel(
    core,
    ahead,
    weight,
    slope,
    x_t,
    act_t,
    partial,
    early,
    pgrad,
    keep,
    last,
    first,
    *rest,
):
    *sends, wide, terms, sems = rest
    frames, size, chans = ahead.shape

    @pl.loop(0, size // CHUNK)
    def _(step):
        start = pl.multiple_of(step * CHUNK, CHUNK)
        at = pl.ds(start, CHUNK)
        block = ahead[0, at, :]
        more = lax.dot_general(block, weight[2], NT, preferred_element_type=F32)
        finish(0, start, partial[0, at, :] + more, slope, wide)
        both = jnp.concatenate([block, ahead[1, at, :]], axis=1)
        taps = jnp.concatenate([weight[1], weight[2]], axis=1)
        more = lax.dot_general(both, taps, NT, preferred_element_type=F32)
        finish(1, start, partial[1, at, :] + more, slope, wide)

    stores = []
    for f in range(frames):
        rows = pl.ds(f * size, size)
        stores.append(pltpu.make_async_copy(wide.at[1, rows], pgrad.at[f], sems.at[f]))
        stores[f].start()
        last[f] = wide[1, (f + 1) * size - COLS : (f + 1) * size, :]
        first[f] = wide[1, f * size : f * size + COLS, :]

    def put(tap, value):
        for h in range(2):
            at = (tap * 2 + h) * chans
            terms[at : at + chans, :] = value[:, h * 128 : (h + 1) * 128].astype(BF)

    left = jnp.concatenate([windows_of(x_t, f, size) for f in range(frames)], axis=1)
    for j in range(3):
        out = jnp.dot(left, wide[j], preferred_element_type=F32)
        for i in range(3):
            put(3 * i + j, out[i * chans : (i + 1) * chans])
    put(9, early[0])
    put(10, early[1] + jnp.dot(act_t[1], ahead[0], preferred_element_type=F32))
    left_t = jnp.concatenate([act_t[0], act_t[1]], axis=1)
    right = ahead[...].reshape(frames * size, chans)
    put(11, jnp.dot(left_t, right, preferred_element_type=F32))
    half = terms.shape[0] // 2
    for c in range(2):

        @pl.when(core[0] == c)
        def _():
            keep[...] = terms[c * half : (c + 1) * half, :]
            cut = sends[0].shape[0]
            for n, send in enumerate(sends):
                at = (1 - c) * half + n * cut
                send[...] = terms[at : at + cut, :]

    for store in stores:
        store.wait()


def add_kernel(a, *refs):
    out = refs[-1]
    cut = refs[0].shape[0]
    for n, b in enumerate(refs[:-1]):
        rows = pl.ds(n * cut, cut)
        out[rows, :] = (a[rows, :].astype(F32) + b[...].astype(F32)).astype(BF)


def sum_kernel(parts, out):
    total = parts[0].astype(F32)
    for i in range(1, parts.shape[0]):
        total = total + parts[i].astype(F32)
    out[...] = total.astype(out.dtype)


def spread_sum_kernel(scale, parts, out):
    total = parts[0].astype(F32)
    for i in range(1, parts.shape[0]):
        total = total + parts[i].astype(F32)
    total = (total * scale).astype(out.dtype)
    for i in range(out.shape[0]):
        out[i] = total


def write_half(first, source, spatial, temporal, wide, sems):
    copies = []
    for n in range(6):
        t = n if first else n + 6
        for h in range(2):
            at = (n * 2 + h) * 256
            wide[n, :, h * 128 : (h + 1) * 128] = source[at : at + 256, :].astype(F32)
        target = spatial.at[t] if t < 9 else temporal.at[t - 9]
        copy = pltpu.make_async_copy(wide.at[n], target, sems.at[n])
        copy.start()
        copies.append(copy)
    for copy in copies:
        copy.wait()


def own_kernel(core, own, spatial, temporal, wide, sems):
    for c in range(2):

        @pl.when(core[0] == c)
        def _():
            write_half(c == 0, own, spatial, temporal, wide, sems)


def other_kernel(core, other, spatial_in, temporal_in, spatial, temporal, wide, sems):
    for c in range(2):

        @pl.when(core[0] == c)
        def _():
            write_half(c == 1, other, spatial, temporal, wide, sems)


def back_taps(taps, j):
    return jnp.concatenate([taps[i, j] for i in range(3)], axis=1)


def back_kernel(grad, top, bottom, weight, dy, out, padded, taps, own, result, sems):
    frames, size, chans = own.shape
    whole = pltpu.make_async_copy(weight, taps, sems.at[0])
    whole.start()
    loads = []
    for f in range(frames):
        base = 1 + 5 * f
        loads.append(
            [
                pltpu.make_async_copy(top.at[f], padded.at[f, pl.ds(0, COLS)], sems.at[base]),
                pltpu.make_async_copy(
                    grad.at[f], padded.at[f, pl.ds(COLS, size)], sems.at[base + 1]
                ),
                pltpu.make_async_copy(
                    bottom.at[f], padded.at[f, pl.ds(COLS + size, COLS)], sems.at[base + 2]
                ),
                pltpu.make_async_copy(dy.at[f], own.at[f], sems.at[base + 3]),
            ]
        )
        for load in loads[f]:
            load.start()
    whole.wait()
    stores = []
    for f in range(frames):
        for load in loads[f]:
            load.wait()

        @pl.loop(0, size // CHUNK)
        def _(step):
            start = pl.multiple_of(step * CHUNK, CHUNK)
            at = pl.ds(start, CHUNK)
            rows = window(padded, f, start, CHUNK, (2, 1, 0))
            column = columns_of(CHUNK, chans)
            z = [
                lax.dot_general(rows, back_taps(taps, j), NT, preferred_element_type=F32)
                for j in range(3)
            ]
            back = shifted(z[0], column, -1) + z[1] + shifted(z[2], column, 1)
            result[f, at, :] = (own[f, at, :].astype(F32) + back).astype(BF)

        store = pltpu.make_async_copy(result.at[f], out.at[f], sems.at[5 + 5 * f])
        store.start()
        stores.append(store)
    for store in stores:
        store.wait()


def mix_kernel(act, behind, weight, x, out, ext):
    frames, size, chans = act.shape
    for f in range(frames):
        ext[f * size : (f + 1) * size, :] = behind[f]
        ext[(frames + f) * size : (frames + f + 1) * size, :] = act[f]

    @pl.loop(0, frames * (size // CHUNK))
    def _(step):
        start = pl.multiple_of(step * CHUNK, CHUNK)
        rows = jnp.concatenate(
            [ext[pl.ds(start + (2 - k) * size, CHUNK), :] for k in range(3)], axis=1
        )
        mixed = jnp.dot(rows, weight[...].reshape(3 * chans, chans), preferred_element_type=F32)
        own = x[pl.ds(start, CHUNK), :].astype(F32)
        out[pl.ds(start, CHUNK), :] = (own + mixed.astype(BF).astype(F32)).astype(BF)


def steps(axes, by):
    count = lax.axis_size(axes)
    return [(i, i + by) for i in range(count) if 0 <= i + by < count]


def exchange(value, axes):
    return lax.all_to_all(value, axes, split_axis=0, concat_axis=0, tiled=True)


def swap_rims(last, first):
    return lax.ppermute(last, SPACE, steps(SPACE, 1)), lax.ppermute(first, SPACE, steps(SPACE, -1))


def local(scale, frames_in, cotangent, spatial_weight, temporal_weight):
    dims = frames_in.shape
    frames, chans = dims[1], dims[4]
    size = dims[2] * dims[3]
    x = frames_in.reshape(frames, size, chans)
    dy = cotangent.reshape(frames, size, chans)
    work = 2 * frames * size * chans * chans
    core = lax.axis_index("core").astype(jnp.int32).reshape(1)
    ahead = lax.ppermute(dy, TM, steps(TM, -1))
    top, bottom = swap_rims(x[:, size - COLS :, :], x[:, :COLS, :])
    act, slope, x_t, act_t = call(
        forward_kernel,
        [
            shape((frames, size, chans)),
            shape((frames, size, chans), F32),
            shape((frames, chans, size + 2 * COLS)),
            shape((frames, chans, size)),
        ],
        (x, top, bottom, spatial_weight),
        [pltpu.VMEM((frames, size + 2 * COLS, chans), BF)],
        flops=9 * work,
        moved=9 << 20,
    )
    partial, early = call(
        early_kernel,
        [shape((frames, size, chans), F32), shape((2, chans, chans), F32)],
        (dy, temporal_weight, act_t),
        flops=6 * work,
        moved=6 << 20,
    )
    behind = lax.ppermute(act, TM, steps(TM, 1))
    flat = frames * size
    rows = 12 * chans
    edges = shape((frames, COLS, chans))
    pgrad, keep, last, first, *send = call(
        gradient_kernel,
        [shape((frames, size, chans)), shape((rows, 128)), edges, edges]
        + [shape((rows // SWAPS, 128))] * SWAPS,
        (core, ahead, temporal_weight, slope, x_t, act_t, partial, early),
        [
            pltpu.VMEM((3, flat, chans), BF),
            pltpu.VMEM((2 * rows, 128), BF),
            pltpu.SemaphoreType.DMA((frames,)),
        ],
        flops=1 << 10,
        moved=1 << 12,
        smem=(0,),
        out_hbm=(0,),
    )
    grad_top, grad_bottom = swap_rims(last, first)
    pair = [(0, 1), (1, 0)]
    got = [lax.ppermute(part, "core", pair) for part in send]
    half = call(add_kernel, shape((rows, 128)), (keep, *got), moved=1 << 12)
    block = pltpu.VMEM((frames, size, chans), BF)
    column, plane = lax.axis_size(COLUMN), lax.axis_size(PLANE)
    share = rows // plane
    first = exchange(half.reshape(plane, share, 128), PLANE)
    first, grad_top, grad_bottom = lax.optimization_barrier((first, grad_top, grad_bottom))
    spread = call(
        functools.partial(spread_sum_kernel, 1.0),
        shape((column, share, 128)),
        (first,),
        moved=1 << 12,
        after=(behind,),
    )
    third = exchange(spread, COLUMN)
    block_out = call(
        mix_kernel,
        shape((flat, chans)),
        (act, behind, temporal_weight, x.reshape(flat, chans)),
        [pltpu.VMEM((2 * flat, chans), BF)],
        flops=3 * work,
        moved=4 << 20,
    )
    input_grad = call(
        back_kernel,
        shape((frames, size, chans)),
        (pgrad, grad_top, grad_bottom, spatial_weight, dy),
        [
            pltpu.VMEM((frames, size + 2 * COLS, chans), BF),
            pltpu.VMEM((3, 3, chans, chans), BF),
            block,
            block,
            pltpu.SemaphoreType.DMA((11,)),
        ],
        flops=9 * work,
        moved=5 << 20,
        hbm=range(5),
        out_hbm=True,
        limit=58,
    )
    wider = call(
        functools.partial(spread_sum_kernel, scale),
        shape((plane, share, 128)),
        (third,),
        moved=1 << 12,
    )
    own = exchange(wider, PLANE).reshape(rows, 128)
    own, block_out, input_grad = lax.optimization_barrier((own, block_out, input_grad))
    other = lax.ppermute(own, "core", pair)
    grads = [shape((9, chans, chans), F32), shape((3, chans, chans), F32)]
    room = [pltpu.VMEM((6, chans, chans), F32), pltpu.SemaphoreType.DMA((6,))]
    spatial, temporal = call(
        own_kernel, grads, (core, own), room, moved=3 << 20, smem=(0,), out_hbm=True
    )
    spatial, temporal = call(
        other_kernel,
        grads,
        (core, other, spatial, temporal),
        room,
        moved=3 << 20,
        smem=(0,),
        hbm=(2, 3),
        out_hbm=True,
        alias={2: 0, 3: 1},
    )
    return (
        block_out.reshape(dims),
        input_grad.reshape(dims),
        spatial.reshape(3, 3, chans, chans),
        temporal,
    )


def solution(mesh):
    fine = Mesh(mesh.devices.reshape(2, 4, 4, 4, 2), ("clip", "y", "zl", "x", "core"))
    blocks = P("clip", TM, SPACE, None, None)

    def run(frames_in, cotangent, spatial_weight, temporal_weight):
        clips, frames, height, width, _ = frames_in.shape
        scale = (clips * frames * height * width) ** -0.5
        return jax.shard_map(
            functools.partial(local, scale),
            mesh=fine,
            in_specs=(blocks, blocks, P(), P()),
            out_specs=(blocks, blocks, P(), P()),
            check_vma=False,
        )(frames_in, cotangent, spatial_weight, temporal_weight)

    return run
```

```python
import functools

import jax
import jax.numpy as jnp
from jax import lax
from jax.experimental import pallas as pl
from jax.experimental.pallas import tpu as pltpu
from jax.sharding import Mesh, PartitionSpec as P

BF = jnp.bfloat16
F32 = jnp.float32
TM = ("y", "zl")
SPACE = ("x", "core")
PLANE = ("x", "y")
COLUMN = ("clip", "zl")
COLS = 128
NT = (((1,), (1,)), ((), ()))


def call(kernel, outs, ins, scratch=(), flops=0, moved=0, limit=20, smem=(), after=(), hbm=(), out_hbm=False, alias=None):
    vmem = pl.BlockSpec(memory_space=pltpu.VMEM)
    specs = [pl.BlockSpec(memory_space=pltpu.SMEM) if i in smem else vmem for i in range(len(ins))]
    specs = [pl.BlockSpec(memory_space=pl.ANY) if i in hbm else p for i, p in enumerate(specs)]
    specs += [pl.BlockSpec(memory_space=pltpu.HBM)] * len(after)
    many = isinstance(outs, list)
    placed = [
        pl.BlockSpec(memory_space=pltpu.HBM) if out_hbm is True or i in (out_hbm or ()) else vmem
        for i in range(len(outs) if many else 1)
    ]
    count = len(ins)

    def body(*refs):
        kernel(*refs[:count], *refs[count + len(after) :])

    return pl.pallas_call(
        body,
        out_shape=outs,
        in_specs=specs,
        out_specs=placed if many else placed[0],
        input_output_aliases=alias or {},
        scratch_shapes=list(scratch),
        cost_estimate=pl.CostEstimate(flops=flops, bytes_accessed=moved, transcendentals=0),
        compiler_params=pltpu.CompilerParams(vmem_limit_bytes=limit << 20),
    )(*ins, *after)


def shape(dims, kind=BF):
    return jax.ShapeDtypeStruct(dims, kind)


def shifted(value, column, step):
    edge = 0 if step == 1 else COLS - 1
    rolled = pltpu.roll(value, step % value.shape[0], 0)
    return jnp.where(column == edge, 0.0, rolled)


def columns_of(rows, width):
    return lax.broadcasted_iota(jnp.int32, (rows, width), 0) % COLS


def window(ref, frame, start, rows, offsets):
    parts = [ref[frame, pl.ds(start + off * COLS, rows), :] for off in offsets]
    return jnp.concatenate(parts, axis=1)


CHUNK = 512
SWAPS = 4


def fill(padded, block, top, bottom, frame):
    size = block.shape[1]
    padded[frame, 0:COLS, :] = top[frame]
    padded[frame, COLS : COLS + size, :] = block[frame]
    padded[frame, COLS + size :, :] = bottom[frame]


def turn_kernel(x, weight, x_t, held):
    for f in range(x.shape[0]):
        x_t[f] = x[f].T
    held[...] = weight[...]


def forward_kernel(x, top, bottom, weight, act, slope, top_t, bottom_t, act_t, padded):
    frames, size, chans = x.shape
    for f in range(frames):
        fill(padded, x, top, bottom, f)

    @pl.loop(0, frames * (size // CHUNK))
    def _(step):
        f = step // (size // CHUNK)
        start = pl.multiple_of((step % (size // CHUNK)) * CHUNK, CHUNK)
        rows = window(padded, f, start, CHUNK, (0, 1, 2))
        column = columns_of(CHUNK, chans)
        z = [
            jnp.dot(rows, weight[:, j].reshape(3 * chans, chans), preferred_element_type=F32)
            for j in range(3)
        ]
        pre = shifted(z[0], column, 1) + z[1] + shifted(z[2], column, -1)
        sigma = 1.0 / (1.0 + jnp.exp(-pre))
        active = (pre * sigma).astype(BF)
        act[f, pl.ds(start, CHUNK), :] = active
        slope[f, pl.ds(start, CHUNK), :] = sigma * (1.0 + pre * (1.0 - sigma))
        act_t[f, :, pl.ds(start, CHUNK)] = active.T

    for f in range(frames):
        top_t[f] = top[f].T
        bottom_t[f] = bottom[f].T


def early_kernel(dy, weight, act_t, partial, terms):
    frames, size, chans = dy.shape

    @pl.loop(0, size // CHUNK)
    def _(step):
        at = pl.ds(pl.multiple_of(step * CHUNK, CHUNK), CHUNK)
        second = dy[1, at, :]
        both = jnp.concatenate([dy[0, at, :], second], axis=1)
        taps = jnp.concatenate([weight[0], weight[1]], axis=1)
        partial[0, at, :] = lax.dot_general(both, taps, NT, preferred_element_type=F32)
        partial[1, at, :] = lax.dot_general(second, weight[0], NT, preferred_element_type=F32)

    left = jnp.concatenate([act_t[0], act_t[1]], axis=1)
    right = dy[...].reshape(frames * size, chans)
    terms[0] = jnp.dot(left, right, preferred_element_type=F32)
    terms[1] = jnp.dot(act_t[0], dy[1], preferred_element_type=F32)


def finish(f, start, agrad, slope, wide):
    at = pl.ds(start, CHUNK)
    grad = (agrad.astype(BF).astype(F32) * slope[f, at, :]).astype(BF)
    full = grad.astype(F32)
    column = columns_of(CHUNK, full.shape[1])
    into = pl.ds(f * slope.shape[1] + start, CHUNK)
    wide[0, into, :] = shifted(full, column, -1).astype(BF)
    wide[1, into, :] = grad
    wide[2, into, :] = shifted(full, column, 1).astype(BF)


def windows_of(x_t, top_t, bottom_t, f, size):
    above = jnp.concatenate([top_t[f], x_t[f, :, : size - COLS]], axis=1)
    below = jnp.concatenate([x_t[f, :, COLS:], bottom_t[f]], axis=1)
    return jnp.concatenate([above, x_t[f], below], axis=0)


def gradient_kernel(
    core,
    ahead,
    weight,
    slope,
    x_t,
    top_t,
    bottom_t,
    act_t,
    partial,
    early,
    pgrad,
    keep,
    last,
    first,
    *rest,
):
    *sends, wide, terms, sems = rest
    frames, size, chans = ahead.shape

    @pl.loop(0, size // CHUNK)
    def _(step):
        start = pl.multiple_of(step * CHUNK, CHUNK)
        at = pl.ds(start, CHUNK)
        block = ahead[0, at, :]
        more = lax.dot_general(block, weight[2], NT, preferred_element_type=F32)
        finish(0, start, partial[0, at, :] + more, slope, wide)
        both = jnp.concatenate([block, ahead[1, at, :]], axis=1)
        taps = jnp.concatenate([weight[1], weight[2]], axis=1)
        more = lax.dot_general(both, taps, NT, preferred_element_type=F32)
        finish(1, start, partial[1, at, :] + more, slope, wide)

    stores = []
    for f in range(frames):
        rows = pl.ds(f * size, size)
        stores.append(pltpu.make_async_copy(wide.at[1, rows], pgrad.at[f], sems.at[f]))
        stores[f].start()
        last[f] = wide[1, (f + 1) * size - COLS : (f + 1) * size, :]
        first[f] = wide[1, f * size : f * size + COLS, :]

    def put(tap, value):
        for h in range(2):
            at = (tap * 2 + h) * chans
            terms[at : at + chans, :] = value[:, h * 128 : (h + 1) * 128].astype(BF)

    left = jnp.concatenate([windows_of(x_t, top_t, bottom_t, f, size) for f in range(frames)], axis=1)
    for j in range(3):
        out = jnp.dot(left, wide[j], preferred_element_type=F32)
        for i in range(3):
            put(3 * i + j, out[i * chans : (i + 1) * chans])
    put(9, early[0])
    put(10, early[1] + jnp.dot(act_t[1], ahead[0], preferred_element_type=F32))
    left_t = jnp.concatenate([act_t[0], act_t[1]], axis=1)
    right = ahead[...].reshape(frames * size, chans)
    put(11, jnp.dot(left_t, right, preferred_element_type=F32))
    half = terms.shape[0] // 2
    for c in range(2):

        @pl.when(core[0] == c)
        def _():
            keep[...] = terms[c * half : (c + 1) * half, :]
            cut = sends[0].shape[0]
            for n, send in enumerate(sends):
                at = (1 - c) * half + n * cut
                send[...] = terms[at : at + cut, :]

    for store in stores:
        store.wait()


def add_kernel(a, *refs):
    out = refs[-1]
    cut = refs[0].shape[0]
    for n, b in enumerate(refs[:-1]):
        rows = pl.ds(n * cut, cut)
        out[rows, :] = (a[rows, :].astype(F32) + b[...].astype(F32)).astype(BF)


def sum_kernel(parts, out):
    total = parts[0].astype(F32)
    for i in range(1, parts.shape[0]):
        total = total + parts[i].astype(F32)
    out[...] = total.astype(out.dtype)


def spread_sum_kernel(scale, parts, out):
    total = parts[0].astype(F32)
    for i in range(1, parts.shape[0]):
        total = total + parts[i].astype(F32)
    total = (total * scale).astype(out.dtype)
    for i in range(out.shape[0]):
        out[i] = total


def write_half(first, source, spatial, temporal, wide, sems):
    copies = []
    for n in range(6):
        t = n if first else n + 6
        for h in range(2):
            at = (n * 2 + h) * 256
            wide[n, :, h * 128 : (h + 1) * 128] = source[at : at + 256, :].astype(F32)
        target = spatial.at[t] if t < 9 else temporal.at[t - 9]
        copy = pltpu.make_async_copy(wide.at[n], target, sems.at[n])
        copy.start()
        copies.append(copy)
    for copy in copies:
        copy.wait()


def own_kernel(core, own, spatial, temporal, wide, sems):
    for c in range(2):

        @pl.when(core[0] == c)
        def _():
            write_half(c == 0, own, spatial, temporal, wide, sems)


def other_kernel(core, other, spatial_in, temporal_in, spatial, temporal, wide, sems):
    for c in range(2):

        @pl.when(core[0] == c)
        def _():
            write_half(c == 1, other, spatial, temporal, wide, sems)


def back_taps(taps, j):
    return jnp.concatenate([taps[i, j] for i in range(3)], axis=1)


def back_kernel(grad, top, bottom, weight, dy, out, padded, taps, own, result, sems):
    frames, size, chans = own.shape
    whole = pltpu.make_async_copy(weight, taps, sems.at[0])
    whole.start()
    loads = []
    for f in range(frames):
        base = 1 + 5 * f
        loads.append(
            [
                pltpu.make_async_copy(top.at[f], padded.at[f, pl.ds(0, COLS)], sems.at[base]),
                pltpu.make_async_copy(
                    grad.at[f], padded.at[f, pl.ds(COLS, size)], sems.at[base + 1]
                ),
                pltpu.make_async_copy(
                    bottom.at[f], padded.at[f, pl.ds(COLS + size, COLS)], sems.at[base + 2]
                ),
                pltpu.make_async_copy(dy.at[f], own.at[f], sems.at[base + 3]),
            ]
        )
        for load in loads[f]:
            load.start()
    whole.wait()
    stores = []
    for f in range(frames):
        for load in loads[f]:
            load.wait()

        @pl.loop(0, size // CHUNK)
        def _(step):
            start = pl.multiple_of(step * CHUNK, CHUNK)
            at = pl.ds(start, CHUNK)
            rows = window(padded, f, start, CHUNK, (2, 1, 0))
            column = columns_of(CHUNK, chans)
            z = [
                lax.dot_general(rows, back_taps(taps, j), NT, preferred_element_type=F32)
                for j in range(3)
            ]
            back = shifted(z[0], column, -1) + z[1] + shifted(z[2], column, 1)
            result[f, at, :] = (own[f, at, :].astype(F32) + back).astype(BF)

        store = pltpu.make_async_copy(result.at[f], out.at[f], sems.at[5 + 5 * f])
        store.start()
        stores.append(store)
    for store in stores:
        store.wait()


def mix_kernel(act, behind, weight, x, out, ext):
    frames, size, chans = act.shape
    for f in range(frames):
        ext[f * size : (f + 1) * size, :] = behind[f]
        ext[(frames + f) * size : (frames + f + 1) * size, :] = act[f]

    @pl.loop(0, frames * (size // CHUNK))
    def _(step):
        start = pl.multiple_of(step * CHUNK, CHUNK)
        rows = jnp.concatenate(
            [ext[pl.ds(start + (2 - k) * size, CHUNK), :] for k in range(3)], axis=1
        )
        mixed = jnp.dot(rows, weight[...].reshape(3 * chans, chans), preferred_element_type=F32)
        own = x[pl.ds(start, CHUNK), :].astype(F32)
        out[pl.ds(start, CHUNK), :] = (own + mixed.astype(BF).astype(F32)).astype(BF)


def steps(axes, by):
    count = lax.axis_size(axes)
    return [(i, i + by) for i in range(count) if 0 <= i + by < count]


def exchange(value, axes):
    return lax.all_to_all(value, axes, split_axis=0, concat_axis=0, tiled=True)


def swap_rims(last, first):
    return lax.ppermute(last, SPACE, steps(SPACE, 1)), lax.ppermute(first, SPACE, steps(SPACE, -1))


def local(scale, frames_in, cotangent, spatial_weight, temporal_weight):
    dims = frames_in.shape
    frames, chans = dims[1], dims[4]
    size = dims[2] * dims[3]
    x = frames_in.reshape(frames, size, chans)
    dy = cotangent.reshape(frames, size, chans)
    work = 2 * frames * size * chans * chans
    core = lax.axis_index("core").astype(jnp.int32).reshape(1)
    ahead = lax.ppermute(dy, TM, steps(TM, -1))
    top, bottom = swap_rims(x[:, size - COLS :, :], x[:, :COLS, :])
    x_t, held = call(
        turn_kernel,
        [shape((frames, chans, size)), shape(spatial_weight.shape)],
        (x, spatial_weight),
        flops=1 << 20,
        moved=2 << 20,
    )
    act, slope, top_t, bottom_t, act_t = call(
        forward_kernel,
        [
            shape((frames, size, chans)),
            shape((frames, size, chans), F32),
            shape((frames, chans, COLS)),
            shape((frames, chans, COLS)),
            shape((frames, chans, size)),
        ],
        (x, top, bottom, held),
        [pltpu.VMEM((frames, size + 2 * COLS, chans), BF)],
        flops=9 * work,
        moved=9 << 20,
    )
    partial, early = call(
        early_kernel,
        [shape((frames, size, chans), F32), shape((2, chans, chans), F32)],
        (dy, temporal_weight, act_t),
        flops=6 * work,
        moved=6 << 20,
    )
    behind = lax.ppermute(act, TM, steps(TM, 1))
    flat = frames * size
    rows = 12 * chans
    edges = shape((frames, COLS, chans))
    pgrad, keep, last, first, *send = call(
        gradient_kernel,
        [shape((frames, size, chans)), shape((rows, 128)), edges, edges]
        + [shape((rows // SWAPS, 128))] * SWAPS,
        (
            core,
            ahead,
            temporal_weight,
            slope,
            x_t,
            top_t,
            bottom_t,
            act_t,
            partial,
            early,
        ),
        [
            pltpu.VMEM((3, flat, chans), BF),
            pltpu.VMEM((2 * rows, 128), BF),
            pltpu.SemaphoreType.DMA((frames,)),
        ],
        flops=1 << 10,
        moved=1 << 12,
        smem=(0,),
        out_hbm=(0,),
    )
    grad_top, grad_bottom = swap_rims(last, first)
    pair = [(0, 1), (1, 0)]
    got = [lax.ppermute(part, "core", pair) for part in send]
    half = call(add_kernel, shape((rows, 128)), (keep, *got), moved=1 << 12)
    block = pltpu.VMEM((frames, size, chans), BF)
    column, plane = lax.axis_size(COLUMN), lax.axis_size(PLANE)
    share = rows // plane
    first = exchange(half.reshape(plane, share, 128), PLANE)
    first, grad_top, grad_bottom = lax.optimization_barrier((first, grad_top, grad_bottom))
    spread = call(
        functools.partial(spread_sum_kernel, 1.0),
        shape((column, share, 128)),
        (first,),
        moved=1 << 12,
        after=(behind,),
    )
    third = exchange(spread, COLUMN)
    block_out = call(
        mix_kernel,
        shape((flat, chans)),
        (act, behind, temporal_weight, x.reshape(flat, chans)),
        [pltpu.VMEM((2 * flat, chans), BF)],
        flops=3 * work,
        moved=4 << 20,
    )
    input_grad = call(
        back_kernel,
        shape((frames, size, chans)),
        (pgrad, grad_top, grad_bottom, spatial_weight, dy),
        [
            pltpu.VMEM((frames, size + 2 * COLS, chans), BF),
            pltpu.VMEM((3, 3, chans, chans), BF),
            block,
            block,
            pltpu.SemaphoreType.DMA((11,)),
        ],
        flops=9 * work,
        moved=5 << 20,
        hbm=range(5),
        out_hbm=True,
        limit=58,
    )
    wider = call(
        functools.partial(spread_sum_kernel, scale),
        shape((plane, share, 128)),
        (third,),
        moved=1 << 12,
    )
    own = exchange(wider, PLANE).reshape(rows, 128)
    own, block_out, input_grad = lax.optimization_barrier((own, block_out, input_grad))
    other = lax.ppermute(own, "core", pair)
    grads = [shape((9, chans, chans), F32), shape((3, chans, chans), F32)]
    room = [pltpu.VMEM((6, chans, chans), F32), pltpu.SemaphoreType.DMA((6,))]
    spatial, temporal = call(
        own_kernel, grads, (core, own), room, moved=3 << 20, smem=(0,), out_hbm=True
    )
    spatial, temporal = call(
        other_kernel,
        grads,
        (core, other, spatial, temporal),
        room,
        moved=3 << 20,
        smem=(0,),
        hbm=(2, 3),
        out_hbm=True,
        alias={2: 0, 3: 1},
    )
    return (
        block_out.reshape(dims),
        input_grad.reshape(dims),
        spatial.reshape(3, 3, chans, chans),
        temporal,
    )


def solution(mesh):
    fine = Mesh(mesh.devices.reshape(2, 4, 4, 4, 2), ("clip", "y", "zl", "x", "core"))
    blocks = P("clip", TM, SPACE, None, None)

    def run(frames_in, cotangent, spatial_weight, temporal_weight):
        clips, frames, height, width, _ = frames_in.shape
        scale = (clips * frames * height * width) ** -0.5
        return jax.shard_map(
            functools.partial(local, scale),
            mesh=fine,
            in_specs=(blocks, blocks, P(), P()),
            out_specs=(blocks, blocks, P(), P()),
            check_vma=False,
        )(frames_in, cotangent, spatial_weight, temporal_weight)

    return run
```

```python
import functools

import jax
import jax.numpy as jnp
from jax import lax
from jax.experimental import pallas as pl
from jax.experimental.pallas import tpu as pltpu
from jax.sharding import Mesh, PartitionSpec as P

BF = jnp.bfloat16
F32 = jnp.float32
TM = ("y", "zl")
SPACE = ("x", "core")
PLANE = ("x", "y")
COLUMN = ("clip", "zl")
COLS = 128
NT = (((1,), (1,)), ((), ()))


def call(kernel, outs, ins, scratch=(), flops=0, moved=0, limit=20, smem=(), after=(), hbm=(), out_hbm=False, alias=None):
    vmem = pl.BlockSpec(memory_space=pltpu.VMEM)
    specs = [pl.BlockSpec(memory_space=pltpu.SMEM) if i in smem else vmem for i in range(len(ins))]
    specs = [pl.BlockSpec(memory_space=pl.ANY) if i in hbm else p for i, p in enumerate(specs)]
    specs += [pl.BlockSpec(memory_space=pltpu.HBM)] * len(after)
    many = isinstance(outs, list)
    placed = [
        pl.BlockSpec(memory_space=pltpu.HBM) if out_hbm is True or i in (out_hbm or ()) else vmem
        for i in range(len(outs) if many else 1)
    ]
    count = len(ins)

    def body(*refs):
        kernel(*refs[:count], *refs[count + len(after) :])

    return pl.pallas_call(
        body,
        out_shape=outs,
        in_specs=specs,
        out_specs=placed if many else placed[0],
        input_output_aliases=alias or {},
        scratch_shapes=list(scratch),
        cost_estimate=pl.CostEstimate(flops=flops, bytes_accessed=moved, transcendentals=0),
        compiler_params=pltpu.CompilerParams(vmem_limit_bytes=limit << 20),
    )(*ins, *after)


def shape(dims, kind=BF):
    return jax.ShapeDtypeStruct(dims, kind)


def shifted(value, column, step):
    edge = 0 if step == 1 else COLS - 1
    rolled = pltpu.roll(value, step % value.shape[0], 0)
    return jnp.where(column == edge, 0.0, rolled)


def columns_of(rows, width):
    return lax.broadcasted_iota(jnp.int32, (rows, width), 0) % COLS


def window(ref, frame, start, rows, offsets):
    parts = [ref[frame, pl.ds(start + off * COLS, rows), :] for off in offsets]
    return jnp.concatenate(parts, axis=1)


CHUNK = 512
SWAPS = 4


def fill(padded, block, top, bottom, frame):
    size = block.shape[1]
    padded[frame, 0:COLS, :] = top[frame]
    padded[frame, COLS : COLS + size, :] = block[frame]
    padded[frame, COLS + size :, :] = bottom[frame]


def turn_kernel(x, weight, x_t, held):
    for f in range(x.shape[0]):
        x_t[f] = x[f].T
    held[...] = weight[...]


def forward_kernel(x, top, bottom, weight, act, slope, top_t, bottom_t, act_t, padded):
    frames, size, chans = x.shape
    for f in range(frames):
        fill(padded, x, top, bottom, f)

    @pl.loop(0, frames * (size // CHUNK))
    def _(step):
        f = step // (size // CHUNK)
        start = pl.multiple_of((step % (size // CHUNK)) * CHUNK, CHUNK)
        rows = window(padded, f, start, CHUNK, (0, 1, 2))
        column = columns_of(CHUNK, chans)
        z = [
            jnp.dot(rows, weight[:, j].reshape(3 * chans, chans), preferred_element_type=F32)
            for j in range(3)
        ]
        pre = shifted(z[0], column, 1) + z[1] + shifted(z[2], column, -1)
        sigma = 1.0 / (1.0 + jnp.exp(-pre))
        active = (pre * sigma).astype(BF)
        act[f, pl.ds(start, CHUNK), :] = active
        slope[f, pl.ds(start, CHUNK), :] = sigma * (1.0 + pre * (1.0 - sigma))
        act_t[f, :, pl.ds(start, CHUNK)] = active.T

    for f in range(frames):
        top_t[f] = top[f].T
        bottom_t[f] = bottom[f].T


def early_kernel(dy, weight, act_t, partial, terms):
    frames, size, chans = dy.shape

    @pl.loop(0, size // CHUNK)
    def _(step):
        at = pl.ds(pl.multiple_of(step * CHUNK, CHUNK), CHUNK)
        second = dy[1, at, :]
        both = jnp.concatenate([dy[0, at, :], second], axis=1)
        taps = jnp.concatenate([weight[0], weight[1]], axis=1)
        partial[0, at, :] = lax.dot_general(both, taps, NT, preferred_element_type=F32)
        partial[1, at, :] = lax.dot_general(second, weight[0], NT, preferred_element_type=F32)

    left = jnp.concatenate([act_t[0], act_t[1]], axis=1)
    right = dy[...].reshape(frames * size, chans)
    terms[0] = jnp.dot(left, right, preferred_element_type=F32)
    terms[1] = jnp.dot(act_t[0], dy[1], preferred_element_type=F32)


def finish(f, start, agrad, slope, wide):
    at = pl.ds(start, CHUNK)
    grad = (agrad.astype(BF).astype(F32) * slope[f, at, :]).astype(BF)
    full = grad.astype(F32)
    column = columns_of(CHUNK, full.shape[1])
    into = pl.ds(f * slope.shape[1] + start, CHUNK)
    wide[0, into, :] = shifted(full, column, -1).astype(BF)
    wide[1, into, :] = grad
    wide[2, into, :] = shifted(full, column, 1).astype(BF)


def windows_of(x_t, top_t, bottom_t, f, size):
    above = jnp.concatenate([top_t[f], x_t[f, :, : size - COLS]], axis=1)
    below = jnp.concatenate([x_t[f, :, COLS:], bottom_t[f]], axis=1)
    return jnp.concatenate([above, x_t[f], below], axis=0)


def gradient_kernel(
    core,
    ahead,
    weight,
    slope,
    x_t,
    top_t,
    bottom_t,
    act_t,
    partial,
    early,
    pgrad,
    keep,
    last,
    first,
    *rest,
):
    *sends, wide, terms, sems = rest
    frames, size, chans = ahead.shape

    @pl.loop(0, size // CHUNK)
    def _(step):
        start = pl.multiple_of(step * CHUNK, CHUNK)
        at = pl.ds(start, CHUNK)
        block = ahead[0, at, :]
        more = lax.dot_general(block, weight[2], NT, preferred_element_type=F32)
        finish(0, start, partial[0, at, :] + more, slope, wide)
        both = jnp.concatenate([block, ahead[1, at, :]], axis=1)
        taps = jnp.concatenate([weight[1], weight[2]], axis=1)
        more = lax.dot_general(both, taps, NT, preferred_element_type=F32)
        finish(1, start, partial[1, at, :] + more, slope, wide)

    stores = []
    for f in range(frames):
        rows = pl.ds(f * size, size)
        stores.append(pltpu.make_async_copy(wide.at[1, rows], pgrad.at[f], sems.at[f]))
        stores[f].start()
        last[f] = wide[1, (f + 1) * size - COLS : (f + 1) * size, :]
        first[f] = wide[1, f * size : f * size + COLS, :]

    def put(tap, value):
        for h in range(2):
            at = (tap * 2 + h) * chans
            terms[at : at + chans, :] = value[:, h * 128 : (h + 1) * 128].astype(BF)

    left = jnp.concatenate([windows_of(x_t, top_t, bottom_t, f, size) for f in range(frames)], axis=1)
    for j in range(3):
        out = jnp.dot(left, wide[j], preferred_element_type=F32)
        for i in range(3):
            put(3 * i + j, out[i * chans : (i + 1) * chans])
    put(9, early[0])
    put(10, early[1] + jnp.dot(act_t[1], ahead[0], preferred_element_type=F32))
    left_t = jnp.concatenate([act_t[0], act_t[1]], axis=1)
    right = ahead[...].reshape(frames * size, chans)
    put(11, jnp.dot(left_t, right, preferred_element_type=F32))
    half = terms.shape[0] // 2
    for c in range(2):

        @pl.when(core[0] == c)
        def _():
            keep[...] = terms[c * half : (c + 1) * half, :]
            cut = sends[0].shape[0]
            for n, send in enumerate(sends):
                at = (1 - c) * half + n * cut
                send[...] = terms[at : at + cut, :]

    for store in stores:
        store.wait()


def add_kernel(a, *refs):
    out = refs[-1]
    cut = refs[0].shape[0]
    for n, b in enumerate(refs[:-1]):
        rows = pl.ds(n * cut, cut)
        out[rows, :] = (a[rows, :].astype(F32) + b[...].astype(F32)).astype(BF)


def sum_kernel(parts, out):
    total = parts[0].astype(F32)
    for i in range(1, parts.shape[0]):
        total = total + parts[i].astype(F32)
    out[...] = total.astype(out.dtype)


def spread_sum_kernel(scale, parts, out):
    total = parts[0].astype(F32)
    for i in range(1, parts.shape[0]):
        total = total + parts[i].astype(F32)
    total = (total * scale).astype(out.dtype)
    for i in range(out.shape[0]):
        out[i] = total


def write_half(first, source, spatial, temporal, wide, sems):
    copies = []
    for n in range(6):
        t = n if first else n + 6
        for h in range(2):
            at = (n * 2 + h) * 256
            wide[n, :, h * 128 : (h + 1) * 128] = source[at : at + 256, :].astype(F32)
        target = spatial.at[t] if t < 9 else temporal.at[t - 9]
        copy = pltpu.make_async_copy(wide.at[n], target, sems.at[n])
        copy.start()
        copies.append(copy)
    for copy in copies:
        copy.wait()


def own_kernel(core, own, spatial, temporal, wide, sems):
    for c in range(2):

        @pl.when(core[0] == c)
        def _():
            write_half(c == 0, own, spatial, temporal, wide, sems)


def other_kernel(core, other, spatial_in, temporal_in, spatial, temporal, wide, sems):
    for c in range(2):

        @pl.when(core[0] == c)
        def _():
            write_half(c == 1, other, spatial, temporal, wide, sems)


def back_taps(taps, j):
    return jnp.concatenate([taps[i, j] for i in range(3)], axis=1)


def last_kernel(
    behind,
    act,
    x,
    grad,
    top,
    bottom,
    dy,
    weight,
    mix,
    block_out,
    input_grad,
    ext,
    own,
    mixed,
    padded,
    taps,
    up,
    result,
    sems,
):
    frames, size, chans = own.shape
    used = iter(range(sems.shape[0]))

    def begin(source, target):
        copy = pltpu.make_async_copy(source, target, sems.at[next(used)])
        copy.start()
        return copy

    old = [begin(behind.at[f], ext.at[f]) for f in range(frames)]
    new = [
        [begin(act.at[f], ext.at[frames + f]), begin(x.at[f], own.at[f])] for f in range(frames)
    ]
    whole = begin(weight, taps)
    loads = [
        [
            begin(top.at[f], padded.at[f, pl.ds(0, COLS)]),
            begin(grad.at[f], padded.at[f, pl.ds(COLS, size)]),
            begin(bottom.at[f], padded.at[f, pl.ds(COLS + size, COLS)]),
            begin(dy.at[f], up.at[f]),
        ]
        for f in range(frames)
    ]
    stores = []
    for copy in old:
        copy.wait()
    for f in range(frames):
        for copy in new[f]:
            copy.wait()

        @pl.loop(0, size // CHUNK)
        def _(step):
            at = pl.ds(pl.multiple_of(step * CHUNK, CHUNK), CHUNK)
            rows = jnp.concatenate([ext[f + 2 - k, at, :] for k in range(3)], axis=1)
            total = jnp.dot(
                rows, mix[...].reshape(3 * chans, chans), preferred_element_type=F32
            ).astype(BF)
            mixed[f, at, :] = (own[f, at, :].astype(F32) + total.astype(F32)).astype(BF)

        stores.append(begin(mixed.at[f], block_out.at[f]))
    whole.wait()
    for f in range(frames):
        for copy in loads[f]:
            copy.wait()

        @pl.loop(0, size // CHUNK)
        def _(step):
            start = pl.multiple_of(step * CHUNK, CHUNK)
            at = pl.ds(start, CHUNK)
            rows = window(padded, f, start, CHUNK, (2, 1, 0))
            column = columns_of(CHUNK, chans)
            z = [
                lax.dot_general(rows, back_taps(taps, j), NT, preferred_element_type=F32)
                for j in range(3)
            ]
            back = shifted(z[0], column, -1) + z[1] + shifted(z[2], column, 1)
            result[f, at, :] = (up[f, at, :].astype(F32) + back).astype(BF)

        stores.append(begin(result.at[f], input_grad.at[f]))
    for store in stores:
        store.wait()


def steps(axes, by):
    count = lax.axis_size(axes)
    return [(i, i + by) for i in range(count) if 0 <= i + by < count]


def exchange(value, axes):
    return lax.all_to_all(value, axes, split_axis=0, concat_axis=0, tiled=True)


def swap_rims(last, first):
    return lax.ppermute(last, SPACE, steps(SPACE, 1)), lax.ppermute(first, SPACE, steps(SPACE, -1))


def local(scale, frames_in, cotangent, spatial_weight, temporal_weight):
    dims = frames_in.shape
    frames, chans = dims[1], dims[4]
    size = dims[2] * dims[3]
    x = frames_in.reshape(frames, size, chans)
    dy = cotangent.reshape(frames, size, chans)
    work = 2 * frames * size * chans * chans
    core = lax.axis_index("core").astype(jnp.int32).reshape(1)
    ahead = lax.ppermute(dy, TM, steps(TM, -1))
    top, bottom = swap_rims(x[:, size - COLS :, :], x[:, :COLS, :])
    x_t, held = call(
        turn_kernel,
        [shape((frames, chans, size)), shape(spatial_weight.shape)],
        (x, spatial_weight),
        flops=1 << 20,
        moved=2 << 20,
    )
    act, slope, top_t, bottom_t, act_t = call(
        forward_kernel,
        [
            shape((frames, size, chans)),
            shape((frames, size, chans), F32),
            shape((frames, chans, COLS)),
            shape((frames, chans, COLS)),
            shape((frames, chans, size)),
        ],
        (x, top, bottom, held),
        [pltpu.VMEM((frames, size + 2 * COLS, chans), BF)],
        flops=9 * work,
        moved=9 << 20,
    )
    partial, early = call(
        early_kernel,
        [shape((frames, size, chans), F32), shape((2, chans, chans), F32)],
        (dy, temporal_weight, act_t),
        flops=6 * work,
        moved=6 << 20,
    )
    behind = lax.ppermute(act, TM, steps(TM, 1))
    flat = frames * size
    rows = 12 * chans
    edges = shape((frames, COLS, chans))
    pgrad, keep, last, first, *send = call(
        gradient_kernel,
        [shape((frames, size, chans)), shape((rows, 128)), edges, edges]
        + [shape((rows // SWAPS, 128))] * SWAPS,
        (
            core,
            ahead,
            temporal_weight,
            slope,
            x_t,
            top_t,
            bottom_t,
            act_t,
            partial,
            early,
        ),
        [
            pltpu.VMEM((3, flat, chans), BF),
            pltpu.VMEM((2 * rows, 128), BF),
            pltpu.SemaphoreType.DMA((frames,)),
        ],
        flops=1 << 10,
        moved=1 << 12,
        smem=(0,),
        out_hbm=(0,),
    )
    grad_top, grad_bottom = swap_rims(last, first)
    pair = [(0, 1), (1, 0)]
    got = [lax.ppermute(part, "core", pair) for part in send]
    half = call(add_kernel, shape((rows, 128)), (keep, *got), moved=1 << 12)
    block = pltpu.VMEM((frames, size, chans), BF)
    column, plane = lax.axis_size(COLUMN), lax.axis_size(PLANE)
    share = rows // plane
    first = exchange(half.reshape(plane, share, 128), PLANE)
    first, grad_top, grad_bottom = lax.optimization_barrier((first, grad_top, grad_bottom))
    spread = call(
        functools.partial(spread_sum_kernel, 1.0),
        shape((column, share, 128)),
        (first,),
        moved=1 << 12,
        after=(behind,),
    )
    third = exchange(spread, COLUMN)
    block_out, input_grad = call(
        last_kernel,
        [shape((frames, size, chans)), shape((frames, size, chans))],
        (behind, act, x, pgrad, grad_top, grad_bottom, dy, spatial_weight, temporal_weight),
        [
            pltpu.VMEM((2 * frames, size, chans), BF),
            block,
            block,
            pltpu.VMEM((frames, size + 2 * COLS, chans), BF),
            pltpu.VMEM((3, 3, chans, chans), BF),
            block,
            block,
            pltpu.SemaphoreType.DMA((3 * frames + 1 + 4 * frames + 2 * frames,)),
        ],
        flops=12 * work,
        moved=9 << 20,
        hbm=range(8),
        out_hbm=True,
        limit=58,
    )
    wider = call(
        functools.partial(spread_sum_kernel, scale),
        shape((plane, share, 128)),
        (third,),
        moved=1 << 12,
    )
    own = exchange(wider, PLANE).reshape(rows, 128)
    own, block_out, input_grad = lax.optimization_barrier((own, block_out, input_grad))
    other = lax.ppermute(own, "core", pair)
    grads = [shape((9, chans, chans), F32), shape((3, chans, chans), F32)]
    room = [pltpu.VMEM((6, chans, chans), F32), pltpu.SemaphoreType.DMA((6,))]
    spatial, temporal = call(
        own_kernel, grads, (core, own), room, moved=3 << 20, smem=(0,), out_hbm=True
    )
    spatial, temporal = call(
        other_kernel,
        grads,
        (core, other, spatial, temporal),
        room,
        moved=3 << 20,
        smem=(0,),
        hbm=(2, 3),
        out_hbm=True,
        alias={2: 0, 3: 1},
    )
    return (
        block_out.reshape(dims),
        input_grad.reshape(dims),
        spatial.reshape(3, 3, chans, chans),
        temporal,
    )


def solution(mesh):
    fine = Mesh(mesh.devices.reshape(2, 4, 4, 4, 2), ("clip", "y", "zl", "x", "core"))
    blocks = P("clip", TM, SPACE, None, None)

    def run(frames_in, cotangent, spatial_weight, temporal_weight):
        clips, frames, height, width, _ = frames_in.shape
        scale = (clips * frames * height * width) ** -0.5
        return jax.shard_map(
            functools.partial(local, scale),
            mesh=fine,
            in_specs=(blocks, blocks, P(), P()),
            out_specs=(blocks, blocks, P(), P()),
            check_vma=False,
        )(frames_in, cotangent, spatial_weight, temporal_weight)

    return run
```

```python
import functools

import jax
import jax.numpy as jnp
from jax import lax
from jax.experimental import pallas as pl
from jax.experimental.pallas import tpu as pltpu
from jax.sharding import Mesh, PartitionSpec as P

BF = jnp.bfloat16
F32 = jnp.float32
TM = ("y", "zl")
SPACE = ("x", "core")
PLANE = ("x", "y")
COLUMN = ("zl", "clip")
COLS = 128
NT = (((1,), (1,)), ((), ()))


def call(kernel, outs, ins, scratch=(), flops=0, moved=0, limit=20, smem=(), after=(), hbm=(), out_hbm=False, alias=None):
    vmem = pl.BlockSpec(memory_space=pltpu.VMEM)
    specs = [pl.BlockSpec(memory_space=pltpu.SMEM) if i in smem else vmem for i in range(len(ins))]
    specs = [pl.BlockSpec(memory_space=pl.ANY) if i in hbm else p for i, p in enumerate(specs)]
    specs += [pl.BlockSpec(memory_space=pltpu.HBM)] * len(after)
    many = isinstance(outs, list)
    placed = [
        pl.BlockSpec(memory_space=pltpu.HBM) if out_hbm is True or i in (out_hbm or ()) else vmem
        for i in range(len(outs) if many else 1)
    ]
    count = len(ins)

    def body(*refs):
        kernel(*refs[:count], *refs[count + len(after) :])

    return pl.pallas_call(
        body,
        out_shape=outs,
        in_specs=specs,
        out_specs=placed if many else placed[0],
        input_output_aliases=alias or {},
        scratch_shapes=list(scratch),
        cost_estimate=pl.CostEstimate(flops=flops, bytes_accessed=moved, transcendentals=0),
        compiler_params=pltpu.CompilerParams(vmem_limit_bytes=limit << 20),
    )(*ins, *after)


def shape(dims, kind=BF):
    return jax.ShapeDtypeStruct(dims, kind)


def shifted(value, column, step):
    edge = 0 if step == 1 else COLS - 1
    rolled = pltpu.roll(value, step % value.shape[0], 0)
    return jnp.where(column == edge, 0.0, rolled)


def columns_of(rows, width):
    return lax.broadcasted_iota(jnp.int32, (rows, width), 0) % COLS


def window(ref, frame, start, rows, offsets):
    parts = [ref[frame, pl.ds(start + off * COLS, rows), :] for off in offsets]
    return jnp.concatenate(parts, axis=1)


CHUNK = 512
BLOCK = 1024
SWAPS = 4


def fill(padded, block, top, bottom, frame):
    size = block.shape[1]
    padded[frame, 0:COLS, :] = top[frame]
    padded[frame, COLS : COLS + size, :] = block[frame]
    padded[frame, COLS + size :, :] = bottom[frame]


def turn_kernel(x, weight, x_t, held):
    for f in range(x.shape[0]):
        x_t[f] = x[f].T
    held[...] = weight[...]


def forward_kernel(x, top, bottom, weight, act, slope, top_t, bottom_t, act_t, padded):
    frames, size, chans = x.shape
    for f in range(frames):
        fill(padded, x, top, bottom, f)

    @pl.loop(0, frames * (size // BLOCK))
    def _(step):
        f = step // (size // BLOCK)
        start = pl.multiple_of((step % (size // BLOCK)) * BLOCK, BLOCK)
        rows = window(padded, f, start, BLOCK, (0, 1, 2))
        column = columns_of(BLOCK, chans)
        z = [
            jnp.dot(rows, weight[:, j].reshape(3 * chans, chans), preferred_element_type=F32)
            for j in range(3)
        ]
        pre = shifted(z[0], column, 1) + z[1] + shifted(z[2], column, -1)
        sigma = 1.0 / (1.0 + jnp.exp(-pre))
        active = (pre * sigma).astype(BF)
        act[f, pl.ds(start, BLOCK), :] = active
        slope[f, pl.ds(start, BLOCK), :] = sigma * (1.0 + pre * (1.0 - sigma))
        act_t[f, :, pl.ds(start, BLOCK)] = active.T

    for f in range(frames):
        top_t[f] = top[f].T
        bottom_t[f] = bottom[f].T


def early_kernel(dy, weight, act_t, partial, terms):
    frames, size, chans = dy.shape

    @pl.loop(0, size // BLOCK)
    def _(step):
        at = pl.ds(pl.multiple_of(step * BLOCK, BLOCK), BLOCK)
        second = dy[1, at, :]
        both = jnp.concatenate([dy[0, at, :], second], axis=1)
        taps = jnp.concatenate([weight[0], weight[1]], axis=1)
        partial[0, at, :] = lax.dot_general(both, taps, NT, preferred_element_type=F32)
        partial[1, at, :] = lax.dot_general(second, weight[0], NT, preferred_element_type=F32)

    left = jnp.concatenate([act_t[0], act_t[1]], axis=1)
    right = dy[...].reshape(frames * size, chans)
    terms[0] = jnp.dot(left, right, preferred_element_type=F32)
    terms[1] = jnp.dot(act_t[0], dy[1], preferred_element_type=F32)


def finish(f, start, agrad, slope, wide):
    at = pl.ds(start, CHUNK)
    grad = (agrad.astype(BF).astype(F32) * slope[f, at, :]).astype(BF)
    full = grad.astype(F32)
    column = columns_of(CHUNK, full.shape[1])
    into = pl.ds(f * slope.shape[1] + start, CHUNK)
    wide[0, into, :] = shifted(full, column, -1).astype(BF)
    wide[1, into, :] = grad
    wide[2, into, :] = shifted(full, column, 1).astype(BF)


def windows_of(x_t, top_t, bottom_t, f, size):
    above = jnp.concatenate([top_t[f], x_t[f, :, : size - COLS]], axis=1)
    below = jnp.concatenate([x_t[f, :, COLS:], bottom_t[f]], axis=1)
    return jnp.concatenate([above, x_t[f], below], axis=0)


def gradient_kernel(
    core,
    ahead,
    weight,
    slope,
    x_t,
    top_t,
    bottom_t,
    act_t,
    partial,
    early,
    pgrad,
    keep,
    last,
    first,
    *rest,
):
    *sends, wide, terms, sems = rest
    frames, size, chans = ahead.shape

    @pl.loop(0, size // CHUNK)
    def _(step):
        start = pl.multiple_of(step * CHUNK, CHUNK)
        at = pl.ds(start, CHUNK)
        block = ahead[0, at, :]
        more = lax.dot_general(block, weight[2], NT, preferred_element_type=F32)
        finish(0, start, partial[0, at, :] + more, slope, wide)
        both = jnp.concatenate([block, ahead[1, at, :]], axis=1)
        taps = jnp.concatenate([weight[1], weight[2]], axis=1)
        more = lax.dot_general(both, taps, NT, preferred_element_type=F32)
        finish(1, start, partial[1, at, :] + more, slope, wide)

    stores = []
    for f in range(frames):
        rows = pl.ds(f * size, size)
        stores.append(pltpu.make_async_copy(wide.at[1, rows], pgrad.at[f], sems.at[f]))
        stores[f].start()
        last[f] = wide[1, (f + 1) * size - COLS : (f + 1) * size, :]
        first[f] = wide[1, f * size : f * size + COLS, :]

    def put(tap, value):
        for h in range(2):
            at = (tap * 2 + h) * chans
            terms[at : at + chans, :] = value[:, h * 128 : (h + 1) * 128].astype(BF)

    left = jnp.concatenate([windows_of(x_t, top_t, bottom_t, f, size) for f in range(frames)], axis=1)
    for j in range(3):
        out = jnp.dot(left, wide[j], preferred_element_type=F32)
        for i in range(3):
            put(3 * i + j, out[i * chans : (i + 1) * chans])
    put(9, early[0])
    put(10, early[1] + jnp.dot(act_t[1], ahead[0], preferred_element_type=F32))
    left_t = jnp.concatenate([act_t[0], act_t[1]], axis=1)
    right = ahead[...].reshape(frames * size, chans)
    put(11, jnp.dot(left_t, right, preferred_element_type=F32))
    half = terms.shape[0] // 2
    for c in range(2):

        @pl.when(core[0] == c)
        def _():
            keep[...] = terms[c * half : (c + 1) * half, :]
            cut = sends[0].shape[0]
            for n, send in enumerate(sends):
                at = (1 - c) * half + n * cut
                send[...] = terms[at : at + cut, :]

    for store in stores:
        store.wait()


def add_kernel(a, *refs):
    out = refs[-1]
    cut = refs[0].shape[0]
    for n, b in enumerate(refs[:-1]):
        rows = pl.ds(n * cut, cut)
        out[rows, :] = (a[rows, :].astype(F32) + b[...].astype(F32)).astype(BF)


def sum_kernel(parts, out):
    total = parts[0].astype(F32)
    for i in range(1, parts.shape[0]):
        total = total + parts[i].astype(F32)
    out[...] = total.astype(out.dtype)


def spread_sum_kernel(scale, parts, out):
    total = parts[0].astype(F32)
    for i in range(1, parts.shape[0]):
        total = total + parts[i].astype(F32)
    total = (total * scale).astype(out.dtype)
    for i in range(out.shape[0]):
        out[i] = total


def write_half(first, source, spatial, temporal, wide, sems):
    copies = []
    for n in range(6):
        t = n if first else n + 6
        for h in range(2):
            at = (n * 2 + h) * 256
            wide[n, :, h * 128 : (h + 1) * 128] = source[at : at + 256, :].astype(F32)
        target = spatial.at[t] if t < 9 else temporal.at[t - 9]
        copy = pltpu.make_async_copy(wide.at[n], target, sems.at[n])
        copy.start()
        copies.append(copy)
    for copy in copies:
        copy.wait()


def own_kernel(core, own, spatial, temporal, wide, sems):
    for c in range(2):

        @pl.when(core[0] == c)
        def _():
            write_half(c == 0, own, spatial, temporal, wide, sems)


def other_kernel(core, other, spatial_in, temporal_in, spatial, temporal, wide, sems):
    for c in range(2):

        @pl.when(core[0] == c)
        def _():
            write_half(c == 1, other, spatial, temporal, wide, sems)


def back_taps(taps, j):
    return jnp.concatenate([taps[i, j] for i in range(3)], axis=1)


def last_kernel(
    behind,
    act,
    x,
    grad,
    top,
    bottom,
    dy,
    weight,
    mix,
    block_out,
    input_grad,
    ext,
    own,
    mixed,
    padded,
    taps,
    up,
    result,
    sems,
):
    frames, size, chans = own.shape
    used = iter(range(sems.shape[0]))

    def begin(source, target):
        copy = pltpu.make_async_copy(source, target, sems.at[next(used)])
        copy.start()
        return copy

    old = [begin(behind.at[f], ext.at[f]) for f in range(frames)]
    new = [
        [begin(act.at[f], ext.at[frames + f]), begin(x.at[f], own.at[f])] for f in range(frames)
    ]
    whole = begin(weight, taps)
    loads = [
        [
            begin(top.at[f], padded.at[f, pl.ds(0, COLS)]),
            begin(grad.at[f], padded.at[f, pl.ds(COLS, size)]),
            begin(bottom.at[f], padded.at[f, pl.ds(COLS + size, COLS)]),
            begin(dy.at[f], up.at[f]),
        ]
        for f in range(frames)
    ]
    stores = []
    for copy in old:
        copy.wait()
    for f in range(frames):
        for copy in new[f]:
            copy.wait()

        @pl.loop(0, size // CHUNK)
        def _(step):
            at = pl.ds(pl.multiple_of(step * CHUNK, CHUNK), CHUNK)
            rows = jnp.concatenate([ext[f + 2 - k, at, :] for k in range(3)], axis=1)
            total = jnp.dot(
                rows, mix[...].reshape(3 * chans, chans), preferred_element_type=F32
            ).astype(BF)
            mixed[f, at, :] = (own[f, at, :].astype(F32) + total.astype(F32)).astype(BF)

        stores.append(begin(mixed.at[f], block_out.at[f]))
    whole.wait()
    for f in range(frames):
        for copy in loads[f]:
            copy.wait()

        @pl.loop(0, size // CHUNK)
        def _(step):
            start = pl.multiple_of(step * CHUNK, CHUNK)
            at = pl.ds(start, CHUNK)
            rows = window(padded, f, start, CHUNK, (2, 1, 0))
            column = columns_of(CHUNK, chans)
            z = [
                lax.dot_general(rows, back_taps(taps, j), NT, preferred_element_type=F32)
                for j in range(3)
            ]
            back = shifted(z[0], column, -1) + z[1] + shifted(z[2], column, 1)
            result[f, at, :] = (up[f, at, :].astype(F32) + back).astype(BF)

        stores.append(begin(result.at[f], input_grad.at[f]))
    for store in stores:
        store.wait()


def steps(axes, by):
    count = lax.axis_size(axes)
    return [(i, i + by) for i in range(count) if 0 <= i + by < count]


def exchange(value, axes):
    return lax.all_to_all(value, axes, split_axis=0, concat_axis=0, tiled=True)


def swap_rims(last, first):
    return lax.ppermute(last, SPACE, steps(SPACE, 1)), lax.ppermute(first, SPACE, steps(SPACE, -1))


def local(scale, frames_in, cotangent, spatial_weight, temporal_weight):
    dims = frames_in.shape
    frames, chans = dims[1], dims[4]
    size = dims[2] * dims[3]
    x = frames_in.reshape(frames, size, chans)
    dy = cotangent.reshape(frames, size, chans)
    work = 2 * frames * size * chans * chans
    core = lax.axis_index("core").astype(jnp.int32).reshape(1)
    ahead = lax.ppermute(dy, TM, steps(TM, -1))
    top, bottom = swap_rims(x[:, size - COLS :, :], x[:, :COLS, :])
    x_t, held = call(
        turn_kernel,
        [shape((frames, chans, size)), shape(spatial_weight.shape)],
        (x, spatial_weight),
        flops=1 << 20,
        moved=2 << 20,
    )
    act, slope, top_t, bottom_t, act_t = call(
        forward_kernel,
        [
            shape((frames, size, chans)),
            shape((frames, size, chans), F32),
            shape((frames, chans, COLS)),
            shape((frames, chans, COLS)),
            shape((frames, chans, size)),
        ],
        (x, top, bottom, held),
        [pltpu.VMEM((frames, size + 2 * COLS, chans), BF)],
        flops=9 * work,
        moved=9 << 20,
    )
    partial, early = call(
        early_kernel,
        [shape((frames, size, chans), F32), shape((2, chans, chans), F32)],
        (dy, temporal_weight, act_t),
        flops=6 * work,
        moved=6 << 20,
    )
    behind = lax.ppermute(act, TM, steps(TM, 1))
    flat = frames * size
    rows = 12 * chans
    edges = shape((frames, COLS, chans))
    pgrad, keep, last, first, *send = call(
        gradient_kernel,
        [shape((frames, size, chans)), shape((rows, 128)), edges, edges]
        + [shape((rows // SWAPS, 128))] * SWAPS,
        (
            core,
            ahead,
            temporal_weight,
            slope,
            x_t,
            top_t,
            bottom_t,
            act_t,
            partial,
            early,
        ),
        [
            pltpu.VMEM((3, flat, chans), BF),
            pltpu.VMEM((2 * rows, 128), BF),
            pltpu.SemaphoreType.DMA((frames,)),
        ],
        flops=1 << 10,
        moved=1 << 12,
        smem=(0,),
        out_hbm=(0,),
    )
    grad_top, grad_bottom = swap_rims(last, first)
    pair = [(0, 1), (1, 0)]
    got = [lax.ppermute(part, "core", pair) for part in send]
    half = call(add_kernel, shape((rows, 128)), (keep, *got), moved=1 << 12)
    block = pltpu.VMEM((frames, size, chans), BF)
    column, plane = lax.axis_size(COLUMN), lax.axis_size(PLANE)
    share = rows // plane
    first = exchange(half.reshape(plane, share, 128), PLANE)
    first, grad_top, grad_bottom = lax.optimization_barrier((first, grad_top, grad_bottom))
    spread = call(
        functools.partial(spread_sum_kernel, 1.0),
        shape((column, share, 128)),
        (first,),
        moved=1 << 12,
        after=(behind,),
    )
    third = exchange(spread, COLUMN)
    block_out, input_grad = call(
        last_kernel,
        [shape((frames, size, chans)), shape((frames, size, chans))],
        (behind, act, x, pgrad, grad_top, grad_bottom, dy, spatial_weight, temporal_weight),
        [
            pltpu.VMEM((2 * frames, size, chans), BF),
            block,
            block,
            pltpu.VMEM((frames, size + 2 * COLS, chans), BF),
            pltpu.VMEM((3, 3, chans, chans), BF),
            block,
            block,
            pltpu.SemaphoreType.DMA((3 * frames + 1 + 4 * frames + 2 * frames,)),
        ],
        flops=12 * work,
        moved=9 << 20,
        hbm=range(8),
        out_hbm=True,
        limit=58,
    )
    wider = call(
        functools.partial(spread_sum_kernel, scale),
        shape((plane, share, 128)),
        (third,),
        moved=1 << 12,
    )
    own = exchange(wider, PLANE).reshape(rows, 128)
    own, block_out, input_grad = lax.optimization_barrier((own, block_out, input_grad))
    other = lax.ppermute(own, "core", pair)
    grads = [shape((9, chans, chans), F32), shape((3, chans, chans), F32)]
    room = [pltpu.VMEM((6, chans, chans), F32), pltpu.SemaphoreType.DMA((6,))]
    spatial, temporal = call(
        own_kernel, grads, (core, own), room, moved=3 << 20, smem=(0,), out_hbm=True
    )
    spatial, temporal = call(
        other_kernel,
        grads,
        (core, other, spatial, temporal),
        room,
        moved=3 << 20,
        smem=(0,),
        hbm=(2, 3),
        out_hbm=True,
        alias={2: 0, 3: 1},
    )
    return (
        block_out.reshape(dims),
        input_grad.reshape(dims),
        spatial.reshape(3, 3, chans, chans),
        temporal,
    )


def solution(mesh):
    fine = Mesh(mesh.devices.reshape(2, 4, 4, 4, 2), ("clip", "y", "zl", "x", "core"))
    blocks = P("clip", TM, SPACE, None, None)

    def run(frames_in, cotangent, spatial_weight, temporal_weight):
        clips, frames, height, width, _ = frames_in.shape
        scale = (clips * frames * height * width) ** -0.5
        return jax.shard_map(
            functools.partial(local, scale),
            mesh=fine,
            in_specs=(blocks, blocks, P(), P()),
            out_specs=(blocks, blocks, P(), P()),
            check_vma=False,
        )(frames_in, cotangent, spatial_weight, temporal_weight)

    return run
```
